32 devices in a mesh: pts: 8 (over y, x, core), blk: 4 (over z).
Axes of the slice: x: 2, y: 2, z: 4, core: 2. Of those that a mesh axis runs over, the one named last changes fastest.
Arguments:
- snapshots: bfloat16 [3072, 4, 8192], P('blk', None, 'pts'), may hold values from -8 to 8
- freq_index: int32 [32], replicated, may hold values from 2 to 383, as said below
- weight_class: int32 [8192], P('pts'), may hold values from 0 to 7
- class_weight: float32 [8], replicated, may hold values from 0.25 to 4
Outputs:
- csd: float32 [32, 2, 8, 8], P('blk')
- eigval: float32 [32], P('blk')
- modes: float32 [32, 2, 4, 8192], P('blk', None, None, 'pts')
The draws below stay inside these ranges and needn't reach their ends.
Inputs may be any that keep to these rules, and one draw needn't show every extreme that they name: `freq_index`: 32 distinct bins; both 2 and 383 are always among them.
All inputs are finite; a program needn't handle non-finite values.
Results may differ from the reference program's by a relative error of at most 0.0018.
Values may be sent and summed in bfloat16 or wider, within the bound.
No kernel may reach another device: no remote copies, remote signals or barrier semaphores. Data moves between devices by JAX's collectives and lax.ppermute only.
A program may use at most 64 MiB of HBM per device.

```python
import math
import jax
import jax.numpy as jnp
from jax import lax

VARS = 4
NFFT = 768
HALF = 384
NB = 8
NTIME = 3072
NF = 32
NPTS = 8192
NCLASS = 8
ITERS = 3


def kept_bins(key):
    key = jax.random.fold_in(key, 1)
    inner = jax.random.permutation(key, HALF - 4).astype(jnp.int32) + 3
    chosen = inner[:NF - 2]
    low_end = jnp.full((1,), 2, jnp.int32)
    high_end = jnp.full((1,), HALF - 1, jnp.int32)
    return jnp.concatenate([low_end, chosen, high_end], axis=0)


def draw_freq_index(key, part):
    return kept_bins(key)


def draw_snapshots(key, part):
    bins = kept_bins(key)
    key = jax.random.fold_in(key, 2)
    keys = jax.random.split(key, 6)
    picked = jax.random.randint(keys[0], (VARS, NPTS), 0, NF).astype(jnp.int32)
    feature_bin = bins[picked]
    start_phase = jax.random.uniform(keys[1], (VARS, NPTS), jnp.float32, -math.pi, math.pi)
    envelope_phase = jax.random.uniform(keys[2], (VARS, NPTS), jnp.float32, -math.pi, math.pi)
    log_amp = jax.random.uniform(keys[3], (VARS, NPTS), jnp.float32, math.log(0.5), math.log(2.0))

    def noise_draw(noise_key):
        return jnp.clip(jax.random.normal(noise_key, (HALF, VARS, NPTS), jnp.float32), -4.0, 4.0)
    amplitude = jnp.exp(log_amp)

    def one_block(index):
        times = index * HALF + jnp.arange(HALF, dtype=jnp.int32)
        phase_int = feature_bin[None, :, :] * times[:, None, None] % NFFT
        angle = 2.0 * math.pi / NFFT * phase_int.astype(jnp.float32) + start_phase[None]
        slow = 2.0 * math.pi / NTIME * times.astype(jnp.float32)
        envelope = 0.7 + 0.3 * jnp.cos(slow[:, None, None] + envelope_phase[None])
        coherent = amplitude[None] * envelope * jnp.cos(angle)
        noise = noise_draw(jax.random.fold_in(keys[5], index))
        return (coherent + noise).astype(jnp.bfloat16)
    blocks = lax.map(one_block, jnp.arange(NB, dtype=jnp.int32))
    return blocks.reshape(NTIME, VARS, NPTS)


def place_ends(result, own_key, smallest, high):
    place = [jax.random.randint(jax.random.fold_in(own_key, axis), (), 0, length) for axis, length in enumerate(result.shape)]
    widest = result.shape.index(max(result.shape))
    beside = place[:widest] + [(place[widest] + 1) % result.shape[widest]] + place[widest + 1:]
    return result.at[tuple(place)].set(smallest).at[tuple(beside)].set(high)


def setup_inputs(seed: int = 0) -> dict:
    key_of = jax.random.split(jax.random.key(seed), 5)
    snapshots = draw_snapshots(jax.random.fold_in(key_of[4], 71), 0)
    freq_index = draw_freq_index(jax.random.fold_in(key_of[4], 71), 0)
    weight_class = place_ends(jax.random.randint(key_of[2], (NPTS,), 0, NCLASS), jax.random.fold_in(key_of[2], 1), 0, NCLASS - 1).astype(jnp.int32)
    class_weight = jnp.clip(jnp.exp(jax.random.uniform(key_of[3], (NCLASS,), jnp.float32, math.log(0.25), math.log(4.0))), 0.25, 4.0)
    return {"snapshots": snapshots, "freq_index": freq_index, "weight_class": weight_class, "class_weight": class_weight}


def transform_table(freq_index):
    times = jnp.arange(NFFT, dtype=jnp.int32)
    phase = freq_index[:, None] * times[None, :] % NFFT
    angle = 2.0 * math.pi / NFFT * phase.astype(jnp.float32)
    window = 0.5 - 0.5 * jnp.cos(2.0 * math.pi / NFFT * times.astype(jnp.float32))
    real_part = window[None, :] * jnp.cos(angle)
    imag_part = -window[None, :] * jnp.sin(angle)
    stacked = jnp.stack([real_part, imag_part], axis=1)
    return stacked.reshape(2 * freq_index.shape[0], NFFT).astype(jnp.bfloat16)

def point_weights(weight_class, class_weight):
    classes = jnp.arange(class_weight.shape[0], dtype=jnp.int32)
    picked = jnp.where(weight_class[:, None] == classes[None, :], class_weight[None, :], jnp.float32(0.0))
    return lax.optimization_barrier(jnp.sum(picked, axis=1))

def apply_csd(real_mat, imag_mat, vec_re, vec_im):
    highest = lax.Precision.HIGHEST
    out_re = jnp.einsum('fab,fb->fa', real_mat, vec_re, precision=highest) - jnp.einsum('fab,fb->fa', imag_mat, vec_im, precision=highest)
    out_im = jnp.einsum('fab,fb->fa', real_mat, vec_im, precision=highest) + jnp.einsum('fab,fb->fa', imag_mat, vec_re, precision=highest)
    return (out_re, out_im)

def reference(snapshots, freq_index, weight_class, class_weight):
    features = VARS * NPTS
    samples = snapshots.reshape(NTIME, features)
    padded = jnp.concatenate([samples, jnp.zeros((HALF, features), jnp.bfloat16)], axis=0)
    transform = transform_table(freq_index)

    def one_block(block_id):
        start = (block_id * HALF).astype(jnp.int32)
        segment = lax.dynamic_slice_in_dim(padded, start, NFFT, 0)
        spectrum = jnp.dot(transform, segment, preferred_element_type=jnp.float32)
        return spectrum.astype(jnp.bfloat16).reshape(NF, 2, features)
    qhat = lax.map(one_block, jnp.arange(NB, dtype=jnp.int32))
    wpoint = point_weights(weight_class, class_weight)
    wfeat = jnp.tile(wpoint, VARS)
    qweighted = (qhat.astype(jnp.float32) * wfeat).astype(jnp.bfloat16)
    by_freq = jnp.moveaxis(qhat, 1, 0)
    by_freq_w = jnp.moveaxis(qweighted, 1, 0)

    def one_gram(pair):
        left, right = pair
        return jnp.einsum('bcp,edp->bced', left.astype(jnp.float32), right.astype(jnp.float32))
    gram = lax.map(one_gram, (by_freq, by_freq_w))
    scaling = 1.0 / (VARS * NPTS * (3.0 * NFFT / 8.0))
    real_mat = scaling * (gram[:, :, 0, :, 0] + gram[:, :, 1, :, 1])
    imag_mat = scaling * (gram[:, :, 0, :, 1] - gram[:, :, 1, :, 0])
    csd = jnp.stack([real_mat, imag_mat], axis=1)
    vec_re = jnp.full((NF, NB), 1.0 / math.sqrt(NB), jnp.float32)
    vec_im = jnp.zeros((NF, NB), jnp.float32)
    for iteration in range(ITERS):
        out_re, out_im = apply_csd(real_mat, imag_mat, vec_re, vec_im)
        length = jnp.sqrt(lax.optimization_barrier(jnp.sum(out_re * out_re + out_im * out_im, axis=1, keepdims=True)))
        vec_re, vec_im = (out_re / length, out_im / length)
    out_re, out_im = apply_csd(real_mat, imag_mat, vec_re, vec_im)
    eigval = lax.optimization_barrier(jnp.sum(vec_re * out_re + vec_im * out_im, axis=1))
    coef = jnp.stack([jnp.stack([vec_re, vec_im], axis=-1), jnp.stack([-vec_im, vec_re], axis=-1)], axis=2).astype(jnp.bfloat16)

    def one_mode(pair):
        spectra, weights = pair
        return jnp.einsum('bcp,bck->kp', spectra.astype(jnp.float32), weights.astype(jnp.float32))
    phi = lax.map(one_mode, (by_freq, coef))
    normsq = lax.optimization_barrier(jnp.sum(wfeat[None, None, :] * phi * phi, axis=(1, 2)))
    modes = phi * jnp.sqrt(VARS * NPTS / normsq)[:, None, None]
    return (csd, eigval, modes.reshape(NF, 2, VARS, NPTS))
```

```python
import functools
import math

import jax
import jax.numpy as jnp
from jax import lax
from jax.experimental import pallas as pl
from jax.experimental.pallas import tpu as pltpu
from jax.sharding import PartitionSpec as P

NFFT = 768
HALF = NFFT // 2
ITERS = 3
LANES = 128
VMEM_LIMIT = 48 * 1024 * 1024
F32 = jnp.float32
BF16 = jnp.bfloat16


def iota(shape, axis):
    return lax.broadcasted_iota(jnp.int32, shape, axis)


def mm(a, b):
    return jnp.dot(a, b, preferred_element_type=F32)


def split3(x):
    high = x.astype(BF16)
    rest = x - high.astype(F32)
    mid = rest.astype(BF16)
    low = (rest - mid.astype(F32)).astype(BF16)
    return (high, mid, low)


def one_hot(condition):
    return jnp.where(condition, 1.0, 0.0).astype(BF16)


def transform_table(freq_rows, group):
    times = jnp.arange(NFFT, dtype=jnp.int32)
    phase = freq_rows[:, None] * times[None, :] % NFFT
    angle = 2.0 * math.pi / NFFT * phase.astype(F32)
    window = 0.5 - 0.5 * jnp.cos(2.0 * math.pi / NFFT * times.astype(F32))
    real_part = window[None, :] * jnp.cos(angle)
    imag_part = -window[None, :] * jnp.sin(angle)
    slots = freq_rows.shape[0] // group
    stacked = jnp.stack(
        [real_part.reshape(slots, group, NFFT), imag_part.reshape(slots, group, NFFT)], axis=1
    )
    return stacked.reshape(2 * freq_rows.shape[0], NFFT).astype(BF16)


def spread(rows, var_count):
    width = HALF * var_count
    pick = one_hot(iota((HALF, width), 1) // var_count == iota((HALF, width), 0))
    wide = mm(rows, pick)
    owner = iota(wide.shape, 1) % var_count
    return jnp.concatenate(
        [jnp.where(owner == v, wide, 0.0).astype(BF16) for v in range(var_count)], axis=0
    )


def load_copies(x_hbm, held, sems):
    return [
        pltpu.make_async_copy(x_hbm.at[:, :, pl.ds(j * LANES, LANES)], held.at[j], sems.at[j])
        for j in range(held.shape[0])
    ]


def columns(held, j, half, var_count):
    rows = HALF * var_count
    parts = [
        held.at[j + i].reshape(2 * rows, LANES)[half * rows : (half + 1) * rows, :]
        for i in range(2)
    ]
    return jnp.concatenate(parts, axis=1)


def halo_kernel(down_rows, up_rows, var_count, points, tab, x_hbm, down, up, held, sems):
    copies = load_copies(x_hbm, held, sems)
    for copy in copies:
        copy.start()
    down_lhs = spread(tab[down_rows[0] : down_rows[1], HALF:], var_count)
    up_lhs = spread(tab[up_rows[0] : up_rows[1], :HALF], var_count)
    count = down_rows[1] - down_rows[0]
    for j in range(0, held.shape[0], 2):
        copies[j].wait()
        copies[j + 1].wait()
        for half, lhs, out in ((0, down_lhs, down), (1, up_lhs, up)):
            got = mm(lhs, columns(held, j, half, var_count))
            for v in range(var_count):
                out[:, v * points + j * LANES : v * points + (j + 2) * LANES] = got[
                    v * count : (v + 1) * count
                ]


def block_kernel(slots, keep, var_count, points, tab, x_hbm, *refs):
    outs, (held, sems) = (refs[: -2], refs[-2:])
    even = outs[:slots]
    lead = outs[slots : slots + len(keep)]
    trail = outs[slots + len(keep) :]
    group = even[0].shape[0]
    copies = load_copies(x_hbm, held, sems)
    for copy in copies:
        copy.start()
    lead_tab = tab[:, :HALF]
    trail_tab = tab[:, HALF:]
    lead_lhs = spread(lead_tab, var_count)
    trail_lhs = spread(trail_tab, var_count)
    keep_rows = jnp.concatenate([lead_tab[s * group : (s + 1) * group] for s in keep], axis=0)
    keep_lhs = spread(keep_rows, var_count)
    half_slots = len(trail)
    own_lhs = spread(trail_tab[: half_slots * group], var_count)
    for j in range(0, held.shape[0], 2):
        copies[j].wait()
        copies[j + 1].wait()
        first = columns(held, j, 0, var_count)
        second = columns(held, j, 1, var_count)
        whole = mm(lead_lhs, first) + mm(trail_lhs, second)
        kept = mm(keep_lhs, second)
        own = mm(own_lhs, first)
        for value, targets in ((whole, even), (kept, lead), (own, trail)):
            total = len(targets) * group
            for v in range(var_count):
                for s, target in enumerate(targets):
                    low = v * total + s * group
                    target[:, v * points + j * LANES : v * points + (j + 2) * LANES] = value[
                        low : low + group
                    ].astype(target.dtype)


def join_kernel(half_slots, group, *refs):
    lead = refs[:half_slots]
    trail = refs[half_slots : 2 * half_slots]
    from_above, from_below = refs[2 * half_slots : 2 * half_slots + 2]
    outs = refs[2 * half_slots + 2 :]
    for i in range(half_slots):
        above = (i + half_slots - 1) % half_slots
        outs[i][...] = (
            lead[i][...] + from_above[above * group : (above + 1) * group, :]
        ).astype(BF16)
        outs[half_slots + i][...] = (
            trail[i][...] + from_below[i * group : (i + 1) * group, :]
        ).astype(BF16)


def gram_kernel(slots, group, var_count, points, weights, classes, *refs):
    half_slots = slots // 2
    even = refs[:slots]
    above = refs[slots : slots + half_slots]
    below = refs[slots + half_slots : 2 * slots]
    last = refs[2 * slots : 2 * slots + half_slots]
    packed, spectra, sems = refs[2 * slots + half_slots :]
    blocks = 2 * slots
    me = lax.axis_index("blk")

    def place(source, block, sem):
        return pltpu.make_async_copy(source, spectra.at[pl.ds(block * group, group), :], sem)

    copies = []
    for s in range(slots):
        copies.append(place(even[s], 2 * ((me + slots - s) % slots), sems.at[s]))
    for copy in copies:
        copy.start()
    offsets = [0] + list(range(half_slots + 1, slots))
    for i, s in enumerate(offsets):
        copy = place(above[i], 2 * ((me + slots - s) % slots) + 1, sems.at[slots + i])
        copy.start()
        copies.append(copy)
    for i in range(half_slots):
        block = (2 * ((me + slots - i) % slots) + blocks - 1) % blocks
        sem = sems.at[slots + half_slots + i]

        @pl.when(me == i)
        def _():
            place(last[i], block, sem).start()

        @pl.when(me != i)
        def _():
            place(below[i], block, sem).start()

        copies.append(place(below[i], block, sem))
    picked = jnp.zeros(classes.shape, F32)
    for k in range(weights.shape[0]):
        picked = picked + jnp.where(classes[...] == k, weights[k], jnp.float32(0.0))
    wide = jnp.concatenate([picked] * var_count, axis=1)
    for copy in copies:
        copy.wait()
    left = spectra[...]
    right = (left.astype(F32) * wide).astype(BF16)
    gram = lax.dot_general(
        left, right, (((1,), (1,)), ((), ())), preferred_element_type=F32
    )
    size = blocks * group
    freqs = group // 2
    same = iota((size, size), 0) % freqs == iota((size, size), 1) % freqs
    gram = jnp.where(same, gram, 0.0).reshape(blocks, 2, freqs, size)
    rows_re = gram[:, 0].reshape(blocks * freqs, size)
    rows_im = gram[:, 1].reshape(blocks * freqs, size)
    width = 2 * blocks * blocks
    row, lane = (iota((size, width), 0), iota((size, width), 1))
    fits = row // group == lane % blocks
    row_part = row // freqs % 2
    lane_part = lane // blocks % 2
    from_re = one_hot(fits & (row_part == lane_part))
    sign = jnp.where(lane_part == 0, 1.0, -1.0)
    from_im = jnp.where(fits & (row_part != lane_part), sign, 0.0).astype(BF16)
    total = jnp.zeros((blocks * freqs, width), F32)
    for part_re, part_im in zip(split3(rows_re), split3(rows_im)):
        total = total + (mm(part_re, from_re) + mm(part_im, from_im))
    mine = iota((freqs, width), 1) // (2 * blocks)
    out = jnp.zeros((freqs, width), F32)
    for b in range(blocks):
        out = out + jnp.where(mine == b, total[b * freqs : (b + 1) * freqs], 0.0)
    packed[...] = out


def mode_kernel(blocks, var_count, points, scaling, feature_count, a_ref, b_ref, spectra, csd, eig, modes):
    raw = a_ref[...] + b_ref[...]
    freqs, width = raw.shape
    group = 2 * freqs
    size = blocks * group
    mat = scaling * raw
    lane_part = iota((freqs, width), 1) // blocks % 2
    is_re = lane_part == 0
    gather = one_hot(
        iota((width, width), 0) // (2 * blocks) == iota((width, width), 1) % blocks
    )

    def apply(matrix, vec_re, vec_im):
        top = matrix * jnp.where(is_re, vec_re, -vec_im)
        bottom = matrix * jnp.where(is_re, vec_im, vec_re)
        both = jnp.concatenate([top, bottom], axis=0)
        parts = jnp.concatenate([p.astype(F32) for p in split3(both)], axis=0).astype(BF16)
        got = mm(parts, gather)
        got = got[: 2 * freqs] + got[2 * freqs : 4 * freqs] + got[4 * freqs :]
        return (got[:freqs], got[freqs:])

    def over_blocks(x):
        return jnp.sum(x, axis=1, keepdims=True) * jnp.float32(1.0 / (2 * blocks))

    vec_re = jnp.full((freqs, width), 1.0 / math.sqrt(blocks), F32)
    vec_im = jnp.zeros((freqs, width), F32)
    for _ in range(ITERS):
        out_re, out_im = apply(mat, vec_re, vec_im)
        length = jnp.sqrt(over_blocks(out_re * out_re + out_im * out_im))
        vec_re, vec_im = (out_re / length, out_im / length)
    out_re, out_im = apply(mat, vec_re, vec_im)
    value = over_blocks(vec_re * out_re + vec_im * out_im)
    diagonal = iota((freqs, freqs), 0) == iota((freqs, freqs), 1)
    eig[...] = jnp.sum(
        jnp.where(diagonal, jnp.broadcast_to(value, (freqs, freqs)), 0.0), axis=0, keepdims=True
    )
    low_re = vec_re.astype(BF16)
    low_im = vec_im.astype(BF16)
    out_re, out_im = apply(raw, low_re.astype(F32), low_im.astype(F32))
    normsq = over_blocks(low_re.astype(F32) * out_re + low_im.astype(F32) * out_im)
    scale = jnp.sqrt(jnp.float32(feature_count) / normsq)
    row, lane = (iota((width, size), 0), iota((width, size), 1))
    expand = one_hot(row == lane // group)
    wide = mm(jnp.concatenate([vec_re, vec_im], axis=0).astype(BF16), expand)
    wide_re, wide_im = (wide[:freqs], wide[freqs:])
    part = iota((freqs, size), 1) // freqs % 2
    mine = iota((freqs, size), 1) % freqs == iota((freqs, size), 0)
    coef_re = jnp.where(mine, jnp.where(part == 0, wide_re, -wide_im), 0.0)
    coef_im = jnp.where(mine, jnp.where(part == 0, wide_im, wide_re), 0.0)
    rows = 2 * var_count
    upper = iota((rows, size), 0) < var_count
    var = iota((rows, size), 0) % var_count
    tall = []
    for f in range(freqs):
        both = jnp.where(
            upper,
            jnp.broadcast_to(coef_re[f : f + 1], (rows, size)),
            jnp.broadcast_to(coef_im[f : f + 1], (rows, size)),
        )
        tall.append(
            jnp.concatenate([jnp.where(var == v, both, 0.0) for v in range(var_count)], axis=1)
        )
    coef = jnp.concatenate(tall, axis=0).astype(BF16)
    stacked = jnp.concatenate(
        [spectra[:, v * points : (v + 1) * points] for v in range(var_count)], axis=0
    )
    phi = mm(coef, stacked)
    for f in range(freqs):
        block = phi[f * rows : (f + 1) * rows] * scale[f : f + 1, :]
        for k in range(2):
            modes[f, k] = block[k * var_count : (k + 1) * var_count]
    tiles = jnp.concatenate(
        [
            jnp.where(
                iota((blocks, width), 1) // (2 * blocks) == iota((blocks, width), 0),
                jnp.broadcast_to(mat[f : f + 1], (blocks, width)),
                0.0,
            )
            for f in range(freqs)
        ],
        axis=0,
    )
    for k in range(2):
        row, lane = (iota((width, blocks), 0), iota((width, blocks), 1))
        fold = one_hot(row % (2 * blocks) == lane + k * blocks)
        got = jnp.zeros((freqs * blocks, blocks), F32)
        for piece in split3(tiles):
            got = got + mm(piece, fold)
        for f in range(freqs):
            csd[f, k] = got[f * blocks : (f + 1) * blocks]


def call(kernel, outs, ins, inputs, scratch, flops, moved):
    vmem = pl.BlockSpec(memory_space=pltpu.VMEM)
    return pl.pallas_call(
        kernel,
        out_shape=outs,
        in_specs=ins,
        out_specs=jax.tree.map(lambda _: vmem, outs),
        scratch_shapes=scratch,
        compiler_params=pltpu.CompilerParams(vmem_limit_bytes=VMEM_LIMIT),
        cost_estimate=pl.CostEstimate(flops=flops, bytes_accessed=moved, transcendentals=0),
    )(*inputs)


def on_device(snapshots, freq_index, weight_class, class_weight):
    row_count, var_count, points = snapshots.shape
    features = var_count * points
    slots = lax.axis_size("blk")
    half_slots = slots // 2
    me = lax.axis_index("blk")
    freqs = freq_index.shape[0] // slots
    group = 2 * freqs
    blocks = 2 * slots
    vmem = pl.BlockSpec(memory_space=pltpu.VMEM)
    smem = pl.BlockSpec(memory_space=pltpu.SMEM)
    hbm = pl.BlockSpec(memory_space=pl.ANY)
    shape = jax.ShapeDtypeStruct
    held = [
        pltpu.VMEM((points // LANES, row_count, var_count, LANES), BF16),
        pltpu.SemaphoreType.DMA((points // LANES,)),
    ]

    turned = lax.dynamic_slice(
        jnp.concatenate([freq_index, freq_index]), (me * freqs,), (freq_index.shape[0],)
    )
    table = transform_table(turned, freqs)
    down_rows = (half_slots * group, slots * group)
    up_rows = (group, (half_slots + 1) * group)
    wide = half_slots * group
    halo = [shape((wide, features), F32)] * 2
    down, up = call(
        functools.partial(halo_kernel, down_rows, up_rows, var_count, points),
        halo,
        [vmem, hbm],
        (table, snapshots),
        held,
        2 * 2 * wide * HALF * features * var_count,
        2 * row_count * features,
    )
    below = [(i, i + 1) for i in range(slots - 1)]
    from_above = lax.ppermute(down, "blk", [(b, a) for a, b in below])
    from_below = lax.ppermute(up, "blk", below)

    keep = [0] + list(range(half_slots + 1, slots))
    piece = shape((group, features), BF16)
    wide_piece = shape((group, features), F32)
    table, _ = lax.optimization_barrier((table, down))
    pieces = call(
        functools.partial(block_kernel, slots, keep, var_count, points),
        [piece] * slots + [wide_piece] * (2 * half_slots),
        [vmem, hbm],
        (table, snapshots),
        held,
        2 * 3 * slots * group * HALF * features * var_count,
        2 * row_count * features,
    )
    even = pieces[:slots]

    def shift(x, s, pairs=None):
        pairs = [(i, (i + s) % slots) for i in range(slots)]
        return lax.ppermute(x, "blk", pairs)

    even = [even[0]] + [shift(even[s], s) for s in range(1, slots)]
    last = [
        lax.ppermute(
            up[i * group : (i + 1) * group].astype(BF16), "blk", [(slots - 1, i)]
        )
        for i in range(half_slots)
    ]
    odd = call(
        functools.partial(join_kernel, half_slots, group),
        [piece] * slots,
        [vmem] * (slots + 2),
        (*pieces[slots:], from_above, from_below),
        [],
        slots * group * features,
        10 * slots * group * features,
    )
    above = [odd[0]] + [shift(odd[i], s) for i, s in enumerate(keep) if i]
    under = [odd[half_slots]]
    for i in range(1, half_slots):
        pairs = [(a, (a + i) % slots) for a in range(1, slots)]
        under.append(lax.ppermute(odd[half_slots + i], "blk", pairs))
    width = 2 * blocks * blocks
    packed, spectra = call(
        functools.partial(gram_kernel, slots, group, var_count, points),
        [shape((freqs, width), F32), shape((blocks * group, features), BF16)],
        [smem, vmem] + [hbm] * (2 * slots + half_slots),
        (class_weight, weight_class.reshape(1, points), *even, *above, *under, *last),
        [pltpu.SemaphoreType.DMA((2 * slots,))],
        2 * (blocks * group) ** 2 * features,
        4 * blocks * group * features,
    )
    devices = lax.axis_size("pts")
    step = 1
    other = None
    while step < devices:
        if other is not None:
            packed = packed + other
        other = lax.ppermute(packed, "pts", [(i, i ^ step) for i in range(devices)])
        step *= 2
    total_features = features * devices
    csd, eigval, modes = call(
        functools.partial(
            mode_kernel,
            blocks,
            var_count,
            points,
            1.0 / (total_features * (3.0 * NFFT / 8.0)),
            total_features,
        ),
        [
            shape((freqs, 2, blocks, blocks), F32),
            shape((1, freqs), F32),
            shape((freqs, 2, var_count, points), F32),
        ],
        [vmem] * 3,
        (packed, other, spectra),
        [],
        2 * 2 * blocks * group * group * features,
        2 * blocks * group * features,
    )
    return (csd, eigval.reshape(freqs), modes)


def solution(mesh):
    in_specs = (P("blk", None, "pts"), P(), P("pts"), P())
    out_specs = (P("blk", None, None, None), P("blk"), P("blk", None, None, "pts"))
    return jax.shard_map(
        on_device, mesh=mesh, in_specs=in_specs, out_specs=out_specs, check_vma=False
    )
```

```python
import functools
import math

import jax
import jax.numpy as jnp
from jax import lax
from jax.experimental import pallas as pl
from jax.experimental.pallas import tpu as pltpu
from jax.sharding import PartitionSpec as P

NFFT = 768
HALF = NFFT // 2
ITERS = 3
LANES = 128
VMEM_LIMIT = 48 * 1024 * 1024
F32 = jnp.float32
BF16 = jnp.bfloat16


def iota(shape, axis):
    return lax.broadcasted_iota(jnp.int32, shape, axis)


def mm(a, b):
    return jnp.dot(a, b, preferred_element_type=F32)


def split3(x):
    high = x.astype(BF16)
    rest = x - high.astype(F32)
    mid = rest.astype(BF16)
    low = (rest - mid.astype(F32)).astype(BF16)
    return (high, mid, low)


def one_hot(condition):
    return jnp.where(condition, 1.0, 0.0).astype(BF16)


def modulo(x, n):
    return jnp.where(x < 0, x + n, x)


def block_of(slot, me, slots):
    half_slots = slots // 2
    above = slot - slots
    below = above - half_slots
    even = 2 * modulo(me - slot, slots)
    upper = 2 * modulo(me - jnp.where(above == 0, 0, above + half_slots), slots) + 1
    lower = modulo(2 * modulo(me - below, slots) - 1, 2 * slots)
    return jnp.where(slot < slots, even, jnp.where(below < 0, upper, lower))


def transform_rows(freqs, me, wanted, slots, group, start):
    count = group // 2
    times = start + iota((count, HALF), 1)
    window = 0.5 - 0.5 * jnp.cos(2.0 * math.pi / NFFT * times.astype(F32))
    row = iota((count, HALF), 0)
    out = []
    for s in wanted:
        owner = lax.rem(me + s, slots)
        freq = jnp.zeros((count, HALF), jnp.int32)
        for f in range(count):
            freq = jnp.where(row == f, freqs[owner * count + f], freq)
        product = freq * times
        thirds = ((product >> 8) * 21846) >> 16
        angle = 2.0 * math.pi / NFFT * (product - NFFT * thirds).astype(F32)
        out.append(window * jnp.cos(angle))
        out.append(-window * jnp.sin(angle))
    return jnp.concatenate(out, axis=0).astype(BF16)


def spread(rows, var_count):
    width = HALF * var_count
    pick = one_hot(iota((HALF, width), 1) // var_count == iota((HALF, width), 0))
    wide = mm(rows, pick)
    owner = iota(wide.shape, 1) % var_count
    return [jnp.where(owner == v, wide, 0.0).astype(BF16) for v in range(var_count)]


def load_copies(x_hbm, held, sems):
    rows = held.shape[1]
    return [
        pltpu.make_async_copy(
            x_hbm.at[pl.ds(0, rows), :, pl.ds(j * LANES, LANES)], held.at[j], sems.at[j]
        )
        for j in range(held.shape[0])
    ]


def columns(held, j, half, var_count):
    rows = HALF * var_count
    total = held.shape[1] * var_count
    parts = [
        held.at[j + i].reshape(total, LANES)[half * rows : (half + 1) * rows, :]
        for i in range(2)
    ]
    return jnp.concatenate(parts, axis=1)


def down_kernel(slots, group, var_count, points, freqs, x_hbm, down, lhs, held, sems):
    copies = load_copies(x_hbm, held, sems)
    for copy in copies:
        copy.start()
    me = lax.axis_index("blk")
    count = down.shape[0]
    rows = transform_rows(freqs, me, range(slots // 2, slots), slots, group, HALF)
    for v, part in enumerate(spread(rows, var_count)):
        lhs[v * count : (v + 1) * count, :] = part
    for j in range(0, held.shape[0], 2):
        copies[j].wait()
        copies[j + 1].wait()
        got = mm(lhs[...], columns(held, j, 0, var_count))
        for v in range(var_count):
            down[:, v * points + j * LANES : v * points + (j + 2) * LANES] = got[
                v * count : (v + 1) * count
            ]


def block_kernel(slots, keep, var_count, points, freqs, x_hbm, _, *refs):
    outs, (lhs, held, sems) = (refs[:-3], refs[-3:])
    half_slots = slots // 2
    up = outs[0]
    even = outs[1 : 1 + slots]
    lead = outs[1 + slots : 1 + slots + half_slots]
    trail = outs[1 + slots + half_slots :]
    group = even[0].shape[0]
    copies = load_copies(x_hbm, held, sems)
    for copy in copies:
        copy.start()
    me = lax.axis_index("blk")
    full = slots * group
    lead_rows = transform_rows(freqs, me, range(slots), slots, group, 0)
    trail_rows = transform_rows(freqs, me, range(slots), slots, group, HALF)
    both = spread(jnp.concatenate([lead_rows, trail_rows], axis=0), var_count)
    for v, part in enumerate(both):
        lhs[2 * v * full : 2 * (v + 1) * full, :] = part
    short = full + half_slots * group
    for j in range(0, held.shape[0], 2):
        copies[j].wait()
        copies[j + 1].wait()
        wanted = [lhs[2 * v * full : 2 * v * full + short, :] for v in range(var_count)]
        first = mm(jnp.concatenate(wanted, axis=0), columns(held, j, 0, var_count))
        second = mm(lhs[...], columns(held, j, 1, var_count))
        for v in range(var_count):
            low = v * points + j * LANES
            high = low + 2 * LANES
            top = first[v * short : (v + 1) * short]
            bottom = second[2 * v * full : 2 * (v + 1) * full]
            whole = (top[:full] + bottom[full:]).astype(BF16)
            for s in range(slots):
                even[s][:, low:high] = whole[s * group : (s + 1) * group]
            up[:, low:high] = bottom[group : group + half_slots * group]
            for s, target in zip(keep, lead):
                target[:, low:high] = bottom[s * group : (s + 1) * group]
            for s, target in enumerate(trail):
                target[:, low:high] = top[full + s * group : full + (s + 1) * group]


def join_kernel(half_slots, group, *refs):
    lead = refs[:half_slots]
    trail = refs[half_slots : 2 * half_slots]
    from_above, from_below = refs[2 * half_slots : 2 * half_slots + 2]
    outs = refs[2 * half_slots + 2 :]
    for i in range(half_slots):
        above = (i + half_slots - 1) % half_slots
        outs[i][...] = (
            lead[i][...] + from_above[above * group : (above + 1) * group, :]
        ).astype(BF16)
        outs[half_slots + i][...] = (
            trail[i][...] + from_below[i * group : (i + 1) * group, :]
        ).astype(BF16)


def gather_pieces(refs, slots, me):
    half_slots = slots // 2
    found = [ref[...] for ref in refs[: slots + half_slots]]
    for i in range(half_slots):
        below = refs[slots + half_slots + i][...]
        last = refs[2 * slots + i][...]
        found.append(jnp.where(me == i, last, below))
    return found


def gram_kernel(slots, group, var_count, points, weights, classes, *refs):
    packed = refs[-1]
    blocks = 2 * slots
    me = lax.axis_index("blk")
    picked = jnp.zeros(classes.shape, F32)
    for k in range(weights.shape[0]):
        picked = picked + jnp.where(classes[...] == k, weights[k], jnp.float32(0.0))
    wide = jnp.concatenate([picked] * var_count, axis=1)
    left = jnp.concatenate(gather_pieces(refs[:-1], slots, me), axis=0)
    right = (left.astype(F32) * wide).astype(BF16)
    gram = lax.dot_general(
        left, right, (((1,), (1,)), ((), ())), preferred_element_type=F32
    )
    size = blocks * group
    freqs = group // 2
    same = iota((size, size), 0) % freqs == iota((size, size), 1) % freqs
    gram = jnp.where(same, gram, 0.0).reshape(blocks, 2, freqs, size)
    rows_re = gram[:, 0].reshape(blocks * freqs, size)
    rows_im = gram[:, 1].reshape(blocks * freqs, size)
    width = 2 * blocks * blocks
    row, lane = (iota((size, width), 0), iota((size, width), 1))
    fits = block_of(row // group, me, slots) == lane % blocks
    row_part = row // freqs % 2
    lane_part = lane // blocks % 2
    from_re = one_hot(fits & (row_part == lane_part))
    sign = jnp.where(lane_part == 0, 1.0, -1.0)
    from_im = jnp.where(fits & (row_part != lane_part), sign, 0.0).astype(BF16)
    total = jnp.zeros((blocks * freqs, width), F32)
    for part_re, part_im in zip(split3(rows_re), split3(rows_im)):
        total = total + (mm(part_re, from_re) + mm(part_im, from_im))
    mine = iota((freqs, width), 1) // (2 * blocks)
    out = jnp.zeros((freqs, width), F32)
    for b in range(blocks):
        block = block_of(jnp.int32(b), me, slots)
        out = out + jnp.where(mine == block, total[b * freqs : (b + 1) * freqs], 0.0)
    packed[...] = out


def mode_kernel(slots, var_count, points, scaling, feature_count, a_ref, b_ref, *refs):
    csd, eig, modes = refs[-3:]
    blocks = 2 * slots
    me = lax.axis_index("blk")
    spectra = gather_pieces(refs[:-3], slots, me)
    raw = a_ref[...] + b_ref[...]
    freqs, width = raw.shape
    group = 2 * freqs
    size = blocks * group
    mat = scaling * raw
    lane_part = iota((freqs, width), 1) // blocks % 2
    is_re = lane_part == 0
    gather = one_hot(
        iota((width, width), 0) // (2 * blocks) == iota((width, width), 1) % blocks
    )

    def apply(matrix, vec_re, vec_im):
        top = matrix * jnp.where(is_re, vec_re, -vec_im)
        bottom = matrix * jnp.where(is_re, vec_im, vec_re)
        both = jnp.concatenate([top, bottom], axis=0)
        parts = jnp.concatenate([p.astype(F32) for p in split3(both)], axis=0).astype(BF16)
        got = mm(parts, gather)
        got = got[: 2 * freqs] + got[2 * freqs : 4 * freqs] + got[4 * freqs :]
        return (got[:freqs], got[freqs:])

    def over_blocks(x):
        return jnp.sum(x, axis=1, keepdims=True) * jnp.float32(1.0 / (2 * blocks))

    vec_re = jnp.full((freqs, width), 1.0 / math.sqrt(blocks), F32)
    vec_im = jnp.zeros((freqs, width), F32)
    for _ in range(ITERS):
        out_re, out_im = apply(mat, vec_re, vec_im)
        length = jnp.sqrt(over_blocks(out_re * out_re + out_im * out_im))
        vec_re, vec_im = (out_re / length, out_im / length)
    out_re, out_im = apply(mat, vec_re, vec_im)
    value = over_blocks(vec_re * out_re + vec_im * out_im)
    diagonal = iota((freqs, freqs), 0) == iota((freqs, freqs), 1)
    eig[...] = jnp.sum(
        jnp.where(diagonal, jnp.broadcast_to(value, (freqs, freqs)), 0.0), axis=0, keepdims=True
    )
    low_re = vec_re.astype(BF16)
    low_im = vec_im.astype(BF16)
    out_re, out_im = apply(raw, low_re.astype(F32), low_im.astype(F32))
    normsq = over_blocks(low_re.astype(F32) * out_re + low_im.astype(F32) * out_im)
    scale = jnp.sqrt(jnp.float32(feature_count) / normsq)
    row, lane = (iota((width, size), 0), iota((width, size), 1))
    expand = one_hot(row == block_of(lane // group, me, slots))
    wide = mm(jnp.concatenate([vec_re, vec_im], axis=0).astype(BF16), expand)
    wide_re, wide_im = (wide[:freqs], wide[freqs:])
    part = iota((freqs, size), 1) // freqs % 2
    mine = iota((freqs, size), 1) % freqs == iota((freqs, size), 0)
    coef_re = jnp.where(mine, jnp.where(part == 0, wide_re, -wide_im), 0.0)
    coef_im = jnp.where(mine, jnp.where(part == 0, wide_im, wide_re), 0.0)
    rows = 2 * var_count
    upper = iota((rows, size), 0) < var_count
    var = iota((rows, size), 0) % var_count
    tall = []
    for f in range(freqs):
        both = jnp.where(
            upper,
            jnp.broadcast_to(coef_re[f : f + 1], (rows, size)),
            jnp.broadcast_to(coef_im[f : f + 1], (rows, size)),
        )
        tall.append(
            jnp.concatenate([jnp.where(var == v, both, 0.0) for v in range(var_count)], axis=1)
        )
    coef = jnp.concatenate(tall, axis=0).astype(BF16)
    stacked = jnp.concatenate(
        [
            piece[:, v * points : (v + 1) * points]
            for v in range(var_count)
            for piece in spectra
        ],
        axis=0,
    )
    phi = mm(coef, stacked)
    for f in range(freqs):
        block = phi[f * rows : (f + 1) * rows] * scale[f : f + 1, :]
        for k in range(2):
            modes[f, k] = block[k * var_count : (k + 1) * var_count]
    tiles = jnp.concatenate(
        [
            jnp.where(
                iota((blocks, width), 1) // (2 * blocks) == iota((blocks, width), 0),
                jnp.broadcast_to(mat[f : f + 1], (blocks, width)),
                0.0,
            )
            for f in range(freqs)
        ],
        axis=0,
    )
    for k in range(2):
        row, lane = (iota((width, blocks), 0), iota((width, blocks), 1))
        fold = one_hot(row % (2 * blocks) == lane + k * blocks)
        got = jnp.zeros((freqs * blocks, blocks), F32)
        for piece in split3(tiles):
            got = got + mm(piece, fold)
        for f in range(freqs):
            csd[f, k] = got[f * blocks : (f + 1) * blocks]


def call(kernel, outs, ins, inputs, scratch, flops, moved):
    vmem = pl.BlockSpec(memory_space=pltpu.VMEM)
    return pl.pallas_call(
        kernel,
        out_shape=outs,
        in_specs=ins,
        out_specs=jax.tree.map(lambda _: vmem, outs),
        scratch_shapes=scratch,
        compiler_params=pltpu.CompilerParams(vmem_limit_bytes=VMEM_LIMIT),
        cost_estimate=pl.CostEstimate(flops=flops, bytes_accessed=moved, transcendentals=0),
    )(*inputs)


def on_device(snapshots, freq_index, weight_class, class_weight):
    row_count, var_count, points = snapshots.shape
    features = var_count * points
    slots = lax.axis_size("blk")
    half_slots = slots // 2
    me = lax.axis_index("blk")
    freqs = freq_index.shape[0] // slots
    group = 2 * freqs
    blocks = 2 * slots
    vmem = pl.BlockSpec(memory_space=pltpu.VMEM)
    smem = pl.BlockSpec(memory_space=pltpu.SMEM)
    hbm = pl.BlockSpec(memory_space=pl.ANY)
    shape = jax.ShapeDtypeStruct

    def scratch(rows, halves):
        return [
            pltpu.VMEM((rows * var_count, HALF * var_count), BF16),
            pltpu.VMEM((points // LANES, halves * HALF, var_count, LANES), BF16),
            pltpu.SemaphoreType.DMA((points // LANES,)),
        ]

    wide = half_slots * group
    down = call(
        functools.partial(down_kernel, slots, group, var_count, points),
        shape((wide, features), F32),
        [smem, hbm],
        (freq_index, snapshots),
        scratch(wide, 1),
        2 * wide * HALF * features * var_count,
        row_count * features,
    )
    below = [(i, i + 1) for i in range(slots - 1)]
    from_above = lax.ppermute(down, "blk", [(b, a) for a, b in below])
    keep = [0] + list(range(half_slots + 1, slots))
    piece = shape((group, features), BF16)
    wide_piece = shape((group, features), F32)
    up, *pieces = call(
        functools.partial(block_kernel, slots, keep, var_count, points),
        [shape((wide, features), F32)] + [piece] * slots + [wide_piece] * (2 * half_slots),
        [smem, hbm, hbm],
        (freq_index, snapshots, down),
        scratch(2 * slots * group, 2),
        2 * 4 * slots * group * HALF * features * var_count,
        2 * row_count * features,
    )
    from_below = lax.ppermute(up, "blk", below)
    even = pieces[:slots]

    def shift(x, s, pairs=None):
        pairs = [(i, (i + s) % slots) for i in range(slots)]
        return lax.ppermute(x, "blk", pairs)

    even = [even[0]] + [shift(even[s], s) for s in range(1, slots)]
    last = [
        lax.ppermute(
            up[i * group : (i + 1) * group].astype(BF16), "blk", [(slots - 1, i)]
        )
        for i in range(half_slots)
    ]
    odd = call(
        functools.partial(join_kernel, half_slots, group),
        [piece] * slots,
        [vmem] * (slots + 2),
        (*pieces[slots:], from_above, from_below),
        [],
        slots * group * features,
        10 * slots * group * features,
    )
    above = [odd[0]] + [shift(odd[i], s) for i, s in enumerate(keep) if i]
    under = [odd[half_slots]]
    for i in range(1, half_slots):
        pairs = [(a, (a + i) % slots) for a in range(1, slots)]
        under.append(lax.ppermute(odd[half_slots + i], "blk", pairs))
    width = 2 * blocks * blocks
    spectra = (*even, *above, *under, *last)
    packed = call(
        functools.partial(gram_kernel, slots, group, var_count, points),
        shape((freqs, width), F32),
        [smem, vmem] + [vmem] * len(spectra),
        (class_weight, weight_class.reshape(1, points), *spectra),
        [],
        2 * (blocks * group) ** 2 * features,
        4 * blocks * group * features,
    )
    devices = lax.axis_size("pts")
    step = 1
    other = None
    while step < devices:
        if other is not None:
            packed = packed + other
        other = lax.ppermute(packed, "pts", [(i, i ^ step) for i in range(devices)])
        step *= 2
    total_features = features * devices
    csd, eigval, modes = call(
        functools.partial(
            mode_kernel,
            slots,
            var_count,
            points,
            1.0 / (total_features * (3.0 * NFFT / 8.0)),
            total_features,
        ),
        [
            shape((freqs, 2, blocks, blocks), F32),
            shape((1, freqs), F32),
            shape((freqs, 2, var_count, points), F32),
        ],
        [vmem] * (2 + len(spectra)),
        (packed, other, *spectra),
        [],
        2 * 2 * blocks * group * group * features,
        2 * blocks * group * features,
    )
    return (csd, eigval.reshape(freqs), modes)


def solution(mesh):
    in_specs = (P("blk", None, "pts"), P(), P("pts"), P())
    out_specs = (P("blk", None, None, None), P("blk"), P("blk", None, None, "pts"))
    return jax.shard_map(
        on_device, mesh=mesh, in_specs=in_specs, out_specs=out_specs, check_vma=False
    )
```

```python
import functools
import math

import jax
import jax.numpy as jnp
from jax import lax
from jax.experimental import pallas as pl
from jax.experimental.pallas import tpu as pltpu
from jax.sharding import PartitionSpec as P

NFFT = 768
HALF = NFFT // 2
ITERS = 3
LANES = 128
VMEM_LIMIT = 32 * 1024 * 1024
F32 = jnp.float32
BF16 = jnp.bfloat16


def iota(shape, axis):
    return lax.broadcasted_iota(jnp.int32, shape, axis)


def mm(a, b):
    return jnp.dot(a, b, preferred_element_type=F32)


def split3(x):
    high = x.astype(BF16)
    rest = x - high.astype(F32)
    mid = rest.astype(BF16)
    low = (rest - mid.astype(F32)).astype(BF16)
    return (high, mid, low)


def one_hot(condition):
    return jnp.where(condition, 1.0, 0.0).astype(BF16)


def modulo(x, n):
    return jnp.where(x < 0, x + n, x)


def block_of(slot, me, slots):
    half_slots = slots // 2
    above = slot - slots
    below = above - half_slots
    even = 2 * slot
    upper = 2 * modulo(me - jnp.where(above == 0, 0, above + half_slots), slots) + 1
    lower = modulo(2 * modulo(me - below, slots) - 1, 2 * slots)
    return jnp.where(slot < slots, even, jnp.where(below < 0, upper, lower))


def trig(phase):
    quarter = ((phase + NFFT // 8) * 1366) >> 18
    angle = (2.0 * math.pi / NFFT) * (phase - (NFFT // 4) * quarter).astype(F32)
    x = angle * angle
    cos = 1.0 + x * (-1.0 / 2 + x * (1.0 / 24 + x * (-1.0 / 720 + x * (1.0 / 40320))))
    sin = 1.0 + x * (-1.0 / 6 + x * (1.0 / 120 + x * (-1.0 / 5040 + x * (1.0 / 362880))))
    sin = angle * sin
    odd = (quarter & 1) != 0
    real_part = jnp.where(odd, sin, cos)
    imag_part = jnp.where(odd, cos, sin)
    real_part = jnp.where(((quarter + 1) & 2) != 0, -real_part, real_part)
    imag_part = jnp.where((quarter & 2) != 0, -imag_part, imag_part)
    return (real_part, imag_part)


def transform_rows(freqs, me, slots, group, start):
    count = group // 2
    times = start + iota((count, HALF), 1)
    window = 0.5 - 0.5 * trig(times)[0]
    row = iota((count, HALF), 0)
    out = []
    for s in range(slots):
        owner = lax.rem(me + s, slots)
        freq = jnp.zeros((count, HALF), jnp.int32)
        for f in range(count):
            freq = jnp.where(row == f, freqs[owner * count + f], freq)
        product = freq * times
        turns = ((product >> 8) * 21846) >> 16
        real_part, imag_part = trig(product - NFFT * turns)
        out.append(window * real_part)
        out.append(-window * imag_part)
    return jnp.concatenate(out, axis=0).astype(BF16)


def spread(rows, var_count):
    width = HALF * var_count
    pick = one_hot(iota((HALF, width), 1) // var_count == iota((HALF, width), 0))
    wide = mm(rows, pick)
    owner = iota(wide.shape, 1) % var_count
    return [jnp.where(owner == v, wide, 0.0).astype(BF16) for v in range(var_count)]


def columns(held, j, half, var_count):
    rows = HALF * var_count
    parts = [
        held.at[j + i].reshape(2 * rows, LANES)[half * rows : (half + 1) * rows, :]
        for i in range(2)
    ]
    return jnp.concatenate(parts, axis=1)


def halo_kernel(slots, group, var_count, points, freqs, x_hbm, inner, outer, lhs, held, sems):
    copies = [
        pltpu.make_async_copy(x_hbm.at[:, :, pl.ds(j * LANES, LANES)], held.at[j], sems.at[j])
        for j in range(held.shape[0])
    ]
    for copy in copies:
        copy.start()
    me = lax.axis_index("blk")
    odd = lax.rem(me, 2) == 1
    full = slots * group
    wide = full // 2
    rows = [transform_rows(freqs, me, slots, group, start) for start in (0, HALF)]
    for v, part in enumerate(spread(jnp.concatenate(rows, axis=0), var_count)):
        lhs[2 * v * full : 2 * (v + 1) * full, :] = part

    def some(low):
        return jnp.concatenate(
            [lhs[2 * v * full + low : 2 * v * full + low + wide, :] for v in range(var_count)],
            axis=0,
        )

    for j in range(0, held.shape[0], 2):
        copies[j].wait()
        copies[j + 1].wait()
        down = mm(some(full + wide), columns(held, j, 0, var_count))
        up = mm(some(group), columns(held, j, 1, var_count))
        for v in range(var_count):
            low = v * points + j * LANES
            lower = down[v * wide : (v + 1) * wide]
            upper = up[v * wide : (v + 1) * wide]
            inner[:, low : low + 2 * LANES] = jnp.where(odd, upper, lower)
            outer[:, low : low + 2 * LANES] = jnp.where(odd, lower, upper)


def block_kernel(slots, keep, var_count, points, lhs, held, *outs):
    half_slots = slots // 2
    even = outs[0]
    lead = outs[1 : 1 + half_slots]
    trail = outs[1 + half_slots :]
    full = even.shape[0]
    group = full // slots
    short = full + half_slots * group
    me = lax.axis_index("blk")

    def some(v, low, high):
        return lhs[2 * v * full + low : 2 * v * full + high, :]

    for j in range(0, held.shape[0], 2):
        parts = [some(v, 0, short) for v in range(var_count)]
        first = mm(jnp.concatenate(parts, axis=0), columns(held, j, 0, var_count))
        parts = []
        for v in range(var_count):
            parts.append(some(v, full, 2 * full))
            parts.extend(some(v, s * group, (s + 1) * group) for s in keep)
        second = mm(jnp.concatenate(parts, axis=0), columns(held, j, 1, var_count))
        for v in range(var_count):
            low = v * points + j * LANES
            high = low + 2 * LANES
            top = first[v * short : (v + 1) * short]
            bottom = second[v * short : (v + 1) * short]
            whole = (top[:full] + bottom[:full]).astype(BF16)
            for s in range(slots):
                owner = pl.multiple_of(lax.rem(me + s, slots) * group, group)
                even[pl.ds(owner, group), low:high] = whole[s * group : (s + 1) * group]
            for i in range(half_slots):
                rows = slice(full + i * group, full + (i + 1) * group)
                lead[i][:, low:high] = bottom[rows]
                trail[i][:, low:high] = top[rows]


def join_kernel(half_slots, group, *refs):
    lead = refs[:half_slots]
    trail = refs[half_slots : 2 * half_slots]
    inner, outer = refs[2 * half_slots : 2 * half_slots + 2]
    outs = refs[2 * half_slots + 2 :]
    odd = lax.rem(lax.axis_index("blk"), 2) == 1
    for i in range(half_slots):
        above = (i + half_slots - 1) % half_slots
        rows = slice(above * group, (above + 1) * group)
        from_above = jnp.where(odd, inner[rows, :], outer[rows, :])
        outs[i][...] = (lead[i][...] + from_above).astype(BF16)
        rows = slice(i * group, (i + 1) * group)
        from_below = jnp.where(odd, outer[rows, :], inner[rows, :])
        outs[half_slots + i][...] = (trail[i][...] + from_below).astype(BF16)


def gather_pieces(refs, slots, me):
    half_slots = slots // 2
    even, above, below, last = (
        refs[0],
        refs[1 : 1 + half_slots],
        refs[1 + half_slots : 1 + slots],
        refs[1 + slots :],
    )
    found = [even[...]] + [ref[...] for ref in above]
    for i in range(half_slots):
        found.append(jnp.where(me == i, last[i][...], below[i][...]))
    return found


def gram_kernel(slots, group, var_count, points, weights, classes, *refs):
    packed = refs[-1]
    blocks = 2 * slots
    me = lax.axis_index("blk")
    picked = jnp.zeros(classes.shape, F32)
    for k in range(weights.shape[0]):
        picked = picked + jnp.where(classes[...] == k, weights[k], jnp.float32(0.0))
    wide = jnp.concatenate([picked] * var_count, axis=1)
    left = jnp.concatenate(gather_pieces(refs[:-1], slots, me), axis=0)
    right = (left.astype(F32) * wide).astype(BF16)
    gram = lax.dot_general(
        left, right, (((1,), (1,)), ((), ())), preferred_element_type=F32
    )
    size = blocks * group
    freqs = group // 2
    same = iota((size, size), 0) % freqs == iota((size, size), 1) % freqs
    gram = jnp.where(same, gram, 0.0).reshape(blocks, 2, freqs, size)
    rows_re = gram[:, 0].reshape(blocks * freqs, size)
    rows_im = gram[:, 1].reshape(blocks * freqs, size)
    width = 2 * blocks * blocks
    row, lane = (iota((size, width), 0), iota((size, width), 1))
    fits = block_of(row // group, me, slots) == lane % blocks
    row_part = row // freqs % 2
    lane_part = lane // blocks % 2
    from_re = one_hot(fits & (row_part == lane_part))
    sign = jnp.where(lane_part == 0, 1.0, -1.0)
    from_im = jnp.where(fits & (row_part != lane_part), sign, 0.0).astype(BF16)
    total = jnp.zeros((blocks * freqs, width), F32)
    for part_re, part_im in zip(split3(rows_re), split3(rows_im)):
        total = total + (mm(part_re, from_re) + mm(part_im, from_im))
    mine = iota((freqs, width), 1) // (2 * blocks)
    out = jnp.zeros((freqs, width), F32)
    for b in range(blocks):
        block = block_of(jnp.int32(b), me, slots)
        out = out + jnp.where(mine == block, total[b * freqs : (b + 1) * freqs], 0.0)
    packed[...] = out


def mode_kernel(slots, var_count, points, scaling, feature_count, a_ref, b_ref, *refs):
    csd, eig, modes = refs[-3:]
    blocks = 2 * slots
    me = lax.axis_index("blk")
    spectra = gather_pieces(refs[:-3], slots, me)
    raw = a_ref[...] + b_ref[...]
    freqs, width = raw.shape
    group = 2 * freqs
    size = blocks * group
    mat = scaling * raw
    lane_part = iota((freqs, width), 1) // blocks % 2
    is_re = lane_part == 0
    gather = one_hot(
        iota((width, width), 0) // (2 * blocks) == iota((width, width), 1) % blocks
    )

    def apply(matrix, vec_re, vec_im):
        top = matrix * jnp.where(is_re, vec_re, -vec_im)
        bottom = matrix * jnp.where(is_re, vec_im, vec_re)
        both = jnp.concatenate([top, bottom], axis=0)
        parts = jnp.concatenate([p.astype(F32) for p in split3(both)], axis=0).astype(BF16)
        got = mm(parts, gather)
        got = got[: 2 * freqs] + got[2 * freqs : 4 * freqs] + got[4 * freqs :]
        return (got[:freqs], got[freqs:])

    def over_blocks(x):
        return jnp.sum(x, axis=1, keepdims=True) * jnp.float32(1.0 / (2 * blocks))

    vec_re = jnp.full((freqs, width), 1.0 / math.sqrt(blocks), F32)
    vec_im = jnp.zeros((freqs, width), F32)
    for _ in range(ITERS):
        out_re, out_im = apply(mat, vec_re, vec_im)
        length = jnp.sqrt(over_blocks(out_re * out_re + out_im * out_im))
        vec_re, vec_im = (out_re / length, out_im / length)
    out_re, out_im = apply(mat, vec_re, vec_im)
    value = over_blocks(vec_re * out_re + vec_im * out_im)
    diagonal = iota((freqs, freqs), 0) == iota((freqs, freqs), 1)
    eig[...] = jnp.sum(
        jnp.where(diagonal, jnp.broadcast_to(value, (freqs, freqs)), 0.0), axis=0, keepdims=True
    )
    low_re = vec_re.astype(BF16)
    low_im = vec_im.astype(BF16)
    out_re, out_im = apply(raw, low_re.astype(F32), low_im.astype(F32))
    normsq = over_blocks(low_re.astype(F32) * out_re + low_im.astype(F32) * out_im)
    scale = jnp.sqrt(jnp.float32(feature_count) / normsq)
    row, lane = (iota((width, size), 0), iota((width, size), 1))
    expand = one_hot(row == block_of(lane // group, me, slots))
    wide = mm(jnp.concatenate([vec_re, vec_im], axis=0).astype(BF16), expand)
    wide_re, wide_im = (wide[:freqs], wide[freqs:])
    part = iota((freqs, size), 1) // freqs % 2
    mine = iota((freqs, size), 1) % freqs == iota((freqs, size), 0)
    coef_re = jnp.where(mine, jnp.where(part == 0, wide_re, -wide_im), 0.0)
    coef_im = jnp.where(mine, jnp.where(part == 0, wide_im, wide_re), 0.0)
    rows = 2 * var_count
    upper = iota((rows, size), 0) < var_count
    var = iota((rows, size), 0) % var_count
    tall = []
    for f in range(freqs):
        both = jnp.where(
            upper,
            jnp.broadcast_to(coef_re[f : f + 1], (rows, size)),
            jnp.broadcast_to(coef_im[f : f + 1], (rows, size)),
        )
        tall.append(
            jnp.concatenate([jnp.where(var == v, both, 0.0) for v in range(var_count)], axis=1)
        )
    coef = jnp.concatenate(tall, axis=0).astype(BF16)
    stacked = jnp.concatenate(
        [
            piece[:, v * points : (v + 1) * points]
            for v in range(var_count)
            for piece in spectra
        ],
        axis=0,
    )
    phi = mm(coef, stacked)
    for f in range(freqs):
        block = phi[f * rows : (f + 1) * rows] * scale[f : f + 1, :]
        for k in range(2):
            modes[f, k] = block[k * var_count : (k + 1) * var_count]
    tiles = jnp.concatenate(
        [
            jnp.where(
                iota((blocks, width), 1) // (2 * blocks) == iota((blocks, width), 0),
                jnp.broadcast_to(mat[f : f + 1], (blocks, width)),
                0.0,
            )
            for f in range(freqs)
        ],
        axis=0,
    )
    for k in range(2):
        row, lane = (iota((width, blocks), 0), iota((width, blocks), 1))
        fold = one_hot(row % (2 * blocks) == lane + k * blocks)
        got = jnp.zeros((freqs * blocks, blocks), F32)
        for piece in split3(tiles):
            got = got + mm(piece, fold)
        for f in range(freqs):
            csd[f, k] = got[f * blocks : (f + 1) * blocks]


def call(kernel, outs, ins, inputs, scratch, flops, moved):
    vmem = pl.BlockSpec(memory_space=pltpu.VMEM)
    return pl.pallas_call(
        kernel,
        out_shape=outs,
        in_specs=ins,
        out_specs=jax.tree.map(lambda _: vmem, outs),
        scratch_shapes=scratch,
        compiler_params=pltpu.CompilerParams(vmem_limit_bytes=VMEM_LIMIT),
        cost_estimate=pl.CostEstimate(flops=flops, bytes_accessed=moved, transcendentals=0),
    )(*inputs)


def on_device(snapshots, freq_index, weight_class, class_weight):
    row_count, var_count, points = snapshots.shape
    features = var_count * points
    slots = lax.axis_size("blk")
    half_slots = slots // 2
    me = lax.axis_index("blk")
    freqs = freq_index.shape[0] // slots
    group = 2 * freqs
    blocks = 2 * slots
    vmem = pl.BlockSpec(memory_space=pltpu.VMEM)
    smem = pl.BlockSpec(memory_space=pltpu.SMEM)
    hbm = pl.BlockSpec(memory_space=pltpu.HBM)
    shape = jax.ShapeDtypeStruct

    wide = half_slots * group
    groups = points // LANES
    inner, outer, lhs, held = call(
        functools.partial(halo_kernel, slots, group, var_count, points),
        [
            shape((wide, features), F32),
            shape((wide, features), F32),
            shape((2 * slots * group * var_count, HALF * var_count), BF16),
            shape((groups, row_count, var_count, LANES), BF16),
        ],
        [smem, hbm],
        (freq_index, pltpu.with_memory_space_constraint(snapshots, pltpu.HBM)),
        [pltpu.SemaphoreType.DMA((groups,))],
        2 * 2 * wide * HALF * features * var_count,
        2 * row_count * features,
    )

    def swap(x, first):
        pairs = [(i, i + 1) for i in range(first, slots - 1, 2)]
        return lax.ppermute(x, "blk", pairs + [(b, a) for a, b in pairs])

    swapped = (swap(inner, 1), swap(outer, 0))
    keep = [0] + list(range(half_slots + 1, slots))
    piece = shape((group, features), BF16)
    wide_piece = shape((group, features), F32)
    pieces = call(
        functools.partial(block_kernel, slots, keep, var_count, points),
        [shape((slots * group, features), BF16)] + [wide_piece] * (2 * half_slots),
        [vmem, vmem],
        (lhs, held),
        [],
        2 * 3 * slots * group * HALF * features * var_count,
        2 * row_count * features,
    )
    even = lax.all_to_all(pieces[0], "blk", split_axis=0, concat_axis=0, tiled=True)
    last = [
        lax.ppermute(
            inner[i * group : (i + 1) * group].astype(BF16), "blk", [(slots - 1, i)]
        )
        for i in range(half_slots)
    ]
    odd = call(
        functools.partial(join_kernel, half_slots, group),
        [piece] * slots,
        [vmem] * (slots + 2),
        (*pieces[1:], *swapped),
        [],
        slots * group * features,
        10 * slots * group * features,
    )

    def shift(x, s, first):
        return lax.ppermute(x, "blk", [(i, (i + s) % slots) for i in range(first, slots)])

    above = [odd[0]] + [shift(odd[i], s, 0) for i, s in enumerate(keep) if i]
    under = [odd[half_slots]] + [shift(odd[half_slots + i], i, 1) for i in range(1, half_slots)]
    width = 2 * blocks * blocks
    spectra = (even, *above, *under, *last)
    packed = call(
        functools.partial(gram_kernel, slots, group, var_count, points),
        shape((freqs, width), F32),
        [smem, vmem] + [vmem] * len(spectra),
        (class_weight, weight_class.reshape(1, points), *spectra),
        [],
        2 * (blocks * group) ** 2 * features,
        4 * blocks * group * features,
    )
    devices = lax.axis_size("pts")
    step = 1
    other = None
    while step < devices:
        if other is not None:
            packed = packed + other
        other = lax.ppermute(packed, "pts", [(i, i ^ step) for i in range(devices)])
        step *= 2
    total_features = features * devices
    csd, eigval, modes = call(
        functools.partial(
            mode_kernel,
            slots,
            var_count,
            points,
            1.0 / (total_features * (3.0 * NFFT / 8.0)),
            total_features,
        ),
        [
            shape((freqs, 2, blocks, blocks), F32),
            shape((1, freqs), F32),
            shape((freqs, 2, var_count, points), F32),
        ],
        [vmem] * (2 + len(spectra)),
        (packed, other, *spectra),
        [],
        2 * 2 * blocks * group * group * features,
        2 * blocks * group * features,
    )
    return (csd, eigval.reshape(freqs), modes)


def solution(mesh):
    in_specs = (P("blk", None, "pts"), P(), P("pts"), P())
    out_specs = (P("blk", None, None, None), P("blk"), P("blk", None, None, "pts"))
    return jax.shard_map(
        on_device, mesh=mesh, in_specs=in_specs, out_specs=out_specs, check_vma=False
    )
```

```python
import functools
import math

import jax
import jax.numpy as jnp
from jax import lax
from jax.experimental import pallas as pl
from jax.experimental.pallas import tpu as pltpu
from jax.sharding import PartitionSpec as P

NFFT = 768
HALF = NFFT // 2
ITERS = 3
LANES = 128
VMEM_LIMIT = 32 * 1024 * 1024
F32 = jnp.float32
BF16 = jnp.bfloat16


def iota(shape, axis):
    return lax.broadcasted_iota(jnp.int32, shape, axis)


def mm(a, b):
    return jnp.dot(a, b, preferred_element_type=F32)


def split3(x):
    high = x.astype(BF16)
    rest = x - high.astype(F32)
    mid = rest.astype(BF16)
    low = (rest - mid.astype(F32)).astype(BF16)
    return (high, mid, low)


def one_hot(condition):
    return jnp.where(condition, 1.0, 0.0).astype(BF16)


def modulo(x, n):
    return jnp.where(x < 0, x + n, x)


def block_of(slot, me, slots):
    half_slots = slots // 2
    above = slot - slots
    below = above - half_slots
    even = 2 * modulo(me - slot, slots)
    upper = 2 * modulo(me - jnp.where(above == 0, 0, above + half_slots), slots) + 1
    lower = modulo(2 * modulo(me - below, slots) - 1, 2 * slots)
    return jnp.where(slot < slots, even, jnp.where(below < 0, upper, lower))


def trig(phase):
    quarter = ((phase + NFFT // 8) * 1366) >> 18
    angle = (2.0 * math.pi / NFFT) * (phase - (NFFT // 4) * quarter).astype(F32)
    x = angle * angle
    cos = 1.0 + x * (-1.0 / 2 + x * (1.0 / 24 + x * (-1.0 / 720 + x * (1.0 / 40320))))
    sin = 1.0 + x * (-1.0 / 6 + x * (1.0 / 120 + x * (-1.0 / 5040 + x * (1.0 / 362880))))
    sin = angle * sin
    odd = (quarter & 1) != 0
    real_part = jnp.where(odd, sin, cos)
    imag_part = jnp.where(odd, cos, sin)
    real_part = jnp.where(((quarter + 1) & 2) != 0, -real_part, real_part)
    imag_part = jnp.where((quarter & 2) != 0, -imag_part, imag_part)
    return (real_part, imag_part)


def transform_rows(freqs, me, slots, group, start):
    count = group // 2
    times = start + iota((count, HALF), 1)
    window = 0.5 - 0.5 * trig(times)[0]
    row = iota((count, HALF), 0)
    out = []
    for s in range(slots):
        owner = lax.rem(me + s, slots)
        freq = jnp.zeros((count, HALF), jnp.int32)
        for f in range(count):
            freq = jnp.where(row == f, freqs[owner * count + f], freq)
        product = freq * times
        turns = ((product >> 8) * 21846) >> 16
        real_part, imag_part = trig(product - NFFT * turns)
        out.append(window * real_part)
        out.append(-window * imag_part)
    return jnp.concatenate(out, axis=0).astype(BF16)


def spread(rows, var_count):
    width = HALF * var_count
    pick = one_hot(iota((HALF, width), 1) // var_count == iota((HALF, width), 0))
    wide = mm(rows, pick)
    owner = iota(wide.shape, 1) % var_count
    return [jnp.where(owner == v, wide, 0.0).astype(BF16) for v in range(var_count)]


def columns(held, j, half, var_count):
    rows = HALF * var_count
    parts = [
        held.at[j + i].reshape(2 * rows, LANES)[half * rows : (half + 1) * rows, :]
        for i in range(2)
    ]
    return jnp.concatenate(parts, axis=1)


def halo_kernel(slots, group, var_count, points, freqs, x_hbm, inner, outer, lhs, held, sems):
    copies = [
        pltpu.make_async_copy(x_hbm.at[:, :, pl.ds(j * LANES, LANES)], held.at[j], sems.at[j])
        for j in range(held.shape[0])
    ]
    for copy in copies:
        copy.start()
    me = lax.axis_index("blk")
    odd = lax.rem(me, 2) == 1
    full = slots * group
    wide = full // 2
    rows = [transform_rows(freqs, me, slots, group, start) for start in (0, HALF)]
    for v, part in enumerate(spread(jnp.concatenate(rows, axis=0), var_count)):
        lhs[2 * v * full : 2 * (v + 1) * full, :] = part

    def some(low):
        return jnp.concatenate(
            [lhs[2 * v * full + low : 2 * v * full + low + wide, :] for v in range(var_count)],
            axis=0,
        )

    for j in range(0, held.shape[0], 2):
        copies[j].wait()
        copies[j + 1].wait()
        down = mm(some(full + wide), columns(held, j, 0, var_count))
        up = mm(some(group), columns(held, j, 1, var_count))
        for v in range(var_count):
            low = v * points + j * LANES
            lower = down[v * wide : (v + 1) * wide]
            upper = up[v * wide : (v + 1) * wide]
            inner[:, low : low + 2 * LANES] = jnp.where(odd, upper, lower)
            outer[:, low : low + 2 * LANES] = jnp.where(odd, lower, upper)


def block_kernel(slots, keep, var_count, points, lhs, held, *outs):
    half_slots = slots // 2
    even = outs[:slots]
    lead = outs[slots : slots + half_slots]
    trail = outs[slots + half_slots :]
    group = even[0].shape[0]
    full = slots * group
    short = full + half_slots * group

    def some(v, low, high):
        return lhs[2 * v * full + low : 2 * v * full + high, :]

    for j in range(0, held.shape[0], 2):
        parts = [some(v, 0, short) for v in range(var_count)]
        first = mm(jnp.concatenate(parts, axis=0), columns(held, j, 0, var_count))
        parts = []
        for v in range(var_count):
            parts.append(some(v, full, 2 * full))
            parts.extend(some(v, s * group, (s + 1) * group) for s in keep)
        second = mm(jnp.concatenate(parts, axis=0), columns(held, j, 1, var_count))
        for v in range(var_count):
            low = v * points + j * LANES
            high = low + 2 * LANES
            top = first[v * short : (v + 1) * short]
            bottom = second[v * short : (v + 1) * short]
            whole = (top[:full] + bottom[:full]).astype(BF16)
            for s in range(slots):
                even[s][:, low:high] = whole[s * group : (s + 1) * group]
            for i in range(half_slots):
                rows = slice(full + i * group, full + (i + 1) * group)
                lead[i][:, low:high] = bottom[rows]
                trail[i][:, low:high] = top[rows]


def join_kernel(half_slots, group, *refs):
    lead = refs[:half_slots]
    trail = refs[half_slots : 2 * half_slots]
    inner, outer = refs[2 * half_slots : 2 * half_slots + 2]
    last = refs[2 * half_slots + 2 : 3 * half_slots + 2]
    outs = refs[3 * half_slots + 2 :]
    me = lax.axis_index("blk")
    odd = lax.rem(me, 2) == 1
    for i in range(half_slots):
        above = (i + half_slots - 1) % half_slots
        rows = slice(above * group, (above + 1) * group)
        from_above = jnp.where(odd, inner[rows, :], outer[rows, :])
        outs[i][...] = (lead[i][...] + from_above).astype(BF16)
        rows = slice(i * group, (i + 1) * group)
        from_below = jnp.where(odd, outer[rows, :], inner[rows, :])
        joined = (trail[i][...] + from_below).astype(BF16)
        if i == 0:
            outs[half_slots][...] = jnp.where(me == 0, last[0][...], joined)
        else:
            outs[half_slots + i][...] = joined
            outs[2 * half_slots + i - 1][...] = last[i][...]


def gather_pieces(refs, slots, me):
    half_slots = slots // 2
    found = [ref[...] for ref in refs[: slots + half_slots + 1]]
    for i in range(1, half_slots):
        below = refs[slots + half_slots + i][...]
        last = refs[2 * slots + i - 1][...]
        found.append(jnp.where(me == i, last, below))
    return found


def gram_kernel(slots, group, var_count, points, weights, classes, *refs):
    packed = refs[-1]
    blocks = 2 * slots
    me = lax.axis_index("blk")
    picked = jnp.zeros(classes.shape, F32)
    for k in range(weights.shape[0]):
        picked = picked + jnp.where(classes[...] == k, weights[k], jnp.float32(0.0))
    wide = jnp.concatenate([picked] * var_count, axis=1)
    left = jnp.concatenate(gather_pieces(refs[:-1], slots, me), axis=0)
    right = (left.astype(F32) * wide).astype(BF16)
    gram = lax.dot_general(
        left, right, (((1,), (1,)), ((), ())), preferred_element_type=F32
    )
    size = blocks * group
    freqs = group // 2
    same = iota((size, size), 0) % freqs == iota((size, size), 1) % freqs
    gram = jnp.where(same, gram, 0.0).reshape(blocks, 2, freqs, size)
    rows_re = gram[:, 0].reshape(blocks * freqs, size)
    rows_im = gram[:, 1].reshape(blocks * freqs, size)
    width = 2 * blocks * blocks
    row, lane = (iota((size, width), 0), iota((size, width), 1))
    fits = block_of(row // group, me, slots) == lane % blocks
    row_part = row // freqs % 2
    lane_part = lane // blocks % 2
    from_re = one_hot(fits & (row_part == lane_part))
    sign = jnp.where(lane_part == 0, 1.0, -1.0)
    from_im = jnp.where(fits & (row_part != lane_part), sign, 0.0).astype(BF16)
    total = jnp.zeros((blocks * freqs, width), F32)
    for part_re, part_im in zip(split3(rows_re), split3(rows_im)):
        total = total + (mm(part_re, from_re) + mm(part_im, from_im))
    mine = iota((freqs, width), 1) // (2 * blocks)
    out = jnp.zeros((freqs, width), F32)
    for b in range(blocks):
        block = block_of(jnp.int32(b), me, slots)
        out = out + jnp.where(mine == block, total[b * freqs : (b + 1) * freqs], 0.0)
    packed[...] = out


def mode_kernel(slots, var_count, points, scaling, feature_count, a_ref, b_ref, *refs):
    csd, eig, modes = refs[-3:]
    blocks = 2 * slots
    me = lax.axis_index("blk")
    spectra = gather_pieces(refs[:-3], slots, me)
    raw = a_ref[...] + b_ref[...]
    freqs, width = raw.shape
    group = 2 * freqs
    size = blocks * group
    mat = scaling * raw
    lane_part = iota((freqs, width), 1) // blocks % 2
    is_re = lane_part == 0
    gather = one_hot(
        iota((width, width), 0) // (2 * blocks) == iota((width, width), 1) % blocks
    )

    def apply(matrix, vec_re, vec_im):
        top = matrix * jnp.where(is_re, vec_re, -vec_im)
        bottom = matrix * jnp.where(is_re, vec_im, vec_re)
        both = jnp.concatenate([top, bottom], axis=0)
        parts = jnp.concatenate([p.astype(F32) for p in split3(both)], axis=0).astype(BF16)
        got = mm(parts, gather)
        got = got[: 2 * freqs] + got[2 * freqs : 4 * freqs] + got[4 * freqs :]
        return (got[:freqs], got[freqs:])

    def over_blocks(x):
        return jnp.sum(x, axis=1, keepdims=True) * jnp.float32(1.0 / (2 * blocks))

    vec_re = jnp.full((freqs, width), 1.0 / math.sqrt(blocks), F32)
    vec_im = jnp.zeros((freqs, width), F32)
    for _ in range(ITERS):
        out_re, out_im = apply(mat, vec_re, vec_im)
        length = jnp.sqrt(over_blocks(out_re * out_re + out_im * out_im))
        vec_re, vec_im = (out_re / length, out_im / length)
    out_re, out_im = apply(mat, vec_re, vec_im)
    value = over_blocks(vec_re * out_re + vec_im * out_im)
    diagonal = iota((freqs, freqs), 0) == iota((freqs, freqs), 1)
    eig[...] = jnp.sum(
        jnp.where(diagonal, jnp.broadcast_to(value, (freqs, freqs)), 0.0), axis=0, keepdims=True
    )
    low_re = vec_re.astype(BF16)
    low_im = vec_im.astype(BF16)
    out_re, out_im = apply(raw, low_re.astype(F32), low_im.astype(F32))
    normsq = over_blocks(low_re.astype(F32) * out_re + low_im.astype(F32) * out_im)
    scale = jnp.sqrt(jnp.float32(feature_count) / normsq)
    row, lane = (iota((width, size), 0), iota((width, size), 1))
    expand = one_hot(row == block_of(lane // group, me, slots))
    wide = mm(jnp.concatenate([vec_re, vec_im], axis=0).astype(BF16), expand)
    wide_re, wide_im = (wide[:freqs], wide[freqs:])
    part = iota((freqs, size), 1) // freqs % 2
    mine = iota((freqs, size), 1) % freqs == iota((freqs, size), 0)
    coef_re = jnp.where(mine, jnp.where(part == 0, wide_re, -wide_im), 0.0)
    coef_im = jnp.where(mine, jnp.where(part == 0, wide_im, wide_re), 0.0)
    rows = 2 * var_count
    upper = iota((rows, size), 0) < var_count
    var = iota((rows, size), 0) % var_count
    tall = []
    for f in range(freqs):
        both = jnp.where(
            upper,
            jnp.broadcast_to(coef_re[f : f + 1], (rows, size)),
            jnp.broadcast_to(coef_im[f : f + 1], (rows, size)),
        )
        tall.append(
            jnp.concatenate([jnp.where(var == v, both, 0.0) for v in range(var_count)], axis=1)
        )
    coef = jnp.concatenate(tall, axis=0).astype(BF16)
    stacked = jnp.concatenate(
        [
            piece[:, v * points : (v + 1) * points]
            for v in range(var_count)
            for piece in spectra
        ],
        axis=0,
    )
    phi = mm(coef, stacked)
    for f in range(freqs):
        block = phi[f * rows : (f + 1) * rows] * scale[f : f + 1, :]
        for k in range(2):
            modes[f, k] = block[k * var_count : (k + 1) * var_count]
    tiles = jnp.concatenate(
        [
            jnp.where(
                iota((blocks, width), 1) // (2 * blocks) == iota((blocks, width), 0),
                jnp.broadcast_to(mat[f : f + 1], (blocks, width)),
                0.0,
            )
            for f in range(freqs)
        ],
        axis=0,
    )
    for k in range(2):
        row, lane = (iota((width, blocks), 0), iota((width, blocks), 1))
        fold = one_hot(row % (2 * blocks) == lane + k * blocks)
        got = jnp.zeros((freqs * blocks, blocks), F32)
        for piece in split3(tiles):
            got = got + mm(piece, fold)
        for f in range(freqs):
            csd[f, k] = got[f * blocks : (f + 1) * blocks]


def call(kernel, outs, ins, inputs, scratch, flops, moved):
    vmem = pl.BlockSpec(memory_space=pltpu.VMEM)
    return pl.pallas_call(
        kernel,
        out_shape=outs,
        in_specs=ins,
        out_specs=jax.tree.map(lambda _: vmem, outs),
        scratch_shapes=scratch,
        compiler_params=pltpu.CompilerParams(vmem_limit_bytes=VMEM_LIMIT),
        cost_estimate=pl.CostEstimate(flops=flops, bytes_accessed=moved, transcendentals=0),
    )(*inputs)


def on_device(snapshots, freq_index, weight_class, class_weight):
    row_count, var_count, points = snapshots.shape
    features = var_count * points
    slots = lax.axis_size("blk")
    half_slots = slots // 2
    me = lax.axis_index("blk")
    freqs = freq_index.shape[0] // slots
    group = 2 * freqs
    blocks = 2 * slots
    vmem = pl.BlockSpec(memory_space=pltpu.VMEM)
    smem = pl.BlockSpec(memory_space=pltpu.SMEM)
    hbm = pl.BlockSpec(memory_space=pltpu.HBM)
    shape = jax.ShapeDtypeStruct

    wide = half_slots * group
    groups = points // LANES
    inner, outer, lhs, held = call(
        functools.partial(halo_kernel, slots, group, var_count, points),
        [
            shape((wide, features), F32),
            shape((wide, features), F32),
            shape((2 * slots * group * var_count, HALF * var_count), BF16),
            shape((groups, row_count, var_count, LANES), BF16),
        ],
        [smem, hbm],
        (freq_index, pltpu.with_memory_space_constraint(snapshots, pltpu.HBM)),
        [pltpu.SemaphoreType.DMA((groups,))],
        2 * 2 * wide * HALF * features * var_count,
        2 * row_count * features,
    )

    def swap(x, first):
        pairs = [(i, i + 1) for i in range(first, slots - 1, 2)]
        return lax.ppermute(x, "blk", pairs + [(b, a) for a, b in pairs])

    from_outer = swap(outer, 0)
    swapped = (swap(inner, 1), from_outer)
    keep = [0] + list(range(half_slots + 1, slots))
    piece = shape((group, features), BF16)
    wide_piece = shape((group, features), F32)
    pieces = call(
        functools.partial(block_kernel, slots, keep, var_count, points),
        [piece] * slots + [wide_piece] * (2 * half_slots),
        [vmem, vmem],
        (lhs, held),
        [],
        2 * 3 * slots * group * HALF * features * var_count,
        2 * row_count * features,
    )

    def shift(x, s, first):
        return lax.ppermute(x, "blk", [(i, (i + s) % slots) for i in range(first, slots)])

    even = [pieces[0]] + [shift(pieces[s], s, 0) for s in range(1, slots)]
    last = [
        lax.ppermute(
            inner[i * group : (i + 1) * group].astype(BF16), "blk", [(slots - 1, i)]
        )
        for i in range(half_slots)
    ]
    odd = call(
        functools.partial(join_kernel, half_slots, group),
        [piece] * (slots + half_slots - 1),
        [vmem] * (slots + 2 + half_slots),
        (*pieces[slots:], *swapped, *last),
        [],
        slots * group * features,
        10 * slots * group * features,
    )

    above = [odd[0]] + [shift(odd[i], s, 0) for i, s in enumerate(keep) if i]
    under = [odd[half_slots]] + [shift(odd[half_slots + i], i, 1) for i in range(1, half_slots)]
    width = 2 * blocks * blocks
    spectra = (*even, *above, *under, *odd[slots:])
    packed = call(
        functools.partial(gram_kernel, slots, group, var_count, points),
        shape((freqs, width), F32),
        [smem, vmem] + [vmem] * len(spectra),
        (class_weight, weight_class.reshape(1, points), *spectra),
        [],
        2 * (blocks * group) ** 2 * features,
        4 * blocks * group * features,
    )
    devices = lax.axis_size("pts")
    step = 1
    other = None
    while step < devices:
        if other is not None:
            packed = packed + other
        other = lax.ppermute(packed, "pts", [(i, i ^ step) for i in range(devices)])
        step *= 2
    total_features = features * devices
    csd, eigval, modes = call(
        functools.partial(
            mode_kernel,
            slots,
            var_count,
            points,
            1.0 / (total_features * (3.0 * NFFT / 8.0)),
            total_features,
        ),
        [
            shape((freqs, 2, blocks, blocks), F32),
            shape((1, freqs), F32),
            shape((freqs, 2, var_count, points), F32),
        ],
        [vmem] * (2 + len(spectra)),
        (packed, other, *spectra),
        [],
        2 * 2 * blocks * group * group * features,
        2 * blocks * group * features,
    )
    return (csd, eigval.reshape(freqs), modes)


def solution(mesh):
    in_specs = (P("blk", None, "pts"), P(), P("pts"), P())
    out_specs = (P("blk", None, None, None), P("blk"), P("blk", None, None, "pts"))
    return jax.shard_map(
        on_device, mesh=mesh, in_specs=in_specs, out_specs=out_specs, check_vma=False
    )
```

```python
import functools
import math

import jax
import jax.numpy as jnp
from jax import lax
from jax.experimental import pallas as pl
from jax.experimental.pallas import tpu as pltpu
from jax.sharding import PartitionSpec as P

NFFT = 768
HALF = NFFT // 2
ITERS = 3
LANES = 128
VMEM_LIMIT = 32 * 1024 * 1024
F32 = jnp.float32
BF16 = jnp.bfloat16


def iota(shape, axis):
    return lax.broadcasted_iota(jnp.int32, shape, axis)


def mm(a, b):
    return jnp.dot(a, b, preferred_element_type=F32)


def split3(x):
    high = x.astype(BF16)
    rest = x - high.astype(F32)
    mid = rest.astype(BF16)
    low = (rest - mid.astype(F32)).astype(BF16)
    return (high, mid, low)


def one_hot(condition):
    return jnp.where(condition, 1.0, 0.0).astype(BF16)


def modulo(x, n):
    return jnp.where(x < 0, x + n, x)


def block_of(slot, me, slots):
    half_slots = slots // 2
    above = slot - slots
    below = above - half_slots
    even = 2 * modulo(me - slot, slots)
    upper = 2 * modulo(me - jnp.where(above == 0, 0, above + half_slots), slots) + 1
    lower = modulo(2 * modulo(me - below, slots) - 1, 2 * slots)
    return jnp.where(slot < slots, even, jnp.where(below < 0, upper, lower))


def trig(phase):
    quarter = ((phase + NFFT // 8) * 1366) >> 18
    angle = (2.0 * math.pi / NFFT) * (phase - (NFFT // 4) * quarter).astype(F32)
    x = angle * angle
    cos = 1.0 + x * (-1.0 / 2 + x * (1.0 / 24 + x * (-1.0 / 720 + x * (1.0 / 40320))))
    sin = 1.0 + x * (-1.0 / 6 + x * (1.0 / 120 + x * (-1.0 / 5040 + x * (1.0 / 362880))))
    sin = angle * sin
    odd = (quarter & 1) != 0
    real_part = jnp.where(odd, sin, cos)
    imag_part = jnp.where(odd, cos, sin)
    real_part = jnp.where(((quarter + 1) & 2) != 0, -real_part, real_part)
    imag_part = jnp.where((quarter & 2) != 0, -imag_part, imag_part)
    return (real_part, imag_part)


def transform_rows(freqs, me, slots, group, start):
    count = group // 2
    times = start + iota((count, HALF), 1)
    window = 0.5 - 0.5 * trig(times)[0]
    row = iota((count, HALF), 0)
    out = []
    for s in range(slots):
        owner = lax.rem(me + s, slots)
        freq = jnp.zeros((count, HALF), jnp.int32)
        for f in range(count):
            freq = jnp.where(row == f, freqs[owner * count + f], freq)
        product = freq * times
        turns = ((product >> 8) * 21846) >> 16
        real_part, imag_part = trig(product - NFFT * turns)
        out.append(window * real_part)
        out.append(-window * imag_part)
    return jnp.concatenate(out, axis=0).astype(BF16)


def spread(rows, var_count):
    width = HALF * var_count
    pick = one_hot(iota((HALF, width), 1) // var_count == iota((HALF, width), 0))
    wide = mm(rows, pick)
    owner = iota(wide.shape, 1) % var_count
    return [jnp.where(owner == v, wide, 0.0).astype(BF16) for v in range(var_count)]


def columns(held, j, half, var_count):
    rows = HALF * var_count
    parts = [
        held.at[j + i].reshape(2 * rows, LANES)[half * rows : (half + 1) * rows, :]
        for i in range(2)
    ]
    return jnp.concatenate(parts, axis=1)


def halo_kernel(slots, group, var_count, points, freqs, x_hbm, inner, outer, lhs, held, *refs):
    last, sems = (refs[:-1], refs[-1])
    copies = []
    for j in range(held.shape[0]):
        for i in range(2):
            rows = pl.ds(i * HALF, HALF)
            copy = pltpu.make_async_copy(
                x_hbm.at[rows, :, pl.ds(j * LANES, LANES)], held.at[j, rows], sems.at[j, i]
            )
            copy.start()
            copies.append(copy)
    me = lax.axis_index("blk")
    odd = lax.rem(me, 2) == 1
    full = slots * group
    wide = full // 2
    rows = [transform_rows(freqs, me, slots, group, start) for start in (0, HALF)]
    for v, part in enumerate(spread(jnp.concatenate(rows, axis=0), var_count)):
        lhs[2 * v * full : 2 * (v + 1) * full, :] = part

    def some(low):
        return jnp.concatenate(
            [lhs[2 * v * full + low : 2 * v * full + low + wide, :] for v in range(var_count)],
            axis=0,
        )

    for j in range(0, held.shape[0], 2):
        for copy in copies[2 * j : 2 * j + 4]:
            copy.wait()
        down = mm(some(full + wide), columns(held, j, 0, var_count))
        up = mm(some(group), columns(held, j, 1, var_count))
        for v in range(var_count):
            low = v * points + j * LANES
            lower = down[v * wide : (v + 1) * wide]
            upper = up[v * wide : (v + 1) * wide]
            inner[:, low : low + 2 * LANES] = jnp.where(odd, upper, lower)
            outer[:, low : low + 2 * LANES] = jnp.where(odd, lower, upper)
            for i, target in enumerate(last):
                target[:, low : low + 2 * LANES] = upper[i * group : (i + 1) * group].astype(BF16)


def block_kernel(slots, keep, var_count, points, lhs, held, *outs):
    half_slots = slots // 2
    even = outs[:slots]
    lead = outs[slots : slots + half_slots]
    trail = outs[slots + half_slots :]
    group = even[0].shape[0]
    full = slots * group
    short = full + half_slots * group

    def some(v, low, high):
        return lhs[2 * v * full + low : 2 * v * full + high, :]

    for j in range(0, held.shape[0], 2):
        parts = [some(v, 0, short) for v in range(var_count)]
        first = mm(jnp.concatenate(parts, axis=0), columns(held, j, 0, var_count))
        parts = []
        for v in range(var_count):
            parts.append(some(v, full, 2 * full))
            parts.extend(some(v, s * group, (s + 1) * group) for s in keep)
        second = mm(jnp.concatenate(parts, axis=0), columns(held, j, 1, var_count))
        for v in range(var_count):
            low = v * points + j * LANES
            high = low + 2 * LANES
            top = first[v * short : (v + 1) * short]
            bottom = second[v * short : (v + 1) * short]
            whole = (top[:full] + bottom[:full]).astype(BF16)
            for s in range(slots):
                even[s][:, low:high] = whole[s * group : (s + 1) * group]
            for i in range(half_slots):
                rows = slice(full + i * group, full + (i + 1) * group)
                lead[i][:, low:high] = bottom[rows]
                trail[i][:, low:high] = top[rows]


def join_kernel(half_slots, group, *refs):
    lead = refs[:half_slots]
    trail = refs[half_slots : 2 * half_slots]
    inner, outer = refs[2 * half_slots : 2 * half_slots + 2]
    last = refs[2 * half_slots + 2 : 3 * half_slots + 2]
    outs = refs[3 * half_slots + 2 :]
    me = lax.axis_index("blk")
    odd = lax.rem(me, 2) == 1
    for i in range(half_slots):
        above = (i + half_slots - 1) % half_slots
        rows = slice(above * group, (above + 1) * group)
        from_above = jnp.where(odd, inner[rows, :], outer[rows, :])
        outs[i][...] = (lead[i][...] + from_above).astype(BF16)
        rows = slice(i * group, (i + 1) * group)
        from_below = jnp.where(odd, outer[rows, :], inner[rows, :])
        joined = (trail[i][...] + from_below).astype(BF16)
        if i == 0:
            outs[half_slots][...] = jnp.where(me == 0, last[0][...], joined)
        else:
            outs[half_slots + i][...] = joined
            outs[2 * half_slots + i - 1][...] = last[i][...]


def gather_pieces(refs, slots, me):
    half_slots = slots // 2
    found = [ref[...] for ref in refs[: slots + half_slots + 1]]
    for i in range(1, half_slots):
        below = refs[slots + half_slots + i][...]
        last = refs[2 * slots + i - 1][...]
        found.append(jnp.where(me == i, last, below))
    return found


def gram_kernel(slots, group, var_count, points, weights, classes, *refs):
    packed = refs[-1]
    blocks = 2 * slots
    me = lax.axis_index("blk")
    picked = jnp.zeros(classes.shape, F32)
    for k in range(weights.shape[0]):
        picked = picked + jnp.where(classes[...] == k, weights[k], jnp.float32(0.0))
    wide = jnp.concatenate([picked] * var_count, axis=1)
    left = jnp.concatenate(gather_pieces(refs[:-1], slots, me), axis=0)
    right = (left.astype(F32) * wide).astype(BF16)
    gram = lax.dot_general(
        left, right, (((1,), (1,)), ((), ())), preferred_element_type=F32
    )
    size = blocks * group
    freqs = group // 2
    same = iota((size, size), 0) % freqs == iota((size, size), 1) % freqs
    gram = jnp.where(same, gram, 0.0).reshape(blocks, 2, freqs, size)
    rows_re = gram[:, 0].reshape(blocks * freqs, size)
    rows_im = gram[:, 1].reshape(blocks * freqs, size)
    width = 2 * blocks * blocks
    row, lane = (iota((size, width), 0), iota((size, width), 1))
    fits = block_of(row // group, me, slots) == lane % blocks
    row_part = row // freqs % 2
    lane_part = lane // blocks % 2
    from_re = one_hot(fits & (row_part == lane_part))
    sign = jnp.where(lane_part == 0, 1.0, -1.0)
    from_im = jnp.where(fits & (row_part != lane_part), sign, 0.0).astype(BF16)
    total = jnp.zeros((blocks * freqs, width), F32)
    for part_re, part_im in zip(split3(rows_re), split3(rows_im)):
        total = total + (mm(part_re, from_re) + mm(part_im, from_im))
    mine = iota((freqs, width), 1) // (2 * blocks)
    out = jnp.zeros((freqs, width), F32)
    for b in range(blocks):
        block = block_of(jnp.int32(b), me, slots)
        out = out + jnp.where(mine == block, total[b * freqs : (b + 1) * freqs], 0.0)
    packed[...] = out


def mode_kernel(slots, var_count, points, scaling, feature_count, sums, *refs):
    csd, eig, modes = refs[-3:]
    blocks = 2 * slots
    me = lax.axis_index("blk")
    spectra = gather_pieces(refs[:-3], slots, me)
    raw = sums[0]
    for i in range(1, sums.shape[0]):
        raw = raw + sums[i]
    freqs, width = raw.shape
    group = 2 * freqs
    size = blocks * group
    mat = scaling * raw
    lane_part = iota((freqs, width), 1) // blocks % 2
    is_re = lane_part == 0
    gather = one_hot(
        iota((width, width), 0) // (2 * blocks) == iota((width, width), 1) % blocks
    )

    def apply(matrix, vec_re, vec_im):
        top = matrix * jnp.where(is_re, vec_re, -vec_im)
        bottom = matrix * jnp.where(is_re, vec_im, vec_re)
        both = jnp.concatenate([top, bottom], axis=0)
        parts = jnp.concatenate([p.astype(F32) for p in split3(both)], axis=0).astype(BF16)
        got = mm(parts, gather)
        got = got[: 2 * freqs] + got[2 * freqs : 4 * freqs] + got[4 * freqs :]
        return (got[:freqs], got[freqs:])

    def over_blocks(x):
        return jnp.sum(x, axis=1, keepdims=True) * jnp.float32(1.0 / (2 * blocks))

    vec_re = jnp.full((freqs, width), 1.0 / math.sqrt(blocks), F32)
    vec_im = jnp.zeros((freqs, width), F32)
    for _ in range(ITERS):
        out_re, out_im = apply(mat, vec_re, vec_im)
        length = jnp.sqrt(over_blocks(out_re * out_re + out_im * out_im))
        vec_re, vec_im = (out_re / length, out_im / length)
    out_re, out_im = apply(mat, vec_re, vec_im)
    value = over_blocks(vec_re * out_re + vec_im * out_im)
    diagonal = iota((freqs, freqs), 0) == iota((freqs, freqs), 1)
    eig[...] = jnp.sum(
        jnp.where(diagonal, jnp.broadcast_to(value, (freqs, freqs)), 0.0), axis=0, keepdims=True
    )
    low_re = vec_re.astype(BF16)
    low_im = vec_im.astype(BF16)
    out_re, out_im = apply(raw, low_re.astype(F32), low_im.astype(F32))
    normsq = over_blocks(low_re.astype(F32) * out_re + low_im.astype(F32) * out_im)
    scale = jnp.sqrt(jnp.float32(feature_count) / normsq)
    row, lane = (iota((width, size), 0), iota((width, size), 1))
    expand = one_hot(row == block_of(lane // group, me, slots))
    wide = mm(jnp.concatenate([vec_re, vec_im], axis=0).astype(BF16), expand)
    wide_re, wide_im = (wide[:freqs], wide[freqs:])
    part = iota((freqs, size), 1) // freqs % 2
    mine = iota((freqs, size), 1) % freqs == iota((freqs, size), 0)
    coef_re = jnp.where(mine, jnp.where(part == 0, wide_re, -wide_im), 0.0)
    coef_im = jnp.where(mine, jnp.where(part == 0, wide_im, wide_re), 0.0)
    rows = 2 * var_count
    upper = iota((rows, size), 0) < var_count
    var = iota((rows, size), 0) % var_count
    tall = []
    for f in range(freqs):
        both = jnp.where(
            upper,
            jnp.broadcast_to(coef_re[f : f + 1], (rows, size)),
            jnp.broadcast_to(coef_im[f : f + 1], (rows, size)),
        )
        tall.append(
            jnp.concatenate([jnp.where(var == v, both, 0.0) for v in range(var_count)], axis=1)
        )
    coef = jnp.concatenate(tall, axis=0).astype(BF16)
    stacked = jnp.concatenate(
        [
            piece[:, v * points : (v + 1) * points]
            for v in range(var_count)
            for piece in spectra
        ],
        axis=0,
    )
    phi = mm(coef, stacked)
    for f in range(freqs):
        block = phi[f * rows : (f + 1) * rows] * scale[f : f + 1, :]
        for k in range(2):
            modes[f, k] = block[k * var_count : (k + 1) * var_count]
    tiles = jnp.concatenate(
        [
            jnp.where(
                iota((blocks, width), 1) // (2 * blocks) == iota((blocks, width), 0),
                jnp.broadcast_to(mat[f : f + 1], (blocks, width)),
                0.0,
            )
            for f in range(freqs)
        ],
        axis=0,
    )
    for k in range(2):
        row, lane = (iota((width, blocks), 0), iota((width, blocks), 1))
        fold = one_hot(row % (2 * blocks) == lane + k * blocks)
        got = jnp.zeros((freqs * blocks, blocks), F32)
        for piece in split3(tiles):
            got = got + mm(piece, fold)
        for f in range(freqs):
            csd[f, k] = got[f * blocks : (f + 1) * blocks]


def call(kernel, outs, ins, inputs, scratch, flops, moved):
    vmem = pl.BlockSpec(memory_space=pltpu.VMEM)
    return pl.pallas_call(
        kernel,
        out_shape=outs,
        in_specs=ins,
        out_specs=jax.tree.map(lambda _: vmem, outs),
        scratch_shapes=scratch,
        compiler_params=pltpu.CompilerParams(vmem_limit_bytes=VMEM_LIMIT),
        cost_estimate=pl.CostEstimate(flops=flops, bytes_accessed=moved, transcendentals=0),
    )(*inputs)


def on_device(snapshots, freq_index, weight_class, class_weight):
    row_count, var_count, points = snapshots.shape
    features = var_count * points
    slots = lax.axis_size("blk")
    half_slots = slots // 2
    me = lax.axis_index("blk")
    freqs = freq_index.shape[0] // slots
    group = 2 * freqs
    blocks = 2 * slots
    vmem = pl.BlockSpec(memory_space=pltpu.VMEM)
    smem = pl.BlockSpec(memory_space=pltpu.SMEM)
    hbm = pl.BlockSpec(memory_space=pltpu.HBM)
    shape = jax.ShapeDtypeStruct

    wide = half_slots * group
    groups = points // LANES
    inner, outer, lhs, held, *last = call(
        functools.partial(halo_kernel, slots, group, var_count, points),
        [
            shape((wide, features), F32),
            shape((wide, features), F32),
            shape((2 * slots * group * var_count, HALF * var_count), BF16),
            shape((groups, row_count, var_count, LANES), BF16),
        ]
        + [shape((group, features), BF16)] * half_slots,
        [smem, hbm],
        (freq_index, pltpu.with_memory_space_constraint(snapshots, pltpu.HBM)),
        [pltpu.SemaphoreType.DMA((groups, 2))],
        2 * 2 * wide * HALF * features * var_count,
        2 * row_count * features,
    )

    def swap(x, first):
        pairs = [(i, i + 1) for i in range(first, slots - 1, 2)]
        return lax.ppermute(x, "blk", pairs + [(b, a) for a, b in pairs])

    from_outer = swap(outer, 0)
    swapped = (swap(inner, 1), from_outer)
    keep = [0] + list(range(half_slots + 1, slots))
    piece = shape((group, features), BF16)
    wide_piece = shape((group, features), F32)
    pieces = call(
        functools.partial(block_kernel, slots, keep, var_count, points),
        [piece] * slots + [wide_piece] * (2 * half_slots),
        [vmem, vmem],
        (lhs, held),
        [],
        2 * 3 * slots * group * HALF * features * var_count,
        2 * row_count * features,
    )

    def shift(x, s, first):
        return lax.ppermute(x, "blk", [(i, (i + s) % slots) for i in range(first, slots)])

    even = [pieces[0]] + [shift(pieces[s], s, 0) for s in range(1, slots)]
    last = [lax.ppermute(x, "blk", [(slots - 1, i)]) for i, x in enumerate(last)]
    odd = call(
        functools.partial(join_kernel, half_slots, group),
        [piece] * (slots + half_slots - 1),
        [vmem] * (slots + 2 + half_slots),
        (*pieces[slots:], *swapped, *last),
        [],
        slots * group * features,
        10 * slots * group * features,
    )

    above = [odd[0]] + [shift(odd[i], s, 0) for i, s in enumerate(keep) if i]
    under = [odd[half_slots]] + [shift(odd[half_slots + i], i, 1) for i in range(1, half_slots)]
    width = 2 * blocks * blocks
    spectra = (*even, *above, *under, *odd[slots:])
    packed = call(
        functools.partial(gram_kernel, slots, group, var_count, points),
        shape((freqs, width), F32),
        [smem, vmem] + [vmem] * len(spectra),
        (class_weight, weight_class.reshape(1, points), *spectra),
        [],
        2 * (blocks * group) ** 2 * features,
        4 * blocks * group * features,
    )
    devices = lax.axis_size("pts")
    packed = lax.all_gather(packed, "pts")
    total_features = features * devices
    csd, eigval, modes = call(
        functools.partial(
            mode_kernel,
            slots,
            var_count,
            points,
            1.0 / (total_features * (3.0 * NFFT / 8.0)),
            total_features,
        ),
        [
            shape((freqs, 2, blocks, blocks), F32),
            shape((1, freqs), F32),
            shape((freqs, 2, var_count, points), F32),
        ],
        [vmem] * (1 + len(spectra)),
        (packed, *spectra),
        [],
        2 * 2 * blocks * group * group * features,
        2 * blocks * group * features,
    )
    return (csd, eigval.reshape(freqs), modes)


def solution(mesh):
    in_specs = (P("blk", None, "pts"), P(), P("pts"), P())
    out_specs = (P("blk", None, None, None), P("blk"), P("blk", None, None, "pts"))
    return jax.shard_map(
        on_device, mesh=mesh, in_specs=in_specs, out_specs=out_specs, check_vma=False
    )
```

```python
import functools
import math

import jax
import jax.numpy as jnp
from jax import lax
from jax.experimental import pallas as pl
from jax.experimental.pallas import tpu as pltpu
from jax.sharding import PartitionSpec as P

NFFT = 768
HALF = NFFT // 2
ITERS = 3
LANES = 128
VMEM_LIMIT = 32 * 1024 * 1024
F32 = jnp.float32
BF16 = jnp.bfloat16


def iota(shape, axis):
    return lax.broadcasted_iota(jnp.int32, shape, axis)


def mm(a, b):
    return jnp.dot(a, b, preferred_element_type=F32)


def split3(x):
    high = x.astype(BF16)
    rest = x - high.astype(F32)
    mid = rest.astype(BF16)
    low = (rest - mid.astype(F32)).astype(BF16)
    return (high, mid, low)


def one_hot(condition):
    return jnp.where(condition, 1.0, 0.0).astype(BF16)


def modulo(x, n):
    return jnp.where(x < 0, x + n, x)


def block_of(slot, me, slots):
    half_slots = slots // 2
    above = slot - slots
    below = above - half_slots
    even = 2 * modulo(me - slot, slots)
    upper = 2 * modulo(me - jnp.where(above == 0, 0, above + half_slots), slots) + 1
    lower = modulo(2 * modulo(me - below, slots) - 1, 2 * slots)
    return jnp.where(slot < slots, even, jnp.where(below < 0, upper, lower))


def trig(phase):
    quarter = ((phase + NFFT // 8) * 1366) >> 18
    angle = (2.0 * math.pi / NFFT) * (phase - (NFFT // 4) * quarter).astype(F32)
    x = angle * angle
    cos = 1.0 + x * (-1.0 / 2 + x * (1.0 / 24 + x * (-1.0 / 720 + x * (1.0 / 40320))))
    sin = 1.0 + x * (-1.0 / 6 + x * (1.0 / 120 + x * (-1.0 / 5040 + x * (1.0 / 362880))))
    sin = angle * sin
    odd = (quarter & 1) != 0
    real_part = jnp.where(odd, sin, cos)
    imag_part = jnp.where(odd, cos, sin)
    real_part = jnp.where(((quarter + 1) & 2) != 0, -real_part, real_part)
    imag_part = jnp.where((quarter & 2) != 0, -imag_part, imag_part)
    return (real_part, imag_part)


def transform_rows(freqs, me, slots, group, start):
    count = group // 2
    times = start + iota((count, HALF), 1)
    window = 0.5 - 0.5 * trig(times)[0]
    row = iota((count, HALF), 0)
    out = []
    for s in range(slots):
        owner = lax.rem(me + s, slots)
        freq = jnp.zeros((count, HALF), jnp.int32)
        for f in range(count):
            freq = jnp.where(row == f, freqs[owner * count + f], freq)
        product = freq * times
        turns = ((product >> 8) * 21846) >> 16
        real_part, imag_part = trig(product - NFFT * turns)
        out.append(window * real_part)
        out.append(-window * imag_part)
    return jnp.concatenate(out, axis=0).astype(BF16)


def spread(rows, var_count):
    width = HALF * var_count
    pick = one_hot(iota((HALF, width), 1) // var_count == iota((HALF, width), 0))
    wide = mm(rows, pick)
    owner = iota(wide.shape, 1) % var_count
    return [jnp.where(owner == v, wide, 0.0).astype(BF16) for v in range(var_count)]


def columns(held, j, half, var_count):
    rows = HALF * var_count
    parts = [
        held.at[j + i].reshape(2 * rows, LANES)[half * rows : (half + 1) * rows, :]
        for i in range(2)
    ]
    return jnp.concatenate(parts, axis=1)


def encode(values, coded):
    rows, features = values.shape
    largest = jnp.max(jnp.abs(values[...]), axis=1, keepdims=True)
    largest = jnp.maximum(largest, 1e-30)
    exponent = jnp.floor(jnp.log2(32000.0 / largest))
    steps = values[...] * jnp.exp2(exponent)
    coded[:, :features] = jnp.round(steps).astype(jnp.int32).astype(jnp.int16)
    tail = jnp.broadcast_to(exponent, (rows, LANES))
    coded[:, features:] = tail.astype(jnp.int32).astype(jnp.int16)


def decode(coded, low, high):
    features = coded.shape[1] - LANES
    exponent = coded[low:high, features:].astype(jnp.int32).astype(F32)[:, :1]
    steps = coded[low:high, :features].astype(jnp.int32).astype(F32)
    return steps * (1.0 / jnp.exp2(exponent))


def halo_kernel(slots, group, var_count, points, freqs, x_hbm, inner, outer, lhs, held, *refs):
    first, second, sems = refs
    copies = []
    for j in range(held.shape[0]):
        for i in range(2):
            rows = pl.ds(i * HALF, HALF)
            copy = pltpu.make_async_copy(
                x_hbm.at[rows, :, pl.ds(j * LANES, LANES)], held.at[j, rows], sems.at[j, i]
            )
            copy.start()
            copies.append(copy)
    me = lax.axis_index("blk")
    odd = lax.rem(me, 2) == 1
    full = slots * group
    wide = full // 2
    rows = [transform_rows(freqs, me, slots, group, start) for start in (0, HALF)]
    for v, part in enumerate(spread(jnp.concatenate(rows, axis=0), var_count)):
        lhs[2 * v * full : 2 * (v + 1) * full, :] = part

    def some(low):
        return jnp.concatenate(
            [lhs[2 * v * full + low : 2 * v * full + low + wide, :] for v in range(var_count)],
            axis=0,
        )

    for j in range(0, held.shape[0], 2):
        for copy in copies[2 * j : 2 * j + 4]:
            copy.wait()
        down = mm(some(full + wide), columns(held, j, 0, var_count))
        up = mm(some(group), columns(held, j, 1, var_count))
        for v in range(var_count):
            low = v * points + j * LANES
            lower = down[v * wide : (v + 1) * wide]
            upper = up[v * wide : (v + 1) * wide]
            first[:, low : low + 2 * LANES] = jnp.where(odd, upper, lower)
            second[:, low : low + 2 * LANES] = jnp.where(odd, lower, upper)
    encode(first, inner)
    encode(second, outer)


def block_kernel(slots, keep, var_count, points, lhs, held, *outs):
    half_slots = slots // 2
    even = outs[:slots]
    lead = outs[slots : slots + half_slots]
    trail = outs[slots + half_slots :]
    group = even[0].shape[0]
    full = slots * group
    short = full + half_slots * group

    def some(v, low, high):
        return lhs[2 * v * full + low : 2 * v * full + high, :]

    for j in range(0, held.shape[0], 2):
        parts = [some(v, 0, short) for v in range(var_count)]
        first = mm(jnp.concatenate(parts, axis=0), columns(held, j, 0, var_count))
        parts = []
        for v in range(var_count):
            parts.append(some(v, full, 2 * full))
            parts.extend(some(v, s * group, (s + 1) * group) for s in keep)
        second = mm(jnp.concatenate(parts, axis=0), columns(held, j, 1, var_count))
        for v in range(var_count):
            low = v * points + j * LANES
            high = low + 2 * LANES
            top = first[v * short : (v + 1) * short]
            bottom = second[v * short : (v + 1) * short]
            whole = (top[:full] + bottom[:full]).astype(BF16)
            for s in range(slots):
                even[s][:, low:high] = whole[s * group : (s + 1) * group]
            for i in range(half_slots):
                rows = slice(full + i * group, full + (i + 1) * group)
                lead[i][:, low:high] = bottom[rows]
                trail[i][:, low:high] = top[rows]


def join_kernel(half_slots, group, *refs):
    lead = refs[:half_slots]
    trail = refs[half_slots : 2 * half_slots]
    inner, outer = refs[2 * half_slots : 2 * half_slots + 2]
    outs = refs[2 * half_slots + 2 :]
    me = lax.axis_index("blk")
    odd = lax.rem(me, 2) == 1
    for i in range(half_slots):
        above = (i + half_slots - 1) % half_slots
        rows = (above * group, (above + 1) * group)
        from_above = jnp.where(odd, decode(inner, *rows), decode(outer, *rows))
        outs[i][...] = (lead[i][...] + from_above).astype(BF16)
        rows = (i * group, (i + 1) * group)
        from_below = jnp.where(odd, decode(outer, *rows), decode(inner, *rows))
        own = jnp.where(me == 0, 0.0, trail[i][...])
        outs[half_slots + i][...] = (own + from_below).astype(BF16)


def gram_kernel(slots, group, var_count, points, weights, classes, *refs):
    packed = refs[-1]
    blocks = 2 * slots
    me = lax.axis_index("blk")
    picked = jnp.zeros(classes.shape, F32)
    for k in range(weights.shape[0]):
        picked = picked + jnp.where(classes[...] == k, weights[k], jnp.float32(0.0))
    wide = jnp.concatenate([picked] * var_count, axis=1)
    left = jnp.concatenate([ref[...] for ref in refs[:-1]], axis=0)
    right = (left.astype(F32) * wide).astype(BF16)
    gram = lax.dot_general(
        left, right, (((1,), (1,)), ((), ())), preferred_element_type=F32
    )
    size = blocks * group
    freqs = group // 2
    same = iota((size, size), 0) % freqs == iota((size, size), 1) % freqs
    gram = jnp.where(same, gram, 0.0).reshape(blocks, 2, freqs, size)
    rows_re = gram[:, 0].reshape(blocks * freqs, size)
    rows_im = gram[:, 1].reshape(blocks * freqs, size)
    width = 2 * blocks * blocks
    row, lane = (iota((size, width), 0), iota((size, width), 1))
    fits = block_of(row // group, me, slots) == lane % blocks
    row_part = row // freqs % 2
    lane_part = lane // blocks % 2
    from_re = one_hot(fits & (row_part == lane_part))
    sign = jnp.where(lane_part == 0, 1.0, -1.0)
    from_im = jnp.where(fits & (row_part != lane_part), sign, 0.0).astype(BF16)
    total = jnp.zeros((blocks * freqs, width), F32)
    for part_re, part_im in zip(split3(rows_re), split3(rows_im)):
        total = total + (mm(part_re, from_re) + mm(part_im, from_im))
    mine = iota((freqs, width), 1) // (2 * blocks)
    out = jnp.zeros((freqs, width), F32)
    for b in range(blocks):
        block = block_of(jnp.int32(b), me, slots)
        out = out + jnp.where(mine == block, total[b * freqs : (b + 1) * freqs], 0.0)
    packed[...] = out


def mode_kernel(slots, var_count, points, scaling, feature_count, a_ref, b_ref, *refs):
    csd, eig, modes = refs[-3:]
    blocks = 2 * slots
    me = lax.axis_index("blk")
    spectra = [ref[...] for ref in refs[:-3]]
    raw = a_ref[...] + b_ref[...]
    freqs, width = raw.shape
    group = 2 * freqs
    size = blocks * group
    mat = scaling * raw
    lane_part = iota((freqs, width), 1) // blocks % 2
    is_re = lane_part == 0
    gather = one_hot(
        iota((width, width), 0) // (2 * blocks) == iota((width, width), 1) % blocks
    )

    def apply(matrix, vec_re, vec_im):
        top = matrix * jnp.where(is_re, vec_re, -vec_im)
        bottom = matrix * jnp.where(is_re, vec_im, vec_re)
        both = jnp.concatenate([top, bottom], axis=0)
        parts = jnp.concatenate([p.astype(F32) for p in split3(both)], axis=0).astype(BF16)
        got = mm(parts, gather)
        got = got[: 2 * freqs] + got[2 * freqs : 4 * freqs] + got[4 * freqs :]
        return (got[:freqs], got[freqs:])

    def over_blocks(x):
        return jnp.sum(x, axis=1, keepdims=True) * jnp.float32(1.0 / (2 * blocks))

    vec_re = jnp.full((freqs, width), 1.0 / math.sqrt(blocks), F32)
    vec_im = jnp.zeros((freqs, width), F32)
    for _ in range(ITERS):
        out_re, out_im = apply(mat, vec_re, vec_im)
        length = jnp.sqrt(over_blocks(out_re * out_re + out_im * out_im))
        vec_re, vec_im = (out_re / length, out_im / length)
    out_re, out_im = apply(mat, vec_re, vec_im)
    value = over_blocks(vec_re * out_re + vec_im * out_im)
    diagonal = iota((freqs, freqs), 0) == iota((freqs, freqs), 1)
    eig[...] = jnp.sum(
        jnp.where(diagonal, jnp.broadcast_to(value, (freqs, freqs)), 0.0), axis=0, keepdims=True
    )
    low_re = vec_re.astype(BF16)
    low_im = vec_im.astype(BF16)
    out_re, out_im = apply(raw, low_re.astype(F32), low_im.astype(F32))
    normsq = over_blocks(low_re.astype(F32) * out_re + low_im.astype(F32) * out_im)
    scale = jnp.sqrt(jnp.float32(feature_count) / normsq)
    row, lane = (iota((width, size), 0), iota((width, size), 1))
    expand = one_hot(row == block_of(lane // group, me, slots))
    wide = mm(jnp.concatenate([vec_re, vec_im], axis=0).astype(BF16), expand)
    wide_re, wide_im = (wide[:freqs], wide[freqs:])
    part = iota((freqs, size), 1) // freqs % 2
    mine = iota((freqs, size), 1) % freqs == iota((freqs, size), 0)
    coef_re = jnp.where(mine, jnp.where(part == 0, wide_re, -wide_im), 0.0)
    coef_im = jnp.where(mine, jnp.where(part == 0, wide_im, wide_re), 0.0)
    rows = 2 * var_count
    upper = iota((rows, size), 0) < var_count
    var = iota((rows, size), 0) % var_count
    tall = []
    for f in range(freqs):
        both = jnp.where(
            upper,
            jnp.broadcast_to(coef_re[f : f + 1], (rows, size)),
            jnp.broadcast_to(coef_im[f : f + 1], (rows, size)),
        )
        tall.append(
            jnp.concatenate([jnp.where(var == v, both, 0.0) for v in range(var_count)], axis=1)
        )
    coef = jnp.concatenate(tall, axis=0).astype(BF16)
    stacked = jnp.concatenate(
        [
            piece[:, v * points : (v + 1) * points]
            for v in range(var_count)
            for piece in spectra
        ],
        axis=0,
    )
    phi = mm(coef, stacked)
    for f in range(freqs):
        block = phi[f * rows : (f + 1) * rows] * scale[f : f + 1, :]
        for k in range(2):
            modes[f, k] = block[k * var_count : (k + 1) * var_count]
    tiles = jnp.concatenate(
        [
            jnp.where(
                iota((blocks, width), 1) // (2 * blocks) == iota((blocks, width), 0),
                jnp.broadcast_to(mat[f : f + 1], (blocks, width)),
                0.0,
            )
            for f in range(freqs)
        ],
        axis=0,
    )
    for k in range(2):
        row, lane = (iota((width, blocks), 0), iota((width, blocks), 1))
        fold = one_hot(row % (2 * blocks) == lane + k * blocks)
        got = jnp.zeros((freqs * blocks, blocks), F32)
        for piece in split3(tiles):
            got = got + mm(piece, fold)
        for f in range(freqs):
            csd[f, k] = got[f * blocks : (f + 1) * blocks]


def call(kernel, outs, ins, inputs, scratch, flops, moved):
    vmem = pl.BlockSpec(memory_space=pltpu.VMEM)
    return pl.pallas_call(
        kernel,
        out_shape=outs,
        in_specs=ins,
        out_specs=jax.tree.map(lambda _: vmem, outs),
        scratch_shapes=scratch,
        compiler_params=pltpu.CompilerParams(vmem_limit_bytes=VMEM_LIMIT),
        cost_estimate=pl.CostEstimate(flops=flops, bytes_accessed=moved, transcendentals=0),
    )(*inputs)


def on_device(snapshots, freq_index, weight_class, class_weight):
    row_count, var_count, points = snapshots.shape
    features = var_count * points
    slots = lax.axis_size("blk")
    half_slots = slots // 2
    me = lax.axis_index("blk")
    freqs = freq_index.shape[0] // slots
    group = 2 * freqs
    blocks = 2 * slots
    vmem = pl.BlockSpec(memory_space=pltpu.VMEM)
    smem = pl.BlockSpec(memory_space=pltpu.SMEM)
    hbm = pl.BlockSpec(memory_space=pltpu.HBM)
    shape = jax.ShapeDtypeStruct

    wide = half_slots * group
    groups = points // LANES
    inner, outer, lhs, held = call(
        functools.partial(halo_kernel, slots, group, var_count, points),
        [
            shape((wide, features + LANES), jnp.int16),
            shape((wide, features + LANES), jnp.int16),
            shape((2 * slots * group * var_count, HALF * var_count), BF16),
            shape((groups, row_count, var_count, LANES), BF16),
        ],
        [smem, hbm],
        (freq_index, pltpu.with_memory_space_constraint(snapshots, pltpu.HBM)),
        [
            pltpu.VMEM((wide, features), F32),
            pltpu.VMEM((wide, features), F32),
            pltpu.SemaphoreType.DMA((groups, 2)),
        ],
        2 * 2 * wide * HALF * features * var_count,
        2 * row_count * features,
    )

    def swap(x, first, also):
        pairs = [(i, i + 1) for i in range(first, slots - 1, 2)]
        return lax.ppermute(x, "blk", pairs + [(b, a) for a, b in pairs] + also)

    from_outer = swap(outer, 0, [])
    swapped = (swap(inner, 1, [(slots - 1, 0)]), from_outer)
    keep = [0] + list(range(half_slots + 1, slots))
    piece = shape((group, features), BF16)
    wide_piece = shape((group, features), F32)
    pieces = call(
        functools.partial(block_kernel, slots, keep, var_count, points),
        [piece] * slots + [wide_piece] * (2 * half_slots),
        [vmem, vmem],
        (lhs, held),
        [],
        2 * 3 * slots * group * HALF * features * var_count,
        2 * row_count * features,
    )

    def shift(x, s):
        return lax.ppermute(x, "blk", [(i, (i + s) % slots) for i in range(slots)])

    even = [pieces[0]] + [shift(pieces[s], s) for s in range(1, slots)]
    odd = call(
        functools.partial(join_kernel, half_slots, group),
        [piece] * slots,
        [vmem] * (slots + 2),
        (*pieces[slots:], *swapped),
        [],
        slots * group * features,
        10 * slots * group * features,
    )

    above = [odd[0]] + [shift(odd[i], s) for i, s in enumerate(keep) if i]
    under = [odd[half_slots]] + [shift(odd[half_slots + i], i) for i in range(1, half_slots)]
    width = 2 * blocks * blocks
    spectra = (*even, *above, *under)
    packed = call(
        functools.partial(gram_kernel, slots, group, var_count, points),
        shape((freqs, width), F32),
        [smem, vmem] + [vmem] * len(spectra),
        (class_weight, weight_class.reshape(1, points), *spectra),
        [],
        2 * (blocks * group) ** 2 * features,
        4 * blocks * group * features,
    )
    devices = lax.axis_size("pts")
    step = 1
    other = None
    while step < devices:
        if other is not None:
            packed = packed + other
        other = lax.ppermute(packed, "pts", [(i, i ^ step) for i in range(devices)])
        step *= 2
    total_features = features * devices
    csd, eigval, modes = call(
        functools.partial(
            mode_kernel,
            slots,
            var_count,
            points,
            1.0 / (total_features * (3.0 * NFFT / 8.0)),
            total_features,
        ),
        [
            shape((freqs, 2, blocks, blocks), F32),
            shape((1, freqs), F32),
            shape((freqs, 2, var_count, points), F32),
        ],
        [vmem] * (2 + len(spectra)),
        (packed, other, *spectra),
        [],
        2 * 2 * blocks * group * group * features,
        2 * blocks * group * features,
    )
    return (csd, eigval.reshape(freqs), modes)


def solution(mesh):
    in_specs = (P("blk", None, "pts"), P(), P("pts"), P())
    out_specs = (P("blk", None, None, None), P("blk"), P("blk", None, None, "pts"))
    return jax.shard_map(
        on_device, mesh=mesh, in_specs=in_specs, out_specs=out_specs, check_vma=False
    )
```

```python
import functools
import math

import jax
import jax.numpy as jnp
from jax import lax
from jax.experimental import pallas as pl
from jax.experimental.pallas import tpu as pltpu
from jax.sharding import PartitionSpec as P

NFFT = 768
HALF = NFFT // 2
ITERS = 3
LANES = 128
VMEM_LIMIT = 32 * 1024 * 1024
F32 = jnp.float32
BF16 = jnp.bfloat16


def iota(shape, axis):
    return lax.broadcasted_iota(jnp.int32, shape, axis)


def div(x, n):
    return x >> (n.bit_length() - 1) if n & (n - 1) == 0 else x // n


def rem(x, n):
    return x & (n - 1) if n & (n - 1) == 0 else x % n


def mm(a, b):
    return jnp.dot(a, b, preferred_element_type=F32)


def split3(x):
    high = x.astype(BF16)
    rest = x - high.astype(F32)
    mid = rest.astype(BF16)
    low = (rest - mid.astype(F32)).astype(BF16)
    return (high, mid, low)


def one_hot(condition):
    return jnp.where(condition, 1.0, 0.0).astype(BF16)


def modulo(x, n):
    return jnp.where(x < 0, x + n, x)


def block_of(slot, me, slots):
    half_slots = slots // 2
    above = slot - slots
    below = above - half_slots
    even = 2 * modulo(me - slot, slots)
    upper = 2 * modulo(me - jnp.where(above == 0, 0, above + half_slots), slots) + 1
    lower = modulo(2 * modulo(me - below, slots) - 1, 2 * slots)
    return jnp.where(slot < slots, even, jnp.where(below < 0, upper, lower))


def trig(phase):
    quarter = ((phase + NFFT // 8) * 1366) >> 18
    angle = (2.0 * math.pi / NFFT) * (phase - (NFFT // 4) * quarter).astype(F32)
    x = angle * angle
    cos = 1.0 + x * (-1.0 / 2 + x * (1.0 / 24 + x * (-1.0 / 720 + x * (1.0 / 40320))))
    sin = 1.0 + x * (-1.0 / 6 + x * (1.0 / 120 + x * (-1.0 / 5040 + x * (1.0 / 362880))))
    sin = angle * sin
    odd = (quarter & 1) != 0
    real_part = jnp.where(odd, sin, cos)
    imag_part = jnp.where(odd, cos, sin)
    real_part = jnp.where(((quarter + 1) & 2) != 0, -real_part, real_part)
    imag_part = jnp.where((quarter & 2) != 0, -imag_part, imag_part)
    return (real_part, imag_part)


def transform_rows(freqs, me, wanted, slots, group, start):
    count = group // 2
    times = start + iota((count, HALF), 1)
    window = 0.5 - 0.5 * trig(times)[0]
    row = iota((count, HALF), 0)
    out = []
    for s in wanted:
        owner = lax.rem(me + s, slots)
        freq = jnp.zeros((count, HALF), jnp.int32)
        for f in range(count):
            freq = jnp.where(row == f, freqs[owner * count + f], freq)
        product = freq * times
        turns = ((product >> 8) * 21846) >> 16
        real_part, imag_part = trig(product - NFFT * turns)
        out.append(window * real_part)
        out.append(-window * imag_part)
    return jnp.concatenate(out, axis=0).astype(BF16)


def spread(rows, var_count):
    width = HALF * var_count
    lane = iota((1, width), 1)
    pick = one_hot(div(lane, var_count) == iota((HALF, width), 0))
    wide = mm(rows, pick)
    owner = rem(lane, var_count)
    return [jnp.where(owner == v, wide, 0.0).astype(BF16) for v in range(var_count)]


def columns(held, j, half, var_count):
    rows = HALF * var_count
    parts = [
        held.at[j + i].reshape(2 * rows, LANES)[half * rows : (half + 1) * rows, :]
        for i in range(2)
    ]
    return jnp.concatenate(parts, axis=1)


def encode(values, largest, coded):
    rows, features = values.shape
    largest = jnp.maximum(jnp.max(largest, axis=1, keepdims=True), 1e-30)
    exponent = jnp.floor(jnp.log2(32000.0 / largest))
    steps = values[...] * jnp.exp2(exponent)
    coded[:, :features] = jnp.round(steps).astype(jnp.int32).astype(jnp.int16)
    tail = jnp.broadcast_to(exponent, (rows, LANES))
    coded[:, features:] = tail.astype(jnp.int32).astype(jnp.int16)


def decode(coded, low, high):
    features = coded.shape[1] - LANES
    exponent = coded[low:high, features:].astype(jnp.int32).astype(F32)[:, :1]
    steps = coded[low:high, :features].astype(jnp.int32).astype(F32)
    return steps * (1.0 / jnp.exp2(exponent))


def bins_copy(bins, freqs, sem):
    return pltpu.make_async_copy(bins, freqs, sem)


def halo_kernel(slots, group, var_count, points, bins, x_hbm, inner, outer, held, *refs):
    freqs, lhs, first, second, bins_sem, sems = refs
    fetch = bins_copy(bins, freqs, bins_sem)
    fetch.start()
    copies = [
        pltpu.make_async_copy(x_hbm.at[:, :, pl.ds(j * LANES, LANES)], held.at[j], sems.at[j])
        for j in range(held.shape[0])
    ]
    for copy in copies:
        copy.start()
    me = lax.axis_index("blk")
    odd = lax.rem(me, 2) == 1
    half_slots = slots // 2
    wide = half_slots * group
    fetch.wait()
    down_rows = transform_rows(freqs, me, range(half_slots, slots), slots, group, HALF)
    up_rows = transform_rows(freqs, me, range(1, half_slots + 1), slots, group, 0)
    parts = spread(jnp.concatenate([down_rows, up_rows], axis=0), var_count)
    size = wide * var_count
    for v, part in enumerate(parts):
        lhs[v * wide : (v + 1) * wide, :] = part[:wide]
        lhs[size + v * wide : size + (v + 1) * wide, :] = part[wide:]
    most_first = jnp.zeros((wide, 2 * LANES), F32)
    most_second = most_first
    for j in range(0, held.shape[0], 2):
        copies[j].wait()
        copies[j + 1].wait()
        down = mm(lhs[:size, :], columns(held, j, 0, var_count))
        up = mm(lhs[size:, :], columns(held, j, 1, var_count))
        for v in range(var_count):
            low = v * points + j * LANES
            lower = down[v * wide : (v + 1) * wide]
            upper = up[v * wide : (v + 1) * wide]
            mine = jnp.where(odd, upper, lower)
            other = jnp.where(odd, lower, upper)
            most_first = jnp.maximum(most_first, jnp.abs(mine))
            most_second = jnp.maximum(most_second, jnp.abs(other))
            first[:, low : low + 2 * LANES] = mine
            second[:, low : low + 2 * LANES] = other
    encode(first, most_first, inner)
    encode(second, most_second, outer)


def block_kernel(slots, keep, var_count, points, bins, held, *refs):
    outs, (freqs, lhs, bins_sem) = (refs[:-3], refs[-3:])
    fetch = bins_copy(bins, freqs, bins_sem)
    fetch.start()
    half_slots = slots // 2
    even = outs[:slots]
    lead = outs[slots : slots + half_slots]
    trail = outs[slots + half_slots :]
    group = even[0].shape[0]
    full = slots * group
    short = full + half_slots * group
    me = lax.axis_index("blk")
    fetch.wait()
    rows = [
        transform_rows(freqs, me, range(slots), slots, group, start) for start in (0, HALF)
    ]
    for v, part in enumerate(spread(jnp.concatenate(rows, axis=0), var_count)):
        lhs[2 * v * full : 2 * (v + 1) * full, :] = part

    def some(v, low, high):
        return lhs[2 * v * full + low : 2 * v * full + high, :]

    for j in range(0, held.shape[0], 2):
        parts = [some(v, 0, short) for v in range(var_count)]
        first = mm(jnp.concatenate(parts, axis=0), columns(held, j, 0, var_count))
        parts = []
        for v in range(var_count):
            parts.append(some(v, full, 2 * full))
            parts.extend(some(v, s * group, (s + 1) * group) for s in keep)
        second = mm(jnp.concatenate(parts, axis=0), columns(held, j, 1, var_count))
        for v in range(var_count):
            low = v * points + j * LANES
            high = low + 2 * LANES
            top = first[v * short : (v + 1) * short]
            bottom = second[v * short : (v + 1) * short]
            whole = (top[:full] + bottom[:full]).astype(BF16)
            for s in range(slots):
                even[s][:, low:high] = whole[s * group : (s + 1) * group]
            for i in range(half_slots):
                rows = slice(full + i * group, full + (i + 1) * group)
                lead[i][:, low:high] = bottom[rows]
                trail[i][:, low:high] = top[rows]


def join_kernel(half_slots, group, *refs):
    lead = refs[:half_slots]
    trail = refs[half_slots : 2 * half_slots]
    inner, outer = refs[2 * half_slots : 2 * half_slots + 2]
    outs = refs[2 * half_slots + 2 :]
    me = lax.axis_index("blk")
    odd = lax.rem(me, 2) == 1
    for i in range(half_slots):
        above = (i + half_slots - 1) % half_slots
        rows = (above * group, (above + 1) * group)
        from_above = jnp.where(odd, decode(inner, *rows), decode(outer, *rows))
        outs[i][...] = (lead[i][...] + from_above).astype(BF16)
        rows = (i * group, (i + 1) * group)
        from_below = jnp.where(odd, decode(outer, *rows), decode(inner, *rows))
        own = jnp.where(me == 0, 0.0, trail[i][...])
        outs[half_slots + i][...] = (own + from_below).astype(BF16)


def gram_kernel(slots, group, var_count, points, weights, classes, *refs):
    packed = refs[-1]
    blocks = 2 * slots
    me = lax.axis_index("blk")
    picked = jnp.zeros(classes.shape, F32)
    for k in range(weights.shape[0]):
        picked = picked + jnp.where(classes[...] == k, weights[k], jnp.float32(0.0))
    wide = jnp.concatenate([picked] * var_count, axis=1)
    left = jnp.concatenate([ref[...] for ref in refs[:-1]], axis=0)
    right = (left.astype(F32) * wide).astype(BF16)
    gram = lax.dot_general(
        left, right, (((1,), (1,)), ((), ())), preferred_element_type=F32
    )
    size = blocks * group
    freqs = group // 2
    same = rem(iota((size, size), 0), freqs) == rem(iota((1, size), 1), freqs)
    gram = jnp.where(same, gram, 0.0).reshape(blocks, 2, freqs, size)
    rows_re = gram[:, 0].reshape(blocks * freqs, size)
    rows_im = gram[:, 1].reshape(blocks * freqs, size)
    width = 2 * blocks * blocks
    row, lane = (iota((size, 1), 0), iota((1, width), 1))
    fits = block_of(div(row, group), me, slots) == rem(lane, blocks)
    row_part = rem(div(row, freqs), 2)
    lane_part = rem(div(lane, blocks), 2)
    from_re = one_hot(fits & (row_part == lane_part))
    sign = jnp.where(lane_part == 0, 1.0, -1.0)
    from_im = jnp.where(fits & (row_part != lane_part), sign, 0.0).astype(BF16)
    total = jnp.zeros((blocks * freqs, width), F32)
    for part_re, part_im in zip(split3(rows_re), split3(rows_im)):
        total = total + (mm(part_re, from_re) + mm(part_im, from_im))
    mine = div(iota((freqs, width), 1), 2 * blocks)
    out = jnp.zeros((freqs, width), F32)
    for b in range(blocks):
        block = block_of(jnp.int32(b), me, slots)
        out = out + jnp.where(mine == block, total[b * freqs : (b + 1) * freqs], 0.0)
    packed[...] = out


def mode_kernel(slots, var_count, points, scaling, feature_count, sums, *refs):
    csd, eig, modes = refs[-3:]
    tiles, refs = ([ref[...] for ref in refs[:sums]], refs[sums:])
    blocks = 2 * slots
    me = lax.axis_index("blk")
    spectra = [ref[...] for ref in refs[:-3]]
    raw = tiles[0] + tiles[1]
    if sums == 4:
        raw = raw + (tiles[2] + tiles[3])
    freqs, width = raw.shape
    group = 2 * freqs
    size = blocks * group
    mat = scaling * raw
    lane_part = rem(div(iota((freqs, width), 1), blocks), 2)
    is_re = lane_part == 0
    gather = one_hot(
        div(iota((width, width), 0), 2 * blocks) == rem(iota((1, width), 1), blocks)
    )

    def apply(matrix, vec_re, vec_im):
        top = matrix * jnp.where(is_re, vec_re, -vec_im)
        bottom = matrix * jnp.where(is_re, vec_im, vec_re)
        both = jnp.concatenate([top, bottom], axis=0)
        parts = jnp.concatenate([p.astype(F32) for p in split3(both)], axis=0).astype(BF16)
        got = mm(parts, gather)
        got = got[: 2 * freqs] + got[2 * freqs : 4 * freqs] + got[4 * freqs :]
        return (got[:freqs], got[freqs:])

    def over_blocks(x):
        return jnp.sum(x, axis=1, keepdims=True) * jnp.float32(1.0 / (2 * blocks))

    vec_re = jnp.full((freqs, width), 1.0 / math.sqrt(blocks), F32)
    vec_im = jnp.zeros((freqs, width), F32)
    for _ in range(ITERS):
        out_re, out_im = apply(mat, vec_re, vec_im)
        length = jnp.sqrt(over_blocks(out_re * out_re + out_im * out_im))
        vec_re, vec_im = (out_re / length, out_im / length)
    out_re, out_im = apply(mat, vec_re, vec_im)
    value = over_blocks(vec_re * out_re + vec_im * out_im)
    diagonal = iota((freqs, freqs), 0) == iota((freqs, freqs), 1)
    eig[...] = jnp.sum(
        jnp.where(diagonal, jnp.broadcast_to(value, (freqs, freqs)), 0.0), axis=0, keepdims=True
    )
    low_re = vec_re.astype(BF16)
    low_im = vec_im.astype(BF16)
    out_re, out_im = apply(raw, low_re.astype(F32), low_im.astype(F32))
    normsq = over_blocks(low_re.astype(F32) * out_re + low_im.astype(F32) * out_im)
    scale = jnp.sqrt(jnp.float32(feature_count) / normsq)
    lane = iota((1, size), 1)
    expand = one_hot(iota((width, size), 0) == block_of(div(lane, group), me, slots))
    wide = mm(jnp.concatenate([vec_re, vec_im], axis=0).astype(BF16), expand)
    wide_re, wide_im = (wide[:freqs], wide[freqs:])
    part = rem(div(lane, freqs), 2)
    mine = rem(lane, freqs) == iota((freqs, size), 0)
    coef_re = jnp.where(mine, jnp.where(part == 0, wide_re, -wide_im), 0.0)
    coef_im = jnp.where(mine, jnp.where(part == 0, wide_im, wide_re), 0.0)
    rows = 2 * var_count
    upper = iota((rows, size), 0) < var_count
    var = rem(iota((rows, size), 0), var_count)
    tall = []
    for f in range(freqs):
        both = jnp.where(
            upper,
            jnp.broadcast_to(coef_re[f : f + 1], (rows, size)),
            jnp.broadcast_to(coef_im[f : f + 1], (rows, size)),
        )
        tall.append(
            jnp.concatenate([jnp.where(var == v, both, 0.0) for v in range(var_count)], axis=1)
        )
    coef = jnp.concatenate(tall, axis=0).astype(BF16)
    stacked = jnp.concatenate(
        [
            piece[:, v * points : (v + 1) * points]
            for v in range(var_count)
            for piece in spectra
        ],
        axis=0,
    )
    phi = mm(coef, stacked)
    for f in range(freqs):
        block = phi[f * rows : (f + 1) * rows] * scale[f : f + 1, :]
        for k in range(2):
            modes[f, k] = block[k * var_count : (k + 1) * var_count]
    split_rows = jnp.concatenate(
        [
            jnp.where(
                div(iota((blocks, width), 1), 2 * blocks) == iota((blocks, width), 0),
                jnp.broadcast_to(mat[f : f + 1], (blocks, width)),
                0.0,
            )
            for f in range(freqs)
        ],
        axis=0,
    )
    for k in range(2):
        row, lane = (iota((width, blocks), 0), iota((width, blocks), 1))
        fold = one_hot(rem(row, 2 * blocks) == lane + k * blocks)
        got = jnp.zeros((freqs * blocks, blocks), F32)
        for piece in split3(split_rows):
            got = got + mm(piece, fold)
        for f in range(freqs):
            csd[f, k] = got[f * blocks : (f + 1) * blocks]


def call(kernel, outs, ins, inputs, scratch, flops, moved):
    vmem = pl.BlockSpec(memory_space=pltpu.VMEM)
    return pl.pallas_call(
        kernel,
        out_shape=outs,
        in_specs=ins,
        out_specs=jax.tree.map(lambda _: vmem, outs),
        scratch_shapes=scratch,
        compiler_params=pltpu.CompilerParams(vmem_limit_bytes=VMEM_LIMIT),
        cost_estimate=pl.CostEstimate(flops=flops, bytes_accessed=moved, transcendentals=0),
    )(*inputs)


def on_device(snapshots, freq_index, weight_class, class_weight):
    row_count, var_count, points = snapshots.shape
    features = var_count * points
    slots = lax.axis_size("blk")
    half_slots = slots // 2
    me = lax.axis_index("blk")
    freqs = freq_index.shape[0] // slots
    group = 2 * freqs
    blocks = 2 * slots
    vmem = pl.BlockSpec(memory_space=pltpu.VMEM)
    smem = pl.BlockSpec(memory_space=pltpu.SMEM)
    hbm = pl.BlockSpec(memory_space=pltpu.HBM)
    shape = jax.ShapeDtypeStruct

    wide = half_slots * group
    groups = points // LANES
    bins = pltpu.with_memory_space_constraint(freq_index, pltpu.HBM)
    bins_smem = pltpu.SMEM(freq_index.shape, jnp.int32)
    inner, outer, held = call(
        functools.partial(halo_kernel, slots, group, var_count, points),
        [
            shape((wide, features + LANES), jnp.int16),
            shape((wide, features + LANES), jnp.int16),
            shape((groups, row_count, var_count, LANES), BF16),
        ],
        [hbm, hbm],
        (bins, pltpu.with_memory_space_constraint(snapshots, pltpu.HBM)),
        [
            bins_smem,
            pltpu.VMEM((2 * wide * var_count, HALF * var_count), BF16),
            pltpu.VMEM((wide, features), F32),
            pltpu.VMEM((wide, features), F32),
            pltpu.SemaphoreType.DMA,
            pltpu.SemaphoreType.DMA((groups,)),
        ],
        2 * 2 * wide * HALF * features * var_count,
        2 * row_count * features,
    )

    def swap(x, first, also):
        pairs = [(i, i + 1) for i in range(first, slots - 1, 2)]
        return lax.ppermute(x, "blk", pairs + [(b, a) for a, b in pairs] + also)

    from_outer = swap(outer, 0, [])
    swapped = (swap(inner, 1, [(slots - 1, 0)]), from_outer)
    keep = [0] + list(range(half_slots + 1, slots))
    piece = shape((group, features), BF16)
    wide_piece = shape((group, features), F32)
    pieces = call(
        functools.partial(block_kernel, slots, keep, var_count, points),
        [piece] * slots + [wide_piece] * (2 * half_slots),
        [hbm, vmem],
        (bins, held),
        [
            bins_smem,
            pltpu.VMEM((2 * slots * group * var_count, HALF * var_count), BF16),
            pltpu.SemaphoreType.DMA,
        ],
        2 * 3 * slots * group * HALF * features * var_count,
        2 * row_count * features,
    )

    def shift(x, s):
        return lax.ppermute(x, "blk", [(i, (i + s) % slots) for i in range(slots)])

    even = [pieces[0]] + [shift(pieces[s], s) for s in range(1, slots)]
    odd = call(
        functools.partial(join_kernel, half_slots, group),
        [piece] * slots,
        [vmem] * (slots + 2),
        (*pieces[slots:], *swapped),
        [],
        slots * group * features,
        10 * slots * group * features,
    )

    above = [odd[0]] + [shift(odd[i], s) for i, s in enumerate(keep) if i]
    under = [odd[half_slots]] + [shift(odd[half_slots + i], i) for i in range(1, half_slots)]
    width = 2 * blocks * blocks
    spectra = (*even, *above, *under)
    packed = call(
        functools.partial(gram_kernel, slots, group, var_count, points),
        shape((freqs, width), F32),
        [smem, vmem] + [vmem] * len(spectra),
        (class_weight, weight_class.reshape(1, points), *spectra),
        [],
        2 * (blocks * group) ** 2 * features,
        4 * blocks * group * features,
    )
    devices = lax.axis_size("pts")
    def from_peer(x, step):
        return lax.ppermute(x, "pts", [(i, i ^ step) for i in range(devices)])

    parts = [packed]
    step = 1
    while step < devices:
        total = functools.reduce(jnp.add, parts[:2])
        if len(parts) == 4:
            total = total + (parts[2] + parts[3])
        by_four = step > 1 and 4 * step <= devices
        steps = (step, 2 * step, 3 * step) if by_four else (step,)
        parts = [total] + [from_peer(total, i) for i in steps]
        step *= 4 if by_four else 2
    total_features = features * devices
    csd, eigval, modes = call(
        functools.partial(
            mode_kernel,
            slots,
            var_count,
            points,
            1.0 / (total_features * (3.0 * NFFT / 8.0)),
            total_features,
            len(parts),
        ),
        [
            shape((freqs, 2, blocks, blocks), F32),
            shape((1, freqs), F32),
            shape((freqs, 2, var_count, points), F32),
        ],
        [vmem] * (len(parts) + len(spectra)),
        (*parts, *spectra),
        [],
        2 * 2 * blocks * group * group * features,
        2 * blocks * group * features,
    )
    return (csd, eigval.reshape(freqs), modes)


def solution(mesh):
    in_specs = (P("blk", None, "pts"), P(), P("pts"), P())
    out_specs = (P("blk", None, None, None), P("blk"), P("blk", None, None, "pts"))
    return jax.shard_map(
        on_device, mesh=mesh, in_specs=in_specs, out_specs=out_specs, check_vma=False
    )
```

```python
import functools
import math

import jax
import jax.numpy as jnp
from jax import lax
from jax.experimental import pallas as pl
from jax.experimental.pallas import tpu as pltpu
from jax.sharding import PartitionSpec as P

NFFT = 768
HALF = NFFT // 2
ITERS = 3
LANES = 128
VMEM_LIMIT = 32 * 1024 * 1024
F32 = jnp.float32
BF16 = jnp.bfloat16


def iota(shape, axis):
    return lax.broadcasted_iota(jnp.int32, shape, axis)


def div(x, n):
    return x >> (n.bit_length() - 1) if n & (n - 1) == 0 else x // n


def rem(x, n):
    return x & (n - 1) if n & (n - 1) == 0 else x % n


def mm(a, b):
    return jnp.dot(a, b, preferred_element_type=F32)


def split3(x):
    high = x.astype(BF16)
    rest = x - high.astype(F32)
    mid = rest.astype(BF16)
    low = (rest - mid.astype(F32)).astype(BF16)
    return (high, mid, low)


def one_hot(condition):
    return jnp.where(condition, 1.0, 0.0).astype(BF16)


def modulo(x, n):
    return jnp.where(x < 0, x + n, x)


def block_of(slot, me, slots):
    half_slots = slots // 2
    above = slot - slots
    below = above - half_slots
    even = 2 * modulo(me - slot, slots)
    upper = 2 * modulo(me - jnp.where(above == 0, 0, above + half_slots), slots) + 1
    lower = modulo(2 * modulo(me - below, slots) - 1, 2 * slots)
    return jnp.where(slot < slots, even, jnp.where(below < 0, upper, lower))


def trig(phase):
    quarter = ((phase + NFFT // 8) * 1366) >> 18
    angle = (2.0 * math.pi / NFFT) * (phase - (NFFT // 4) * quarter).astype(F32)
    x = angle * angle
    cos = 1.0 + x * (-1.0 / 2 + x * (1.0 / 24 + x * (-1.0 / 720 + x * (1.0 / 40320))))
    sin = 1.0 + x * (-1.0 / 6 + x * (1.0 / 120 + x * (-1.0 / 5040 + x * (1.0 / 362880))))
    sin = angle * sin
    odd = (quarter & 1) != 0
    real_part = jnp.where(odd, sin, cos)
    imag_part = jnp.where(odd, cos, sin)
    real_part = jnp.where(((quarter + 1) & 2) != 0, -real_part, real_part)
    imag_part = jnp.where((quarter & 2) != 0, -imag_part, imag_part)
    return (real_part, imag_part)


def transform_rows(freqs, me, wanted, slots, group, start):
    count = group // 2
    times = start + iota((count, HALF), 1)
    window = 0.5 - 0.5 * trig(times)[0]
    row = iota((count, HALF), 0)
    out = []
    for s in wanted:
        owner = lax.rem(me + s, slots)
        freq = jnp.zeros((count, HALF), jnp.int32)
        for f in range(count):
            freq = jnp.where(row == f, freqs[owner * count + f], freq)
        product = freq * times
        turns = ((product >> 8) * 21846) >> 16
        real_part, imag_part = trig(product - NFFT * turns)
        out.append(window * real_part)
        out.append(-window * imag_part)
    return jnp.concatenate(out, axis=0).astype(BF16)


def spread(rows, var_count):
    width = HALF * var_count
    lane = iota((1, width), 1)
    pick = one_hot(div(lane, var_count) == iota((HALF, width), 0))
    wide = mm(rows, pick)
    owner = rem(lane, var_count)
    return [jnp.where(owner == v, wide, 0.0).astype(BF16) for v in range(var_count)]


def columns(held, j, var_count):
    rows = HALF * var_count
    parts = [held.at[j + i].reshape(rows, LANES)[...] for i in range(2)]
    return jnp.concatenate(parts, axis=1)


def load_copies(x_hbm, half, held, sems):
    rows = pl.ds(half * HALF, HALF)
    return [
        pltpu.make_async_copy(x_hbm.at[rows, :, pl.ds(j * LANES, LANES)], held.at[j], sems.at[j])
        for j in range(held.shape[0])
    ]


def encode(values, largest, coded):
    rows, features = values.shape
    largest = jnp.maximum(jnp.max(largest, axis=1, keepdims=True), 1e-30)
    exponent = jnp.floor(jnp.log2(32000.0 / largest))
    steps = values[...] * jnp.exp2(exponent)
    coded[:, :features] = jnp.round(steps).astype(jnp.int32).astype(jnp.int16)
    tail = jnp.broadcast_to(exponent, (rows, LANES))
    coded[:, features:] = tail.astype(jnp.int32).astype(jnp.int16)


def decode(coded, low, high):
    features = coded.shape[1] - LANES
    exponent = coded[low:high, features:].astype(jnp.int32).astype(F32)[:, :1]
    steps = coded[low:high, :features].astype(jnp.int32).astype(F32)
    return steps * (1.0 / jnp.exp2(exponent))


def bins_copy(bins, freqs, sem):
    return pltpu.make_async_copy(bins, freqs, sem)


def inner_kernel(slots, group, var_count, points, bins, x_hbm, inner, near, *refs):
    freqs, lhs, raw, bins_sem, sems = refs
    fetch = bins_copy(bins, freqs, bins_sem)
    fetch.start()
    me = lax.axis_index("blk")
    odd = lax.rem(me, 2)
    copies = load_copies(x_hbm, odd, near, sems)
    for copy in copies:
        copy.start()
    half_slots = slots // 2
    wide = half_slots * group
    first = jnp.where(odd == 1, 1, half_slots)
    fetch.wait()
    wanted = [first + i for i in range(half_slots)]
    rows = transform_rows(freqs, me, wanted, slots, group, (1 - odd) * HALF)
    for v, part in enumerate(spread(rows, var_count)):
        lhs[v * wide : (v + 1) * wide, :] = part
    most = jnp.zeros((wide, 2 * LANES), F32)
    for j in range(0, near.shape[0], 2):
        copies[j].wait()
        copies[j + 1].wait()
        got = mm(lhs[...], columns(near, j, var_count))
        for v in range(var_count):
            low = v * points + j * LANES
            mine = got[v * wide : (v + 1) * wide]
            most = jnp.maximum(most, jnp.abs(mine))
            raw[:, low : low + 2 * LANES] = mine
    encode(raw, most, inner)


def block_kernel(slots, keep, group, var_count, points, bins, x_hbm, near, *refs):
    outs, (freqs, lhs, far, raw, bins_sem, sems) = (refs[:-6], refs[-6:])
    fetch = bins_copy(bins, freqs, bins_sem)
    fetch.start()
    me = lax.axis_index("blk")
    odd = lax.rem(me, 2)
    copies = load_copies(x_hbm, 1 - odd, far, sems)
    for copy in copies:
        copy.start()
    half_slots = slots // 2
    outer = outs[0]
    even = outs[1 : 1 + slots]
    lead = outs[1 + slots : 1 + slots + half_slots]
    trail = outs[1 + slots + half_slots :]
    full = slots * group
    short = full + half_slots * group
    fetch.wait()
    rows = [
        transform_rows(freqs, me, range(slots), slots, group, start * HALF)
        for start in (odd, 1 - odd)
    ]
    for v, part in enumerate(spread(jnp.concatenate(rows, axis=0), var_count)):
        lhs[2 * v * full : 2 * (v + 1) * full, :] = part
    is_odd = odd == 1
    near_parts = []
    far_parts = []
    for v in range(var_count):
        base = 2 * v * full
        near_parts.append((base, full))
        for i, s in enumerate(keep):
            slot = jnp.where(is_odd, s, i)
            near_parts.append((pl.multiple_of(base + full + slot * group, group), group))
        far_parts.append((base + full, full))
        far_parts.append((base, full))

    def rows_of(parts):
        return jnp.concatenate([lhs[pl.ds(low, size), :] for low, size in parts], axis=0)

    most = jnp.zeros((half_slots * group, 2 * LANES), F32)
    for j in range(0, far.shape[0], 2):
        from_near = mm(rows_of(near_parts), columns(near, j, var_count))
        copies[j].wait()
        copies[j + 1].wait()
        from_far = mm(rows_of(far_parts), columns(far, j, var_count))
        for v in range(var_count):
            low = v * points + j * LANES
            high = low + 2 * LANES
            top = from_near[v * short : (v + 1) * short]
            bottom = from_far[2 * v * full : 2 * (v + 1) * full]
            whole = (top[:full] + bottom[:full]).astype(BF16)
            other = bottom[full:]
            for s in range(slots):
                even[s][:, low:high] = whole[s * group : (s + 1) * group]
            for i, s in enumerate(keep):
                mine = top[full + i * group : full + (i + 1) * group]
                begun = other[s * group : (s + 1) * group]
                ended = other[i * group : (i + 1) * group]
                lead[i][:, low:high] = jnp.where(is_odd, mine, begun)
                trail[i][:, low:high] = jnp.where(is_odd, ended, mine)
            sent = jnp.where(
                is_odd, other[half_slots * group :], other[group : (half_slots + 1) * group]
            )
            most = jnp.maximum(most, jnp.abs(sent))
            raw[:, low:high] = sent
    encode(raw, most, outer)


def inner_join_kernel(half_slots, group, *refs):
    lead = refs[:half_slots]
    trail = refs[half_slots : 2 * half_slots]
    inner = refs[2 * half_slots]
    joined = refs[2 * half_slots + 1 :]
    me = lax.axis_index("blk")
    odd = lax.rem(me, 2) == 1
    for i in range(half_slots):
        above = (i + half_slots - 1) % half_slots
        begun = lead[i][...] + decode(inner, above * group, (above + 1) * group)
        own = jnp.where(me == 0, 0.0, trail[i][...])
        ended = own + decode(inner, i * group, (i + 1) * group)
        joined[i][...] = jnp.where(odd, begun, ended).astype(BF16)


def outer_join_kernel(half_slots, group, *refs):
    lead = refs[:half_slots]
    trail = refs[half_slots : 2 * half_slots]
    outer = refs[2 * half_slots]
    joined = refs[2 * half_slots + 1 : 3 * half_slots + 1]
    outs = refs[3 * half_slots + 1 :]
    odd = lax.rem(lax.axis_index("blk"), 2) == 1
    for i in range(half_slots):
        above = (i + half_slots - 1) % half_slots
        begun = lead[i][...] + decode(outer, above * group, (above + 1) * group)
        ended = trail[i][...] + decode(outer, i * group, (i + 1) * group)
        other = jnp.where(odd, ended, begun).astype(BF16)
        outs[i][...] = jnp.where(odd, joined[i][...], other)
        outs[half_slots + i][...] = jnp.where(odd, other, joined[i][...])


def gram_kernel(slots, group, var_count, points, weights, classes, *refs):
    packed = refs[-1]
    blocks = 2 * slots
    me = lax.axis_index("blk")
    picked = jnp.zeros(classes.shape, F32)
    for k in range(weights.shape[0]):
        picked = picked + jnp.where(classes[...] == k, weights[k], jnp.float32(0.0))
    wide = jnp.concatenate([picked] * var_count, axis=1)
    left = jnp.concatenate([ref[...] for ref in refs[:-1]], axis=0)
    right = (left.astype(F32) * wide).astype(BF16)
    gram = lax.dot_general(
        left, right, (((1,), (1,)), ((), ())), preferred_element_type=F32
    )
    size = blocks * group
    freqs = group // 2
    same = rem(iota((size, size), 0), freqs) == rem(iota((1, size), 1), freqs)
    gram = jnp.where(same, gram, 0.0).reshape(blocks, 2, freqs, size)
    rows_re = gram[:, 0].reshape(blocks * freqs, size)
    rows_im = gram[:, 1].reshape(blocks * freqs, size)
    width = 2 * blocks * blocks
    row, lane = (iota((size, 1), 0), iota((1, width), 1))
    fits = block_of(div(row, group), me, slots) == rem(lane, blocks)
    row_part = rem(div(row, freqs), 2)
    lane_part = rem(div(lane, blocks), 2)
    from_re = one_hot(fits & (row_part == lane_part))
    sign = jnp.where(lane_part == 0, 1.0, -1.0)
    from_im = jnp.where(fits & (row_part != lane_part), sign, 0.0).astype(BF16)
    total = jnp.zeros((blocks * freqs, width), F32)
    for part_re, part_im in zip(split3(rows_re), split3(rows_im)):
        total = total + (mm(part_re, from_re) + mm(part_im, from_im))
    mine = div(iota((freqs, width), 1), 2 * blocks)
    out = jnp.zeros((freqs, width), F32)
    for b in range(blocks):
        block = block_of(jnp.int32(b), me, slots)
        out = out + jnp.where(mine == block, total[b * freqs : (b + 1) * freqs], 0.0)
    packed[...] = out


def mode_kernel(slots, var_count, points, scaling, feature_count, sums, *refs):
    csd, eig, modes = refs[-3:]
    tiles, refs = ([ref[...] for ref in refs[:sums]], refs[sums:])
    blocks = 2 * slots
    me = lax.axis_index("blk")
    spectra = [ref[...] for ref in refs[:-3]]
    raw = tiles[0] + tiles[1]
    if sums == 4:
        raw = raw + (tiles[2] + tiles[3])
    freqs, width = raw.shape
    group = 2 * freqs
    size = blocks * group
    mat = scaling * raw
    lane_part = rem(div(iota((freqs, width), 1), blocks), 2)
    is_re = lane_part == 0
    gather = one_hot(
        div(iota((width, width), 0), 2 * blocks) == rem(iota((1, width), 1), blocks)
    )

    def apply(matrix, vec_re, vec_im):
        top = matrix * jnp.where(is_re, vec_re, -vec_im)
        bottom = matrix * jnp.where(is_re, vec_im, vec_re)
        both = jnp.concatenate([top, bottom], axis=0)
        parts = jnp.concatenate([p.astype(F32) for p in split3(both)], axis=0).astype(BF16)
        got = mm(parts, gather)
        got = got[: 2 * freqs] + got[2 * freqs : 4 * freqs] + got[4 * freqs :]
        return (got[:freqs], got[freqs:])

    def over_blocks(x):
        return jnp.sum(x, axis=1, keepdims=True) * jnp.float32(1.0 / (2 * blocks))

    vec_re = jnp.full((freqs, width), 1.0 / math.sqrt(blocks), F32)
    vec_im = jnp.zeros((freqs, width), F32)
    for _ in range(ITERS):
        out_re, out_im = apply(mat, vec_re, vec_im)
        length = jnp.sqrt(over_blocks(out_re * out_re + out_im * out_im))
        vec_re, vec_im = (out_re / length, out_im / length)
    out_re, out_im = apply(mat, vec_re, vec_im)
    value = over_blocks(vec_re * out_re + vec_im * out_im)
    diagonal = iota((freqs, freqs), 0) == iota((freqs, freqs), 1)
    eig[...] = jnp.sum(
        jnp.where(diagonal, jnp.broadcast_to(value, (freqs, freqs)), 0.0), axis=0, keepdims=True
    )
    low_re = vec_re.astype(BF16)
    low_im = vec_im.astype(BF16)
    out_re, out_im = apply(raw, low_re.astype(F32), low_im.astype(F32))
    normsq = over_blocks(low_re.astype(F32) * out_re + low_im.astype(F32) * out_im)
    scale = jnp.sqrt(jnp.float32(feature_count) / normsq)
    lane = iota((1, size), 1)
    expand = one_hot(iota((width, size), 0) == block_of(div(lane, group), me, slots))
    wide = mm(jnp.concatenate([vec_re, vec_im], axis=0).astype(BF16), expand)
    wide_re, wide_im = (wide[:freqs], wide[freqs:])
    part = rem(div(lane, freqs), 2)
    mine = rem(lane, freqs) == iota((freqs, size), 0)
    coef_re = jnp.where(mine, jnp.where(part == 0, wide_re, -wide_im), 0.0)
    coef_im = jnp.where(mine, jnp.where(part == 0, wide_im, wide_re), 0.0)
    rows = 2 * var_count
    upper = iota((rows, size), 0) < var_count
    var = rem(iota((rows, size), 0), var_count)
    tall = []
    for f in range(freqs):
        both = jnp.where(
            upper,
            jnp.broadcast_to(coef_re[f : f + 1], (rows, size)),
            jnp.broadcast_to(coef_im[f : f + 1], (rows, size)),
        )
        tall.append(
            jnp.concatenate([jnp.where(var == v, both, 0.0) for v in range(var_count)], axis=1)
        )
    coef = jnp.concatenate(tall, axis=0).astype(BF16)
    stacked = jnp.concatenate(
        [
            piece[:, v * points : (v + 1) * points]
            for v in range(var_count)
            for piece in spectra
        ],
        axis=0,
    )
    phi = mm(coef, stacked)
    for f in range(freqs):
        block = phi[f * rows : (f + 1) * rows] * scale[f : f + 1, :]
        for k in range(2):
            modes[f, k] = block[k * var_count : (k + 1) * var_count]
    split_rows = jnp.concatenate(
        [
            jnp.where(
                div(iota((blocks, width), 1), 2 * blocks) == iota((blocks, width), 0),
                jnp.broadcast_to(mat[f : f + 1], (blocks, width)),
                0.0,
            )
            for f in range(freqs)
        ],
        axis=0,
    )
    for k in range(2):
        row, lane = (iota((width, blocks), 0), iota((width, blocks), 1))
        fold = one_hot(rem(row, 2 * blocks) == lane + k * blocks)
        got = jnp.zeros((freqs * blocks, blocks), F32)
        for piece in split3(split_rows):
            got = got + mm(piece, fold)
        for f in range(freqs):
            csd[f, k] = got[f * blocks : (f + 1) * blocks]


def call(kernel, outs, ins, inputs, scratch, flops, moved):
    vmem = pl.BlockSpec(memory_space=pltpu.VMEM)
    return pl.pallas_call(
        kernel,
        out_shape=outs,
        in_specs=ins,
        out_specs=jax.tree.map(lambda _: vmem, outs),
        scratch_shapes=scratch,
        compiler_params=pltpu.CompilerParams(vmem_limit_bytes=VMEM_LIMIT),
        cost_estimate=pl.CostEstimate(flops=flops, bytes_accessed=moved, transcendentals=0),
    )(*inputs)


def on_device(snapshots, freq_index, weight_class, class_weight):
    row_count, var_count, points = snapshots.shape
    features = var_count * points
    slots = lax.axis_size("blk")
    half_slots = slots // 2
    me = lax.axis_index("blk")
    freqs = freq_index.shape[0] // slots
    group = 2 * freqs
    blocks = 2 * slots
    vmem = pl.BlockSpec(memory_space=pltpu.VMEM)
    smem = pl.BlockSpec(memory_space=pltpu.SMEM)
    hbm = pl.BlockSpec(memory_space=pltpu.HBM)
    shape = jax.ShapeDtypeStruct

    wide = half_slots * group
    groups = points // LANES
    bins = pltpu.with_memory_space_constraint(freq_index, pltpu.HBM)
    bins_smem = pltpu.SMEM(freq_index.shape, jnp.int32)
    source = pltpu.with_memory_space_constraint(snapshots, pltpu.HBM)
    half_block = (groups, HALF, var_count, LANES)
    payload = shape((wide, features + LANES), jnp.int16)
    width = HALF * var_count
    sems = [pltpu.SemaphoreType.DMA, pltpu.SemaphoreType.DMA((groups,))]
    raw = pltpu.VMEM((wide, features), F32)
    inner, near = call(
        functools.partial(inner_kernel, slots, group, var_count, points),
        [payload, shape(half_block, BF16)],
        [hbm, hbm],
        (bins, source),
        [bins_smem, pltpu.VMEM((wide * var_count, width), BF16), raw, *sems],
        2 * wide * features * width,
        row_count * features,
    )

    def swap(x, first, also):
        pairs = [(i, i + 1) for i in range(first, slots - 1, 2)]
        return lax.ppermute(x, "blk", pairs + [(b, a) for a, b in pairs] + also)

    keep = [0] + list(range(half_slots + 1, slots))
    piece = shape((group, features), BF16)
    wide_piece = shape((group, features), F32)
    outer, *pieces = call(
        functools.partial(block_kernel, slots, keep, group, var_count, points),
        [payload] + [piece] * slots + [wide_piece] * (2 * half_slots),
        [hbm, hbm, vmem],
        (bins, source, near),
        [
            bins_smem,
            pltpu.VMEM((2 * slots * group * var_count, width), BF16),
            pltpu.VMEM(half_block, BF16),
            raw,
            *sems,
        ],
        2 * 4 * slots * group * features * width,
        row_count * features,
    )
    from_outer = swap(outer, 0, [])
    from_inner = swap(inner, 1, [(slots - 1, 0)])

    def shift(x, s):
        return lax.ppermute(x, "blk", [(i, (i + s) % slots) for i in range(slots)])

    even = [pieces[0]] + [shift(pieces[s], s) for s in range(1, slots)]
    halves = pieces[slots:]
    joined = call(
        functools.partial(inner_join_kernel, half_slots, group),
        [piece] * half_slots,
        [vmem] * (slots + 1),
        (*halves, from_inner),
        [],
        slots * group * features,
        10 * slots * group * features,
    )
    odd = call(
        functools.partial(outer_join_kernel, half_slots, group),
        [piece] * slots,
        [vmem] * (slots + half_slots + 1),
        (*halves, from_outer, *joined),
        [],
        slots * group * features,
        10 * slots * group * features,
    )
    above = [odd[0]] + [shift(odd[i], s) for i, s in enumerate(keep) if i]
    under = [odd[half_slots]] + [shift(odd[half_slots + i], i) for i in range(1, half_slots)]
    tile = 2 * blocks * blocks
    spectra = (*even, *above, *under)
    packed = call(
        functools.partial(gram_kernel, slots, group, var_count, points),
        shape((freqs, tile), F32),
        [smem, vmem] + [vmem] * len(spectra),
        (class_weight, weight_class.reshape(1, points), *spectra),
        [],
        2 * (blocks * group) ** 2 * features,
        4 * blocks * group * features,
    )
    devices = lax.axis_size("pts")
    def from_peer(x, step):
        return lax.ppermute(x, "pts", [(i, i ^ step) for i in range(devices)])

    parts = [packed]
    step = 1
    while step < devices:
        total = functools.reduce(jnp.add, parts[:2])
        if len(parts) == 4:
            total = total + (parts[2] + parts[3])
        by_four = step > 1 and 4 * step <= devices
        steps = (step, 2 * step, 3 * step) if by_four else (step,)
        parts = [total] + [from_peer(total, i) for i in steps]
        step *= 4 if by_four else 2
    total_features = features * devices
    csd, eigval, modes = call(
        functools.partial(
            mode_kernel,
            slots,
            var_count,
            points,
            1.0 / (total_features * (3.0 * NFFT / 8.0)),
            total_features,
            len(parts),
        ),
        [
            shape((freqs, 2, blocks, blocks), F32),
            shape((1, freqs), F32),
            shape((freqs, 2, var_count, points), F32),
        ],
        [vmem] * (len(parts) + len(spectra)),
        (*parts, *spectra),
        [],
        2 * 2 * blocks * group * group * features,
        2 * blocks * group * features,
    )
    return (csd, eigval.reshape(freqs), modes)


def solution(mesh):
    in_specs = (P("blk", None, "pts"), P(), P("pts"), P())
    out_specs = (P("blk", None, None, None), P("blk"), P("blk", None, None, "pts"))
    return jax.shard_map(
        on_device, mesh=mesh, in_specs=in_specs, out_specs=out_specs, check_vma=False
    )
```

```python
import functools
import math

import jax
import jax.numpy as jnp
from jax import lax
from jax.experimental import pallas as pl
from jax.experimental.pallas import tpu as pltpu
from jax.sharding import PartitionSpec as P

NFFT = 768
HALF = NFFT // 2
ITERS = 3
LANES = 128
VMEM_LIMIT = 32 * 1024 * 1024
F32 = jnp.float32
BF16 = jnp.bfloat16


def iota(shape, axis):
    return lax.broadcasted_iota(jnp.int32, shape, axis)


def div(x, n):
    return x >> (n.bit_length() - 1) if n & (n - 1) == 0 else x // n


def rem(x, n):
    return x & (n - 1) if n & (n - 1) == 0 else x % n


def mm(a, b):
    return jnp.dot(a, b, preferred_element_type=F32)


def split3(x):
    high = x.astype(BF16)
    rest = x - high.astype(F32)
    mid = rest.astype(BF16)
    low = (rest - mid.astype(F32)).astype(BF16)
    return (high, mid, low)


def one_hot(condition):
    return jnp.where(condition, 1.0, 0.0).astype(BF16)


def modulo(x, n):
    return jnp.where(x < 0, x + n, x)


def block_of(slot, me, slots):
    half_slots = slots // 2
    above = slot - slots
    below = above - half_slots
    even = 2 * modulo(me - slot, slots)
    upper = 2 * modulo(me - jnp.where(above == 0, 0, above + half_slots), slots) + 1
    lower = modulo(2 * modulo(me - below, slots) - 1, 2 * slots)
    return jnp.where(slot < slots, even, jnp.where(below < 0, upper, lower))


def trig(phase):
    quarter = ((phase + NFFT // 8) * 1366) >> 18
    angle = (2.0 * math.pi / NFFT) * (phase - (NFFT // 4) * quarter).astype(F32)
    x = angle * angle
    cos = 1.0 + x * (-1.0 / 2 + x * (1.0 / 24 + x * (-1.0 / 720 + x * (1.0 / 40320))))
    sin = 1.0 + x * (-1.0 / 6 + x * (1.0 / 120 + x * (-1.0 / 5040 + x * (1.0 / 362880))))
    sin = angle * sin
    odd = (quarter & 1) != 0
    real_part = jnp.where(odd, sin, cos)
    imag_part = jnp.where(odd, cos, sin)
    real_part = jnp.where(((quarter + 1) & 2) != 0, -real_part, real_part)
    imag_part = jnp.where((quarter & 2) != 0, -imag_part, imag_part)
    return (real_part, imag_part)


def transform_rows(freqs, me, wanted, slots, group, start):
    count = group // 2
    times = start + iota((count, HALF), 1)
    window = 0.5 - 0.5 * trig(times)[0]
    row = iota((count, HALF), 0)
    out = []
    for s in wanted:
        owner = lax.rem(me + s, slots)
        freq = jnp.zeros((count, HALF), jnp.int32)
        for f in range(count):
            freq = jnp.where(row == f, freqs[owner * count + f], freq)
        product = freq * times
        turns = ((product >> 8) * 21846) >> 16
        real_part, imag_part = trig(product - NFFT * turns)
        out.append(window * real_part)
        out.append(-window * imag_part)
    return jnp.concatenate(out, axis=0).astype(BF16)


def spread(rows, var_count):
    lane = iota((1, LANES * var_count), 1)
    pick = one_hot(div(lane, var_count) == iota((LANES, LANES * var_count), 0))
    pieces = [mm(rows[:, t : t + LANES], pick) for t in range(0, HALF, LANES)]
    wide = jnp.concatenate(pieces, axis=1)
    owner = rem(iota((1, HALF * var_count), 1), var_count)
    return [jnp.where(owner == v, wide, 0.0).astype(BF16) for v in range(var_count)]


def columns(held, j, var_count):
    rows = HALF * var_count
    parts = [held.at[j + i].reshape(rows, LANES)[...] for i in range(2)]
    return jnp.concatenate(parts, axis=1)


def load_copies(x_hbm, half, held, sems):
    rows = pl.ds(half * HALF, HALF)
    return [
        pltpu.make_async_copy(x_hbm.at[rows, :, pl.ds(j * LANES, LANES)], held.at[j], sems.at[j])
        for j in range(held.shape[0])
    ]


def encode(values, largest, coded):
    rows, features = values.shape
    largest = jnp.maximum(jnp.max(largest, axis=1, keepdims=True), 1e-30)
    exponent = jnp.floor(jnp.log2(32000.0 / largest))
    steps = values[...] * jnp.exp2(exponent)
    coded[:, :features] = jnp.round(steps).astype(jnp.int32).astype(jnp.int16)
    tail = jnp.broadcast_to(exponent, (rows, LANES))
    coded[:, features:] = tail.astype(jnp.int32).astype(jnp.int16)


def decode(coded, low, high):
    features = coded.shape[1] - LANES
    exponent = coded[low:high, features:].astype(jnp.int32).astype(F32)[:, :1]
    steps = coded[low:high, :features].astype(jnp.int32).astype(F32)
    return steps * (1.0 / jnp.exp2(exponent))


def bins_copy(bins, freqs, sem):
    return pltpu.make_async_copy(bins, freqs, sem)


def inner_kernel(slots, group, var_count, points, bins, x_hbm, inner, near, *refs):
    freqs, lhs, raw, bins_sem, sems = refs
    fetch = bins_copy(bins, freqs, bins_sem)
    fetch.start()
    me = lax.axis_index("blk")
    odd = lax.rem(me, 2)
    copies = load_copies(x_hbm, odd, near, sems)
    for copy in copies:
        copy.start()
    half_slots = slots // 2
    wide = half_slots * group
    first = jnp.where(odd == 1, 1, half_slots)
    fetch.wait()
    wanted = [first + i for i in range(half_slots)]
    rows = transform_rows(freqs, me, wanted, slots, group, (1 - odd) * HALF)
    for v, part in enumerate(spread(rows, var_count)):
        lhs[v * wide : (v + 1) * wide, :] = part
    most = jnp.zeros((wide, 2 * LANES), F32)
    for j in range(0, near.shape[0], 2):
        copies[j].wait()
        copies[j + 1].wait()
        got = mm(lhs[...], columns(near, j, var_count))
        for v in range(var_count):
            low = v * points + j * LANES
            mine = got[v * wide : (v + 1) * wide]
            most = jnp.maximum(most, jnp.abs(mine))
            raw[:, low : low + 2 * LANES] = mine
    encode(raw, most, inner)


def block_kernel(slots, keep, group, var_count, points, bins, x_hbm, near, *refs):
    outs, (freqs, lhs, far, raw, bins_sem, sems) = (refs[:-6], refs[-6:])
    fetch = bins_copy(bins, freqs, bins_sem)
    fetch.start()
    me = lax.axis_index("blk")
    odd = lax.rem(me, 2)
    copies = load_copies(x_hbm, 1 - odd, far, sems)
    for copy in copies:
        copy.start()
    half_slots = slots // 2
    outer = outs[0]
    even = outs[1 : 1 + slots]
    lead = outs[1 + slots : 1 + slots + half_slots]
    trail = outs[1 + slots + half_slots :]
    full = slots * group
    short = full + half_slots * group
    fetch.wait()
    rows = [
        transform_rows(freqs, me, range(slots), slots, group, start * HALF)
        for start in (odd, 1 - odd)
    ]
    for v, part in enumerate(spread(jnp.concatenate(rows, axis=0), var_count)):
        lhs[2 * v * full : 2 * (v + 1) * full, :] = part
    is_odd = odd == 1
    near_parts = []
    far_parts = []
    for v in range(var_count):
        base = 2 * v * full
        near_parts.append((base, full))
        for i, s in enumerate(keep):
            slot = jnp.where(is_odd, s, i)
            near_parts.append((pl.multiple_of(base + full + slot * group, group), group))
        far_parts.append((base + full, full))
        far_parts.append((base, full))

    def rows_of(parts):
        return jnp.concatenate([lhs[pl.ds(low, size), :] for low, size in parts], axis=0)

    most = jnp.zeros((half_slots * group, 2 * LANES), F32)
    for j in range(0, far.shape[0], 2):
        from_near = mm(rows_of(near_parts), columns(near, j, var_count))
        copies[j].wait()
        copies[j + 1].wait()
        from_far = mm(rows_of(far_parts), columns(far, j, var_count))
        for v in range(var_count):
            low = v * points + j * LANES
            high = low + 2 * LANES
            top = from_near[v * short : (v + 1) * short]
            bottom = from_far[2 * v * full : 2 * (v + 1) * full]
            whole = (top[:full] + bottom[:full]).astype(BF16)
            other = bottom[full:]
            for s in range(slots):
                even[s][:, low:high] = whole[s * group : (s + 1) * group]
            for i, s in enumerate(keep):
                mine = top[full + i * group : full + (i + 1) * group]
                begun = other[s * group : (s + 1) * group]
                ended = other[i * group : (i + 1) * group]
                lead[i][:, low:high] = jnp.where(is_odd, mine, begun)
                trail[i][:, low:high] = jnp.where(is_odd, ended, mine)
            sent = jnp.where(
                is_odd, other[half_slots * group :], other[group : (half_slots + 1) * group]
            )
            most = jnp.maximum(most, jnp.abs(sent))
            raw[:, low:high] = sent
    encode(raw, most, outer)


def inner_join_kernel(half_slots, group, *refs):
    lead = refs[:half_slots]
    trail = refs[half_slots : 2 * half_slots]
    inner = refs[2 * half_slots]
    joined = refs[2 * half_slots + 1 :]
    me = lax.axis_index("blk")
    odd = lax.rem(me, 2) == 1
    for i in range(half_slots):
        above = (i + half_slots - 1) % half_slots
        begun = lead[i][...] + decode(inner, above * group, (above + 1) * group)
        own = jnp.where(me == 0, 0.0, trail[i][...])
        ended = own + decode(inner, i * group, (i + 1) * group)
        joined[i][...] = jnp.where(odd, begun, ended).astype(BF16)


def outer_join_kernel(half_slots, group, *refs):
    lead = refs[:half_slots]
    trail = refs[half_slots : 2 * half_slots]
    outer = refs[2 * half_slots]
    joined = refs[2 * half_slots + 1 : 3 * half_slots + 1]
    outs = refs[3 * half_slots + 1 :]
    odd = lax.rem(lax.axis_index("blk"), 2) == 1
    for i in range(half_slots):
        above = (i + half_slots - 1) % half_slots
        begun = lead[i][...] + decode(outer, above * group, (above + 1) * group)
        ended = trail[i][...] + decode(outer, i * group, (i + 1) * group)
        other = jnp.where(odd, ended, begun).astype(BF16)
        outs[i][...] = jnp.where(odd, joined[i][...], other)
        outs[half_slots + i][...] = jnp.where(odd, other, joined[i][...])


def gram_kernel(slots, group, var_count, points, weights, classes, *refs):
    packed = refs[-1]
    blocks = 2 * slots
    me = lax.axis_index("blk")
    picked = jnp.zeros(classes.shape, F32)
    for k in range(weights.shape[0]):
        picked = picked + jnp.where(classes[...] == k, weights[k], jnp.float32(0.0))
    wide = jnp.concatenate([picked] * var_count, axis=1)
    left = jnp.concatenate([ref[...] for ref in refs[:-1]], axis=0)
    right = (left.astype(F32) * wide).astype(BF16)
    gram = lax.dot_general(
        left, right, (((1,), (1,)), ((), ())), preferred_element_type=F32
    )
    size = blocks * group
    freqs = group // 2
    same = rem(iota((size, size), 0), freqs) == rem(iota((1, size), 1), freqs)
    gram = jnp.where(same, gram, 0.0).reshape(blocks, 2, freqs, size)
    rows_re = gram[:, 0].reshape(blocks * freqs, size)
    rows_im = gram[:, 1].reshape(blocks * freqs, size)
    width = 2 * blocks * blocks
    row, lane = (iota((size, 1), 0), iota((1, width), 1))
    fits = block_of(div(row, group), me, slots) == rem(lane, blocks)
    row_part = rem(div(row, freqs), 2)
    lane_part = rem(div(lane, blocks), 2)
    from_re = one_hot(fits & (row_part == lane_part))
    sign = jnp.where(lane_part == 0, 1.0, -1.0)
    from_im = jnp.where(fits & (row_part != lane_part), sign, 0.0).astype(BF16)
    total = jnp.zeros((blocks * freqs, width), F32)
    for part_re, part_im in zip(split3(rows_re), split3(rows_im)):
        total = total + (mm(part_re, from_re) + mm(part_im, from_im))
    mine = div(iota((freqs, width), 1), 2 * blocks)
    out = jnp.zeros((freqs, width), F32)
    for b in range(blocks):
        block = block_of(jnp.int32(b), me, slots)
        out = out + jnp.where(mine == block, total[b * freqs : (b + 1) * freqs], 0.0)
    packed[...] = out


def mode_kernel(slots, var_count, points, scaling, feature_count, sums, *refs):
    csd, eig, modes = refs[-3:]
    tiles, refs = ([ref[...] for ref in refs[:sums]], refs[sums:])
    blocks = 2 * slots
    me = lax.axis_index("blk")
    spectra = [ref[...] for ref in refs[:-3]]
    raw = tiles[0] + tiles[1]
    if sums == 4:
        raw = raw + (tiles[2] + tiles[3])
    freqs, width = raw.shape
    group = 2 * freqs
    size = blocks * group
    mat = scaling * raw
    lane_part = rem(div(iota((freqs, width), 1), blocks), 2)
    is_re = lane_part == 0
    gather = one_hot(
        div(iota((width, width), 0), 2 * blocks) == rem(iota((1, width), 1), blocks)
    )

    def apply(matrix, vec_re, vec_im):
        top = matrix * jnp.where(is_re, vec_re, -vec_im)
        bottom = matrix * jnp.where(is_re, vec_im, vec_re)
        both = jnp.concatenate([top, bottom], axis=0)
        parts = jnp.concatenate([p.astype(F32) for p in split3(both)], axis=0).astype(BF16)
        got = mm(parts, gather)
        got = got[: 2 * freqs] + got[2 * freqs : 4 * freqs] + got[4 * freqs :]
        return (got[:freqs], got[freqs:])

    def over_blocks(x):
        return jnp.sum(x, axis=1, keepdims=True) * jnp.float32(1.0 / (2 * blocks))

    vec_re = jnp.full((freqs, width), 1.0 / math.sqrt(blocks), F32)
    vec_im = jnp.zeros((freqs, width), F32)
    for _ in range(ITERS):
        out_re, out_im = apply(mat, vec_re, vec_im)
        length = jnp.sqrt(over_blocks(out_re * out_re + out_im * out_im))
        vec_re, vec_im = (out_re / length, out_im / length)
    out_re, out_im = apply(mat, vec_re, vec_im)
    value = over_blocks(vec_re * out_re + vec_im * out_im)
    diagonal = iota((freqs, freqs), 0) == iota((freqs, freqs), 1)
    eig[...] = jnp.sum(
        jnp.where(diagonal, jnp.broadcast_to(value, (freqs, freqs)), 0.0), axis=0, keepdims=True
    )
    low_re = vec_re.astype(BF16)
    low_im = vec_im.astype(BF16)
    out_re, out_im = apply(raw, low_re.astype(F32), low_im.astype(F32))
    normsq = over_blocks(low_re.astype(F32) * out_re + low_im.astype(F32) * out_im)
    scale = jnp.sqrt(jnp.float32(feature_count) / normsq)
    lane = iota((1, size), 1)
    expand = one_hot(iota((width, size), 0) == block_of(div(lane, group), me, slots))
    wide = mm(jnp.concatenate([vec_re, vec_im], axis=0).astype(BF16), expand)
    wide_re, wide_im = (wide[:freqs], wide[freqs:])
    part = rem(div(lane, freqs), 2)
    mine = rem(lane, freqs) == iota((freqs, size), 0)
    coef_re = jnp.where(mine, jnp.where(part == 0, wide_re, -wide_im), 0.0)
    coef_im = jnp.where(mine, jnp.where(part == 0, wide_im, wide_re), 0.0)
    rows = 2 * var_count
    upper = iota((rows, size), 0) < var_count
    var = rem(iota((rows, size), 0), var_count)
    tall = []
    for f in range(freqs):
        both = jnp.where(
            upper,
            jnp.broadcast_to(coef_re[f : f + 1], (rows, size)),
            jnp.broadcast_to(coef_im[f : f + 1], (rows, size)),
        )
        tall.append(
            jnp.concatenate([jnp.where(var == v, both, 0.0) for v in range(var_count)], axis=1)
        )
    coef = jnp.concatenate(tall, axis=0).astype(BF16)
    stacked = jnp.concatenate(
        [
            piece[:, v * points : (v + 1) * points]
            for v in range(var_count)
            for piece in spectra
        ],
        axis=0,
    )
    phi = mm(coef, stacked)
    for f in range(freqs):
        block = phi[f * rows : (f + 1) * rows] * scale[f : f + 1, :]
        for k in range(2):
            modes[f, k] = block[k * var_count : (k + 1) * var_count]
    split_rows = jnp.concatenate(
        [
            jnp.where(
                div(iota((blocks, width), 1), 2 * blocks) == iota((blocks, width), 0),
                jnp.broadcast_to(mat[f : f + 1], (blocks, width)),
                0.0,
            )
            for f in range(freqs)
        ],
        axis=0,
    )
    for k in range(2):
        row, lane = (iota((width, blocks), 0), iota((width, blocks), 1))
        fold = one_hot(rem(row, 2 * blocks) == lane + k * blocks)
        got = jnp.zeros((freqs * blocks, blocks), F32)
        for piece in split3(split_rows):
            got = got + mm(piece, fold)
        for f in range(freqs):
            csd[f, k] = got[f * blocks : (f + 1) * blocks]


def call(kernel, outs, ins, inputs, scratch, flops, moved):
    vmem = pl.BlockSpec(memory_space=pltpu.VMEM)
    return pl.pallas_call(
        kernel,
        out_shape=outs,
        in_specs=ins,
        out_specs=jax.tree.map(lambda _: vmem, outs),
        scratch_shapes=scratch,
        compiler_params=pltpu.CompilerParams(vmem_limit_bytes=VMEM_LIMIT),
        cost_estimate=pl.CostEstimate(flops=flops, bytes_accessed=moved, transcendentals=0),
    )(*inputs)


def on_device(snapshots, freq_index, weight_class, class_weight):
    row_count, var_count, points = snapshots.shape
    features = var_count * points
    slots = lax.axis_size("blk")
    half_slots = slots // 2
    me = lax.axis_index("blk")
    freqs = freq_index.shape[0] // slots
    group = 2 * freqs
    blocks = 2 * slots
    vmem = pl.BlockSpec(memory_space=pltpu.VMEM)
    smem = pl.BlockSpec(memory_space=pltpu.SMEM)
    hbm = pl.BlockSpec(memory_space=pltpu.HBM)
    shape = jax.ShapeDtypeStruct

    wide = half_slots * group
    groups = points // LANES
    bins = pltpu.with_memory_space_constraint(freq_index, pltpu.HBM)
    bins_smem = pltpu.SMEM(freq_index.shape, jnp.int32)
    source = pltpu.with_memory_space_constraint(snapshots, pltpu.HBM)
    half_block = (groups, HALF, var_count, LANES)
    payload = shape((wide, features + LANES), jnp.int16)
    width = HALF * var_count
    sems = [pltpu.SemaphoreType.DMA, pltpu.SemaphoreType.DMA((groups,))]
    raw = pltpu.VMEM((wide, features), F32)
    inner, near = call(
        functools.partial(inner_kernel, slots, group, var_count, points),
        [payload, shape(half_block, BF16)],
        [hbm, hbm],
        (bins, source),
        [bins_smem, pltpu.VMEM((wide * var_count, width), BF16), raw, *sems],
        2 * wide * features * width,
        row_count * features,
    )

    def swap(x, first, also):
        pairs = [(i, i + 1) for i in range(first, slots - 1, 2)]
        return lax.ppermute(x, "blk", pairs + [(b, a) for a, b in pairs] + also)

    keep = [0] + list(range(half_slots + 1, slots))
    piece = shape((group, features), BF16)
    wide_piece = shape((group, features), F32)
    outer, *pieces = call(
        functools.partial(block_kernel, slots, keep, group, var_count, points),
        [payload] + [piece] * slots + [wide_piece] * (2 * half_slots),
        [hbm, hbm, vmem],
        (bins, source, near),
        [
            bins_smem,
            pltpu.VMEM((2 * slots * group * var_count, width), BF16),
            pltpu.VMEM(half_block, BF16),
            raw,
            *sems,
        ],
        2 * 4 * slots * group * features * width,
        row_count * features,
    )
    from_outer = swap(outer, 0, [])
    from_inner = swap(inner, 1, [(slots - 1, 0)])

    def shift(x, s):
        return lax.ppermute(x, "blk", [(i, (i + s) % slots) for i in range(slots)])

    even = [pieces[0]] + [shift(pieces[s], s) for s in range(1, slots)]
    halves = pieces[slots:]
    joined = call(
        functools.partial(inner_join_kernel, half_slots, group),
        [piece] * half_slots,
        [vmem] * (slots + 1),
        (*halves, from_inner),
        [],
        slots * group * features,
        10 * slots * group * features,
    )
    odd = call(
        functools.partial(outer_join_kernel, half_slots, group),
        [piece] * slots,
        [vmem] * (slots + half_slots + 1),
        (*halves, from_outer, *joined),
        [],
        slots * group * features,
        10 * slots * group * features,
    )
    above = [odd[0]] + [shift(odd[i], s) for i, s in enumerate(keep) if i]
    under = [odd[half_slots]] + [shift(odd[half_slots + i], i) for i in range(1, half_slots)]
    tile = 2 * blocks * blocks
    spectra = (*even, *above, *under)
    packed = call(
        functools.partial(gram_kernel, slots, group, var_count, points),
        shape((freqs, tile), F32),
        [smem, vmem] + [vmem] * len(spectra),
        (class_weight, weight_class.reshape(1, points), *spectra),
        [],
        2 * (blocks * group) ** 2 * features,
        4 * blocks * group * features,
    )
    devices = lax.axis_size("pts")
    def from_peer(x, step):
        return lax.ppermute(x, "pts", [(i, i ^ step) for i in range(devices)])

    parts = [packed]
    step = 1
    while step < devices:
        total = functools.reduce(jnp.add, parts[:2])
        if len(parts) == 4:
            total = total + (parts[2] + parts[3])
        by_four = step > 1 and 4 * step <= devices
        steps = (step, 2 * step, 3 * step) if by_four else (step,)
        parts = [total] + [from_peer(total, i) for i in steps]
        step *= 4 if by_four else 2
    total_features = features * devices
    csd, eigval, modes = call(
        functools.partial(
            mode_kernel,
            slots,
            var_count,
            points,
            1.0 / (total_features * (3.0 * NFFT / 8.0)),
            total_features,
            len(parts),
        ),
        [
            shape((freqs, 2, blocks, blocks), F32),
            shape((1, freqs), F32),
            shape((freqs, 2, var_count, points), F32),
        ],
        [vmem] * (len(parts) + len(spectra)),
        (*parts, *spectra),
        [],
        2 * 2 * blocks * group * group * features,
        2 * blocks * group * features,
    )
    return (csd, eigval.reshape(freqs), modes)


def solution(mesh):
    in_specs = (P("blk", None, "pts"), P(), P("pts"), P())
    out_specs = (P("blk", None, None, None), P("blk"), P("blk", None, None, "pts"))
    return jax.shard_map(
        on_device, mesh=mesh, in_specs=in_specs, out_specs=out_specs, check_vma=False
    )
```

```python
import functools
import math

import jax
import jax.numpy as jnp
from jax import lax
from jax.experimental import pallas as pl
from jax.experimental.pallas import tpu as pltpu
from jax.sharding import PartitionSpec as P

NFFT = 768
HALF = NFFT // 2
ITERS = 3
LANES = 128
VMEM_LIMIT = 32 * 1024 * 1024
F32 = jnp.float32
BF16 = jnp.bfloat16


def iota(shape, axis):
    return lax.broadcasted_iota(jnp.int32, shape, axis)


def div(x, n):
    return x >> (n.bit_length() - 1) if n & (n - 1) == 0 else x // n


def rem(x, n):
    return x & (n - 1) if n & (n - 1) == 0 else x % n


def mm(a, b):
    return jnp.dot(a, b, preferred_element_type=F32)


def split3(x):
    high = x.astype(BF16)
    rest = x - high.astype(F32)
    mid = rest.astype(BF16)
    low = (rest - mid.astype(F32)).astype(BF16)
    return (high, mid, low)


def one_hot(condition):
    return jnp.where(condition, 1.0, 0.0).astype(BF16)


def modulo(x, n):
    return jnp.where(x < 0, x + n, x)


def block_of(slot, me, slots):
    half_slots = slots // 2
    above = slot - slots
    below = above - half_slots
    even = 2 * modulo(me - slot, slots)
    upper = 2 * modulo(me - jnp.where(above == 0, 0, above + half_slots), slots) + 1
    lower = modulo(2 * modulo(me - below, slots) - 1, 2 * slots)
    return jnp.where(slot < slots, even, jnp.where(below < 0, upper, lower))


def trig(phase):
    quarter = ((phase + NFFT // 8) * 1366) >> 18
    angle = (2.0 * math.pi / NFFT) * (phase - (NFFT // 4) * quarter).astype(F32)
    x = angle * angle
    cos = 1.0 + x * (-1.0 / 2 + x * (1.0 / 24 + x * (-1.0 / 720 + x * (1.0 / 40320))))
    sin = 1.0 + x * (-1.0 / 6 + x * (1.0 / 120 + x * (-1.0 / 5040 + x * (1.0 / 362880))))
    sin = angle * sin
    odd = (quarter & 1) != 0
    real_part = jnp.where(odd, sin, cos)
    imag_part = jnp.where(odd, cos, sin)
    real_part = jnp.where(((quarter + 1) & 2) != 0, -real_part, real_part)
    imag_part = jnp.where((quarter & 2) != 0, -imag_part, imag_part)
    return (real_part, imag_part)


def transform_rows(freqs, me, wanted, slots, group, start):
    count = group // 2
    times = start + iota((count, HALF), 1)
    window = 0.5 - 0.5 * trig(times)[0]
    row = iota((count, HALF), 0)
    out = []
    for s in wanted:
        owner = lax.rem(me + s, slots)
        freq = jnp.zeros((count, HALF), jnp.int32)
        for f in range(count):
            freq = jnp.where(row == f, freqs[owner * count + f], freq)
        product = freq * times
        turns = ((product >> 8) * 21846) >> 16
        real_part, imag_part = trig(product - NFFT * turns)
        out.append(window * real_part)
        out.append(-window * imag_part)
    return jnp.concatenate(out, axis=0).astype(BF16)


def spread(rows, var_count):
    lane = iota((1, LANES * var_count), 1)
    pick = one_hot(div(lane, var_count) == iota((LANES, LANES * var_count), 0))
    pieces = [mm(rows[:, t : t + LANES], pick) for t in range(0, HALF, LANES)]
    wide = jnp.concatenate(pieces, axis=1)
    owner = rem(iota((1, HALF * var_count), 1), var_count)
    return [jnp.where(owner == v, wide, 0.0).astype(BF16) for v in range(var_count)]


def columns(held, j, var_count):
    rows = HALF * var_count
    parts = [held.at[j + i].reshape(rows, LANES)[...] for i in range(2)]
    return jnp.concatenate(parts, axis=1)


def load_copies(x_hbm, half, held, sems):
    rows = pl.ds(half * HALF, HALF)
    return [
        pltpu.make_async_copy(x_hbm.at[rows, :, pl.ds(j * LANES, LANES)], held.at[j], sems.at[j])
        for j in range(held.shape[0])
    ]


def encode(values, largest, coded):
    rows, features = values.shape
    largest = jnp.maximum(jnp.max(largest, axis=1, keepdims=True), 1e-30)
    exponent = jnp.floor(jnp.log2(32000.0 / largest))
    steps = values[...] * jnp.exp2(exponent)
    coded[:, :features] = jnp.round(steps).astype(jnp.int32).astype(jnp.int16)
    tail = jnp.broadcast_to(exponent, (rows, LANES))
    coded[:, features:] = tail.astype(jnp.int32).astype(jnp.int16)


def decode(coded, low, high):
    features = coded.shape[1] - LANES
    exponent = coded[low:high, features:].astype(jnp.int32).astype(F32)[:, :1]
    steps = coded[low:high, :features].astype(jnp.int32).astype(F32)
    return steps * (1.0 / jnp.exp2(exponent))


def bins_copy(bins, freqs, sem):
    return pltpu.make_async_copy(bins, freqs, sem)


def inner_kernel(slots, group, var_count, points, bins, x_hbm, inner, near, *refs):
    freqs, lhs, raw, bins_sem, sems = refs
    fetch = bins_copy(bins, freqs, bins_sem)
    fetch.start()
    me = lax.axis_index("blk")
    odd = lax.rem(me, 2)
    copies = load_copies(x_hbm, odd, near, sems)
    for copy in copies:
        copy.start()
    half_slots = slots // 2
    wide = half_slots * group
    first = jnp.where(odd == 1, 1, half_slots)
    fetch.wait()
    wanted = [first + i for i in range(half_slots)]
    rows = transform_rows(freqs, me, wanted, slots, group, (1 - odd) * HALF)
    for v, part in enumerate(spread(rows, var_count)):
        lhs[v * wide : (v + 1) * wide, :] = part
    most = jnp.zeros((wide, 2 * LANES), F32)
    for j in range(0, near.shape[0], 2):
        copies[j].wait()
        copies[j + 1].wait()
        got = mm(lhs[...], columns(near, j, var_count))
        for v in range(var_count):
            low = v * points + j * LANES
            mine = got[v * wide : (v + 1) * wide]
            most = jnp.maximum(most, jnp.abs(mine))
            raw[:, low : low + 2 * LANES] = mine
    encode(raw, most, inner)


def block_kernel(slots, keep, group, var_count, points, bins, x_hbm, near, *refs):
    outs, (freqs, lhs, far, raw, bins_sem, sems) = (refs[:-6], refs[-6:])
    fetch = bins_copy(bins, freqs, bins_sem)
    fetch.start()
    me = lax.axis_index("blk")
    odd = lax.rem(me, 2)
    copies = load_copies(x_hbm, 1 - odd, far, sems)
    for copy in copies:
        copy.start()
    half_slots = slots // 2
    outer = outs[0]
    even = outs[1 : 1 + slots]
    lead = outs[1 + slots : 1 + slots + half_slots]
    trail = outs[1 + slots + half_slots :]
    full = slots * group
    short = full + half_slots * group
    fetch.wait()
    rows = [
        transform_rows(freqs, me, range(slots), slots, group, start * HALF)
        for start in (odd, 1 - odd)
    ]
    for v, part in enumerate(spread(jnp.concatenate(rows, axis=0), var_count)):
        lhs[2 * v * full : 2 * (v + 1) * full, :] = part
    is_odd = odd == 1
    near_parts = []
    far_parts = []
    for v in range(var_count):
        base = 2 * v * full
        near_parts.append((base, full))
        for i, s in enumerate(keep):
            slot = jnp.where(is_odd, s, i)
            near_parts.append((pl.multiple_of(base + full + slot * group, group), group))
        far_parts.append((base + full, full))
        far_parts.append((base, full))

    def rows_of(parts):
        return jnp.concatenate([lhs[pl.ds(low, size), :] for low, size in parts], axis=0)

    most = jnp.zeros((half_slots * group, 2 * LANES), F32)
    for j in range(0, far.shape[0], 2):
        from_near = mm(rows_of(near_parts), columns(near, j, var_count))
        copies[j].wait()
        copies[j + 1].wait()
        from_far = mm(rows_of(far_parts), columns(far, j, var_count))
        for v in range(var_count):
            low = v * points + j * LANES
            high = low + 2 * LANES
            top = from_near[v * short : (v + 1) * short]
            bottom = from_far[2 * v * full : 2 * (v + 1) * full]
            whole = (top[:full] + bottom[:full]).astype(BF16)
            other = bottom[full:]
            for s in range(slots):
                even[s][:, low:high] = whole[s * group : (s + 1) * group]
            for i, s in enumerate(keep):
                mine = top[full + i * group : full + (i + 1) * group]
                begun = other[s * group : (s + 1) * group]
                ended = other[i * group : (i + 1) * group]
                lead[i][:, low:high] = jnp.where(is_odd, mine, begun)
                trail[i][:, low:high] = jnp.where(is_odd, ended, mine)
            sent = jnp.where(
                is_odd, other[half_slots * group :], other[group : (half_slots + 1) * group]
            )
            most = jnp.maximum(most, jnp.abs(sent))
            raw[:, low:high] = sent
    encode(raw, most, outer)


def inner_join_kernel(half_slots, group, *refs):
    lead = refs[:half_slots]
    trail = refs[half_slots : 2 * half_slots]
    inner = refs[2 * half_slots]
    later = 2 * half_slots - 2
    held_back = refs[2 * half_slots + 1 : 2 * half_slots + 1 + later]
    joined = refs[2 * half_slots + 1 + later :]
    for source, target in zip(held_back, joined[half_slots:]):
        target[...] = source[...]
    me = lax.axis_index("blk")
    odd = lax.rem(me, 2) == 1
    for i in range(half_slots):
        above = (i + half_slots - 1) % half_slots
        begun = lead[i][...] + decode(inner, above * group, (above + 1) * group)
        own = jnp.where(me == 0, 0.0, trail[i][...])
        ended = own + decode(inner, i * group, (i + 1) * group)
        joined[i][...] = jnp.where(odd, begun, ended).astype(BF16)


def outer_join_kernel(half_slots, group, *refs):
    lead = refs[:half_slots]
    trail = refs[half_slots : 2 * half_slots]
    outer = refs[2 * half_slots]
    joined = refs[2 * half_slots + 1 : 3 * half_slots + 1]
    outs = refs[3 * half_slots + 1 :]
    odd = lax.rem(lax.axis_index("blk"), 2) == 1
    for i in range(half_slots):
        above = (i + half_slots - 1) % half_slots
        begun = lead[i][...] + decode(outer, above * group, (above + 1) * group)
        ended = trail[i][...] + decode(outer, i * group, (i + 1) * group)
        other = jnp.where(odd, ended, begun).astype(BF16)
        outs[i][...] = jnp.where(odd, joined[i][...], other)
        outs[half_slots + i][...] = jnp.where(odd, other, joined[i][...])


def gram_kernel(slots, group, var_count, points, weights, classes, *refs):
    packed = refs[-1]
    blocks = 2 * slots
    me = lax.axis_index("blk")
    picked = jnp.zeros(classes.shape, F32)
    for k in range(weights.shape[0]):
        picked = picked + jnp.where(classes[...] == k, weights[k], jnp.float32(0.0))
    wide = jnp.concatenate([picked] * var_count, axis=1)
    left = jnp.concatenate([ref[...] for ref in refs[:-1]], axis=0)
    right = (left.astype(F32) * wide).astype(BF16)
    gram = lax.dot_general(
        left, right, (((1,), (1,)), ((), ())), preferred_element_type=F32
    )
    size = blocks * group
    freqs = group // 2
    same = rem(iota((size, size), 0), freqs) == rem(iota((1, size), 1), freqs)
    gram = jnp.where(same, gram, 0.0).reshape(blocks, 2, freqs, size)
    rows_re = gram[:, 0].reshape(blocks * freqs, size)
    rows_im = gram[:, 1].reshape(blocks * freqs, size)
    width = 2 * blocks * blocks
    row, lane = (iota((size, 1), 0), iota((1, width), 1))
    fits = block_of(div(row, group), me, slots) == rem(lane, blocks)
    row_part = rem(div(row, freqs), 2)
    lane_part = rem(div(lane, blocks), 2)
    from_re = one_hot(fits & (row_part == lane_part))
    sign = jnp.where(lane_part == 0, 1.0, -1.0)
    from_im = jnp.where(fits & (row_part != lane_part), sign, 0.0).astype(BF16)
    total = jnp.zeros((blocks * freqs, width), F32)
    for part_re, part_im in zip(split3(rows_re), split3(rows_im)):
        total = total + (mm(part_re, from_re) + mm(part_im, from_im))
    mine = div(iota((freqs, width), 1), 2 * blocks)
    out = jnp.zeros((freqs, width), F32)
    for b in range(blocks):
        block = block_of(jnp.int32(b), me, slots)
        out = out + jnp.where(mine == block, total[b * freqs : (b + 1) * freqs], 0.0)
    packed[...] = out


def mode_kernel(slots, var_count, points, scaling, feature_count, sums, *refs):
    csd, eig, modes = refs[-3:]
    tiles, refs = ([ref[...] for ref in refs[:sums]], refs[sums:])
    blocks = 2 * slots
    me = lax.axis_index("blk")
    spectra = [ref[...] for ref in refs[:-3]]
    raw = tiles[0] + tiles[1]
    if sums == 4:
        raw = raw + (tiles[2] + tiles[3])
    freqs, width = raw.shape
    group = 2 * freqs
    size = blocks * group
    mat = scaling * raw
    lane_part = rem(div(iota((freqs, width), 1), blocks), 2)
    is_re = lane_part == 0
    gather = one_hot(
        div(iota((width, width), 0), 2 * blocks) == rem(iota((1, width), 1), blocks)
    )

    def apply(matrix, vec_re, vec_im):
        top = matrix * jnp.where(is_re, vec_re, -vec_im)
        bottom = matrix * jnp.where(is_re, vec_im, vec_re)
        both = jnp.concatenate([top, bottom], axis=0)
        parts = jnp.concatenate([p.astype(F32) for p in split3(both)], axis=0).astype(BF16)
        got = mm(parts, gather)
        got = got[: 2 * freqs] + got[2 * freqs : 4 * freqs] + got[4 * freqs :]
        return (got[:freqs], got[freqs:])

    def over_blocks(x):
        return jnp.sum(x, axis=1, keepdims=True) * jnp.float32(1.0 / (2 * blocks))

    vec_re = jnp.full((freqs, width), 1.0 / math.sqrt(blocks), F32)
    vec_im = jnp.zeros((freqs, width), F32)
    for _ in range(ITERS):
        out_re, out_im = apply(mat, vec_re, vec_im)
        length = jnp.sqrt(over_blocks(out_re * out_re + out_im * out_im))
        vec_re, vec_im = (out_re / length, out_im / length)
    out_re, out_im = apply(mat, vec_re, vec_im)
    value = over_blocks(vec_re * out_re + vec_im * out_im)
    diagonal = iota((freqs, freqs), 0) == iota((freqs, freqs), 1)
    eig[...] = jnp.sum(
        jnp.where(diagonal, jnp.broadcast_to(value, (freqs, freqs)), 0.0), axis=0, keepdims=True
    )
    low_re = vec_re.astype(BF16)
    low_im = vec_im.astype(BF16)
    out_re, out_im = apply(raw, low_re.astype(F32), low_im.astype(F32))
    normsq = over_blocks(low_re.astype(F32) * out_re + low_im.astype(F32) * out_im)
    scale = jnp.sqrt(jnp.float32(feature_count) / normsq)
    lane = iota((1, size), 1)
    expand = one_hot(iota((width, size), 0) == block_of(div(lane, group), me, slots))
    wide = mm(jnp.concatenate([vec_re, vec_im], axis=0).astype(BF16), expand)
    wide_re, wide_im = (wide[:freqs], wide[freqs:])
    part = rem(div(lane, freqs), 2)
    mine = rem(lane, freqs) == iota((freqs, size), 0)
    coef_re = jnp.where(mine, jnp.where(part == 0, wide_re, -wide_im), 0.0)
    coef_im = jnp.where(mine, jnp.where(part == 0, wide_im, wide_re), 0.0)
    rows = 2 * var_count
    upper = iota((rows, size), 0) < var_count
    var = rem(iota((rows, size), 0), var_count)
    tall = []
    for f in range(freqs):
        both = jnp.where(
            upper,
            jnp.broadcast_to(coef_re[f : f + 1], (rows, size)),
            jnp.broadcast_to(coef_im[f : f + 1], (rows, size)),
        )
        tall.append(
            jnp.concatenate([jnp.where(var == v, both, 0.0) for v in range(var_count)], axis=1)
        )
    coef = jnp.concatenate(tall, axis=0).astype(BF16)
    stacked = jnp.concatenate(
        [
            piece[:, v * points : (v + 1) * points]
            for v in range(var_count)
            for piece in spectra
        ],
        axis=0,
    )
    phi = mm(coef, stacked)
    for f in range(freqs):
        block = phi[f * rows : (f + 1) * rows] * scale[f : f + 1, :]
        for k in range(2):
            modes[f, k] = block[k * var_count : (k + 1) * var_count]
    split_rows = jnp.concatenate(
        [
            jnp.where(
                div(iota((blocks, width), 1), 2 * blocks) == iota((blocks, width), 0),
                jnp.broadcast_to(mat[f : f + 1], (blocks, width)),
                0.0,
            )
            for f in range(freqs)
        ],
        axis=0,
    )
    for k in range(2):
        row, lane = (iota((width, blocks), 0), iota((width, blocks), 1))
        fold = one_hot(rem(row, 2 * blocks) == lane + k * blocks)
        got = jnp.zeros((freqs * blocks, blocks), F32)
        for piece in split3(split_rows):
            got = got + mm(piece, fold)
        for f in range(freqs):
            csd[f, k] = got[f * blocks : (f + 1) * blocks]


def call(kernel, outs, ins, inputs, scratch, flops, moved):
    vmem = pl.BlockSpec(memory_space=pltpu.VMEM)
    return pl.pallas_call(
        kernel,
        out_shape=outs,
        in_specs=ins,
        out_specs=jax.tree.map(lambda _: vmem, outs),
        scratch_shapes=scratch,
        compiler_params=pltpu.CompilerParams(vmem_limit_bytes=VMEM_LIMIT),
        cost_estimate=pl.CostEstimate(flops=flops, bytes_accessed=moved, transcendentals=0),
    )(*inputs)


def on_device(snapshots, freq_index, weight_class, class_weight):
    row_count, var_count, points = snapshots.shape
    features = var_count * points
    slots = lax.axis_size("blk")
    half_slots = slots // 2
    me = lax.axis_index("blk")
    freqs = freq_index.shape[0] // slots
    group = 2 * freqs
    blocks = 2 * slots
    vmem = pl.BlockSpec(memory_space=pltpu.VMEM)
    smem = pl.BlockSpec(memory_space=pltpu.SMEM)
    hbm = pl.BlockSpec(memory_space=pltpu.HBM)
    shape = jax.ShapeDtypeStruct

    wide = half_slots * group
    groups = points // LANES
    bins = pltpu.with_memory_space_constraint(freq_index, pltpu.HBM)
    bins_smem = pltpu.SMEM(freq_index.shape, jnp.int32)
    source = pltpu.with_memory_space_constraint(snapshots, pltpu.HBM)
    half_block = (groups, HALF, var_count, LANES)
    payload = shape((wide, features + LANES), jnp.int16)
    width = HALF * var_count
    sems = [pltpu.SemaphoreType.DMA, pltpu.SemaphoreType.DMA((groups,))]
    raw = pltpu.VMEM((wide, features), F32)
    inner, near = call(
        functools.partial(inner_kernel, slots, group, var_count, points),
        [payload, shape(half_block, BF16)],
        [hbm, hbm],
        (bins, source),
        [bins_smem, pltpu.VMEM((wide * var_count, width), BF16), raw, *sems],
        2 * wide * features * width,
        row_count * features,
    )

    def swap(x, first, also):
        pairs = [(i, i + 1) for i in range(first, slots - 1, 2)]
        return lax.ppermute(x, "blk", pairs + [(b, a) for a, b in pairs] + also)

    keep = [0] + list(range(half_slots + 1, slots))
    piece = shape((group, features), BF16)
    wide_piece = shape((group, features), F32)
    outer, *pieces = call(
        functools.partial(block_kernel, slots, keep, group, var_count, points),
        [payload] + [piece] * slots + [wide_piece] * (2 * half_slots),
        [hbm, hbm, vmem],
        (bins, source, near),
        [
            bins_smem,
            pltpu.VMEM((2 * slots * group * var_count, width), BF16),
            pltpu.VMEM(half_block, BF16),
            raw,
            *sems,
        ],
        2 * 4 * slots * group * features * width,
        row_count * features,
    )
    from_outer = swap(outer, 0, [])
    from_inner = swap(inner, 1, [(slots - 1, 0)])

    def shift(x, s):
        return lax.ppermute(x, "blk", [(i, (i + s) % slots) for i in range(slots)])

    later = [s for s in range(1, slots) if s != half_slots]
    halves = pieces[slots:]
    joined = call(
        functools.partial(inner_join_kernel, half_slots, group),
        [piece] * (half_slots + len(later)),
        [vmem] * (slots + 1 + len(later)),
        (*halves, from_inner, *[pieces[s] for s in later]),
        [],
        slots * group * features,
        10 * slots * group * features,
    )
    even = {s: shift(x, s) for s, x in zip(later, joined[half_slots:])}
    even = [
        pieces[0] if s == 0 else shift(pieces[s], s) if s == half_slots else even[s]
        for s in range(slots)
    ]
    odd = call(
        functools.partial(outer_join_kernel, half_slots, group),
        [piece] * slots,
        [vmem] * (slots + half_slots + 1),
        (*halves, from_outer, *joined[:half_slots]),
        [],
        slots * group * features,
        10 * slots * group * features,
    )
    above = [odd[0]] + [shift(odd[i], s) for i, s in enumerate(keep) if i]
    under = [odd[half_slots]] + [shift(odd[half_slots + i], i) for i in range(1, half_slots)]
    tile = 2 * blocks * blocks
    spectra = (*even, *above, *under)
    packed = call(
        functools.partial(gram_kernel, slots, group, var_count, points),
        shape((freqs, tile), F32),
        [smem, vmem] + [vmem] * len(spectra),
        (class_weight, weight_class.reshape(1, points), *spectra),
        [],
        2 * (blocks * group) ** 2 * features,
        4 * blocks * group * features,
    )
    devices = lax.axis_size("pts")
    def from_peer(x, step):
        return lax.ppermute(x, "pts", [(i, i ^ step) for i in range(devices)])

    parts = [packed]
    step = 1
    while step < devices:
        total = functools.reduce(jnp.add, parts[:2])
        if len(parts) == 4:
            total = total + (parts[2] + parts[3])
        by_four = step > 1 and 4 * step <= devices
        steps = (step, 2 * step, 3 * step) if by_four else (step,)
        parts = [total] + [from_peer(total, i) for i in steps]
        step *= 4 if by_four else 2
    total_features = features * devices
    csd, eigval, modes = call(
        functools.partial(
            mode_kernel,
            slots,
            var_count,
            points,
            1.0 / (total_features * (3.0 * NFFT / 8.0)),
            total_features,
            len(parts),
        ),
        [
            shape((freqs, 2, blocks, blocks), F32),
            shape((1, freqs), F32),
            shape((freqs, 2, var_count, points), F32),
        ],
        [vmem] * (len(parts) + len(spectra)),
        (*parts, *spectra),
        [],
        2 * 2 * blocks * group * group * features,
        2 * blocks * group * features,
    )
    return (csd, eigval.reshape(freqs), modes)


def solution(mesh):
    in_specs = (P("blk", None, "pts"), P(), P("pts"), P())
    out_specs = (P("blk", None, None, None), P("blk"), P("blk", None, None, "pts"))
    return jax.shard_map(
        on_device, mesh=mesh, in_specs=in_specs, out_specs=out_specs, check_vma=False
    )
```

```python
import functools
import math

import jax
import jax.numpy as jnp
from jax import lax
from jax.experimental import pallas as pl
from jax.experimental.pallas import tpu as pltpu
from jax.sharding import PartitionSpec as P

NFFT = 768
HALF = NFFT // 2
ITERS = 3
LANES = 128
VMEM_LIMIT = 32 * 1024 * 1024
F32 = jnp.float32
BF16 = jnp.bfloat16


def iota(shape, axis):
    return lax.broadcasted_iota(jnp.int32, shape, axis)


def div(x, n):
    return x >> (n.bit_length() - 1) if n & (n - 1) == 0 else x // n


def rem(x, n):
    return x & (n - 1) if n & (n - 1) == 0 else x % n


def mm(a, b):
    return jnp.dot(a, b, preferred_element_type=F32)


def split3(x):
    high = x.astype(BF16)
    rest = x - high.astype(F32)
    mid = rest.astype(BF16)
    low = (rest - mid.astype(F32)).astype(BF16)
    return (high, mid, low)


def sum_thirds(x):
    rows = x.shape[0] // 3
    return x[:rows] + (x[rows : 2 * rows] + x[2 * rows :])


def one_hot(condition):
    return jnp.where(condition, 1.0, 0.0).astype(BF16)


def modulo(x, n):
    return jnp.where(x < 0, x + n, x)


def block_of(slot, me, slots):
    half_slots = slots // 2
    above = slot - slots
    below = above - half_slots
    even = 2 * modulo(me - slot, slots)
    upper = 2 * modulo(me - jnp.where(above == 0, 0, above + half_slots), slots) + 1
    lower = modulo(2 * modulo(me - below, slots) - 1, 2 * slots)
    return jnp.where(slot < slots, even, jnp.where(below < 0, upper, lower))


def trig(phase):
    quarter = ((phase + NFFT // 8) * 1366) >> 18
    angle = (2.0 * math.pi / NFFT) * (phase - (NFFT // 4) * quarter).astype(F32)
    x = angle * angle
    cos = 1.0 + x * (-1.0 / 2 + x * (1.0 / 24 + x * (-1.0 / 720 + x * (1.0 / 40320))))
    sin = 1.0 + x * (-1.0 / 6 + x * (1.0 / 120 + x * (-1.0 / 5040 + x * (1.0 / 362880))))
    sin = angle * sin
    odd = (quarter & 1) != 0
    real_part = jnp.where(odd, sin, cos)
    imag_part = jnp.where(odd, cos, sin)
    real_part = jnp.where(((quarter + 1) & 2) != 0, -real_part, real_part)
    imag_part = jnp.where((quarter & 2) != 0, -imag_part, imag_part)
    return (real_part, imag_part)


def transform_rows(freqs, me, wanted, slots, group, start):
    count = group // 2
    times = start + iota((count, HALF), 1)
    window = 0.5 - 0.5 * trig(times)[0]
    row = iota((count, HALF), 0)
    out = []
    for s in wanted:
        owner = lax.rem(me + s, slots)
        freq = jnp.zeros((count, HALF), jnp.int32)
        for f in range(count):
            freq = jnp.where(row == f, freqs[owner * count + f], freq)
        product = freq * times
        turns = ((product >> 8) * 21846) >> 16
        real_part, imag_part = trig(product - NFFT * turns)
        out.append(window * real_part)
        out.append(-window * imag_part)
    return jnp.concatenate(out, axis=0).astype(BF16)


def spread(rows, var_count):
    lane = iota((1, LANES * var_count), 1)
    pick = one_hot(div(lane, var_count) == iota((LANES, LANES * var_count), 0))
    pieces = [mm(rows[:, t : t + LANES], pick) for t in range(0, HALF, LANES)]
    wide = jnp.concatenate(pieces, axis=1)
    owner = rem(iota((1, HALF * var_count), 1), var_count)
    return [jnp.where(owner == v, wide, 0.0).astype(BF16) for v in range(var_count)]


def columns(held, j, var_count):
    rows = HALF * var_count
    parts = [held.at[j + i].reshape(rows, LANES)[...] for i in range(2)]
    return jnp.concatenate(parts, axis=1)


def load_copies(x_hbm, half, held, sems):
    rows = pl.ds(half * HALF, HALF)
    return [
        pltpu.make_async_copy(x_hbm.at[rows, :, pl.ds(j * LANES, LANES)], held.at[j], sems.at[j])
        for j in range(held.shape[0])
    ]


def encode(values, largest, coded):
    rows, features = values.shape
    largest = jnp.maximum(jnp.max(largest, axis=1, keepdims=True), 1e-30)
    exponent = jnp.floor(jnp.log2(32000.0 / largest))
    steps = values[...] * jnp.exp2(exponent)
    coded[:, :features] = jnp.round(steps).astype(jnp.int32).astype(jnp.int16)
    tail = jnp.broadcast_to(exponent, (rows, LANES))
    coded[:, features:] = tail.astype(jnp.int32).astype(jnp.int16)


def decode(coded, low, high):
    features = coded.shape[1] - LANES
    exponent = coded[low:high, features:].astype(jnp.int32).astype(F32)[:, :1]
    steps = coded[low:high, :features].astype(jnp.int32).astype(F32)
    return steps * (1.0 / jnp.exp2(exponent))


def bins_copy(bins, freqs, sem):
    return pltpu.make_async_copy(bins, freqs, sem)


def inner_kernel(slots, group, var_count, points, bins, x_hbm, inner, near, *refs):
    freqs, lhs, raw, bins_sem, sems = refs
    fetch = bins_copy(bins, freqs, bins_sem)
    fetch.start()
    me = lax.axis_index("blk")
    odd = lax.rem(me, 2)
    copies = load_copies(x_hbm, odd, near, sems)
    for copy in copies:
        copy.start()
    half_slots = slots // 2
    wide = half_slots * group
    first = jnp.where(odd == 1, 1, half_slots)
    fetch.wait()
    wanted = [first + i for i in range(half_slots)]
    rows = transform_rows(freqs, me, wanted, slots, group, (1 - odd) * HALF)
    for v, part in enumerate(spread(rows, var_count)):
        lhs[v * wide : (v + 1) * wide, :] = part
    most = jnp.zeros((wide, 2 * LANES), F32)
    for j in range(0, near.shape[0], 2):
        copies[j].wait()
        copies[j + 1].wait()
        got = mm(lhs[...], columns(near, j, var_count))
        for v in range(var_count):
            low = v * points + j * LANES
            mine = got[v * wide : (v + 1) * wide]
            most = jnp.maximum(most, jnp.abs(mine))
            raw[:, low : low + 2 * LANES] = mine
    encode(raw, most, inner)


def block_kernel(slots, keep, group, var_count, points, bins, x_hbm, near, *refs):
    outs, (freqs, lhs, far, raw, bins_sem, sems) = (refs[:-6], refs[-6:])
    fetch = bins_copy(bins, freqs, bins_sem)
    fetch.start()
    me = lax.axis_index("blk")
    odd = lax.rem(me, 2)
    copies = load_copies(x_hbm, 1 - odd, far, sems)
    for copy in copies:
        copy.start()
    half_slots = slots // 2
    outer = outs[0]
    even = outs[1 : 1 + slots]
    lead = outs[1 + slots : 1 + slots + half_slots]
    trail = outs[1 + slots + half_slots :]
    full = slots * group
    short = full + half_slots * group
    fetch.wait()
    rows = [
        transform_rows(freqs, me, range(slots), slots, group, start * HALF)
        for start in (odd, 1 - odd)
    ]
    for v, part in enumerate(spread(jnp.concatenate(rows, axis=0), var_count)):
        lhs[2 * v * full : 2 * (v + 1) * full, :] = part
    is_odd = odd == 1
    near_parts = []
    far_parts = []
    for v in range(var_count):
        base = 2 * v * full
        near_parts.append((base, full))
        for i, s in enumerate(keep):
            slot = jnp.where(is_odd, s, i)
            near_parts.append((pl.multiple_of(base + full + slot * group, group), group))
        far_parts.append((base + full, full))
        far_parts.append((base, full))

    def rows_of(parts):
        return jnp.concatenate([lhs[pl.ds(low, size), :] for low, size in parts], axis=0)

    most = jnp.zeros((half_slots * group, 2 * LANES), F32)
    for j in range(0, far.shape[0], 2):
        from_near = mm(rows_of(near_parts), columns(near, j, var_count))
        copies[j].wait()
        copies[j + 1].wait()
        from_far = mm(rows_of(far_parts), columns(far, j, var_count))
        for v in range(var_count):
            low = v * points + j * LANES
            high = low + 2 * LANES
            top = from_near[v * short : (v + 1) * short]
            bottom = from_far[2 * v * full : 2 * (v + 1) * full]
            whole = (top[:full] + bottom[:full]).astype(BF16)
            other = bottom[full:]
            for s in range(slots):
                even[s][:, low:high] = whole[s * group : (s + 1) * group]
            for i, s in enumerate(keep):
                mine = top[full + i * group : full + (i + 1) * group]
                begun = other[s * group : (s + 1) * group]
                ended = other[i * group : (i + 1) * group]
                lead[i][:, low:high] = jnp.where(is_odd, mine, begun)
                trail[i][:, low:high] = jnp.where(is_odd, ended, mine)
            sent = jnp.where(
                is_odd, other[half_slots * group :], other[group : (half_slots + 1) * group]
            )
            most = jnp.maximum(most, jnp.abs(sent))
            raw[:, low:high] = sent
    encode(raw, most, outer)


def inner_join_kernel(half_slots, group, *refs):
    lead = refs[:half_slots]
    trail = refs[half_slots : 2 * half_slots]
    inner = refs[2 * half_slots]
    joined = refs[2 * half_slots + 1 :]
    me = lax.axis_index("blk")
    odd = lax.rem(me, 2) == 1
    for i in range(half_slots):
        above = (i + half_slots - 1) % half_slots
        begun = lead[i][...] + decode(inner, above * group, (above + 1) * group)
        own = jnp.where(me == 0, 0.0, trail[i][...])
        ended = own + decode(inner, i * group, (i + 1) * group)
        joined[i][...] = jnp.where(odd, begun, ended).astype(BF16)


def outer_join_kernel(half_slots, group, *refs):
    lead = refs[:half_slots]
    trail = refs[half_slots : 2 * half_slots]
    outer = refs[2 * half_slots]
    joined = refs[2 * half_slots + 1 : 3 * half_slots + 1]
    outs = refs[3 * half_slots + 1 :]
    odd = lax.rem(lax.axis_index("blk"), 2) == 1
    for i in range(half_slots):
        above = (i + half_slots - 1) % half_slots
        begun = lead[i][...] + decode(outer, above * group, (above + 1) * group)
        ended = trail[i][...] + decode(outer, i * group, (i + 1) * group)
        other = jnp.where(odd, ended, begun).astype(BF16)
        outs[i][...] = jnp.where(odd, joined[i][...], other)
        outs[half_slots + i][...] = jnp.where(odd, other, joined[i][...])


def gram_kernel(slots, group, var_count, points, weights, classes, *refs):
    packed = refs[-1]
    blocks = 2 * slots
    me = lax.axis_index("blk")
    picked = jnp.zeros(classes.shape, F32)
    for k in range(weights.shape[0]):
        picked = picked + jnp.where(classes[...] == k, weights[k], jnp.float32(0.0))
    gram = None
    for v in range(var_count):
        part = slice(v * points, (v + 1) * points)
        left = jnp.concatenate([ref[:, part] for ref in refs[:-1]], axis=0)
        right = (left.astype(F32) * picked).astype(BF16)
        product = lax.dot_general(
            left, right, (((1,), (1,)), ((), ())), preferred_element_type=F32
        )
        gram = product if gram is None else gram + product
    size = blocks * group
    freqs = group // 2
    same = rem(iota((size, size), 0), freqs) == rem(iota((1, size), 1), freqs)
    gram = jnp.where(same, gram, 0.0).reshape(blocks, 2, freqs, size)
    rows_re = gram[:, 0].reshape(blocks * freqs, size)
    rows_im = gram[:, 1].reshape(blocks * freqs, size)
    width = 2 * blocks * blocks
    row, lane = (iota((size, 1), 0), iota((1, width), 1))
    fits = block_of(div(row, group), me, slots) == rem(lane, blocks)
    row_part = rem(div(row, freqs), 2)
    lane_part = rem(div(lane, blocks), 2)
    from_re = one_hot(fits & (row_part == lane_part))
    sign = jnp.where(lane_part == 0, 1.0, -1.0)
    from_im = jnp.where(fits & (row_part != lane_part), sign, 0.0).astype(BF16)
    total = mm(jnp.concatenate(split3(rows_re), axis=0), from_re)
    total = total + mm(jnp.concatenate(split3(rows_im), axis=0), from_im)
    total = sum_thirds(total)
    mine = div(iota((freqs, width), 1), 2 * blocks)
    out = jnp.zeros((freqs, width), F32)
    for b in range(blocks):
        block = block_of(jnp.int32(b), me, slots)
        out = out + jnp.where(mine == block, total[b * freqs : (b + 1) * freqs], 0.0)
    packed[...] = out


def mode_kernel(slots, var_count, points, scaling, feature_count, sums, *refs):
    csd, eig, modes = refs[-3:]
    tiles, refs = ([ref[...] for ref in refs[:sums]], refs[sums:])
    blocks = 2 * slots
    me = lax.axis_index("blk")
    spectra = [ref[...] for ref in refs[:-3]]
    raw = tiles[0] + tiles[1]
    if sums == 4:
        raw = raw + (tiles[2] + tiles[3])
    freqs, width = raw.shape
    group = 2 * freqs
    size = blocks * group
    mat = scaling * raw
    lane_part = rem(div(iota((freqs, width), 1), blocks), 2)
    is_re = lane_part == 0
    gather = one_hot(
        div(iota((width, width), 0), 2 * blocks) == rem(iota((1, width), 1), blocks)
    )

    def apply(*items):
        rows = []
        for matrix, vec_re, vec_im in items:
            rows.append(matrix * jnp.where(is_re, vec_re, -vec_im))
            rows.append(matrix * jnp.where(is_re, vec_im, vec_re))
        both = jnp.concatenate(rows, axis=0)
        got = sum_thirds(mm(jnp.concatenate(split3(both), axis=0), gather))
        return [got[i * freqs : (i + 1) * freqs] for i in range(2 * len(items))]

    def over_blocks(x):
        return jnp.sum(x, axis=1, keepdims=True) * jnp.float32(1.0 / (2 * blocks))

    vec_re = jnp.full((freqs, width), 1.0 / math.sqrt(blocks), F32)
    vec_im = jnp.zeros((freqs, width), F32)
    for _ in range(ITERS):
        out_re, out_im = apply((mat, vec_re, vec_im))
        length = jnp.sqrt(over_blocks(out_re * out_re + out_im * out_im))
        vec_re, vec_im = (out_re / length, out_im / length)
    low_re = vec_re.astype(BF16).astype(F32)
    low_im = vec_im.astype(BF16).astype(F32)
    out_re, out_im, low_out_re, low_out_im = apply((mat, vec_re, vec_im), (raw, low_re, low_im))
    value = over_blocks(vec_re * out_re + vec_im * out_im)
    diagonal = iota((freqs, freqs), 0) == iota((freqs, freqs), 1)
    eig[...] = jnp.sum(
        jnp.where(diagonal, jnp.broadcast_to(value, (freqs, freqs)), 0.0), axis=0, keepdims=True
    )
    normsq = over_blocks(low_re * low_out_re + low_im * low_out_im)
    scale = jnp.sqrt(jnp.float32(feature_count) / normsq)
    lane = iota((1, size), 1)
    expand = one_hot(iota((width, size), 0) == block_of(div(lane, group), me, slots))
    wide = mm(jnp.concatenate([vec_re, vec_im], axis=0).astype(BF16), expand)
    wide_re, wide_im = (wide[:freqs], wide[freqs:])
    part = rem(div(lane, freqs), 2)
    mine = rem(lane, freqs) == iota((freqs, size), 0)
    coef_re = jnp.where(mine, jnp.where(part == 0, wide_re, -wide_im), 0.0)
    coef_im = jnp.where(mine, jnp.where(part == 0, wide_im, wide_re), 0.0)
    rows = 2 * var_count
    upper = iota((rows, size), 0) < var_count
    var = rem(iota((rows, size), 0), var_count)
    tall = []
    for f in range(freqs):
        both = jnp.where(
            upper,
            jnp.broadcast_to(coef_re[f : f + 1], (rows, size)),
            jnp.broadcast_to(coef_im[f : f + 1], (rows, size)),
        )
        tall.append(
            jnp.concatenate([jnp.where(var == v, both, 0.0) for v in range(var_count)], axis=1)
        )
    coef = jnp.concatenate(tall, axis=0).astype(BF16)
    stacked = jnp.concatenate(
        [
            piece[:, v * points : (v + 1) * points]
            for v in range(var_count)
            for piece in spectra
        ],
        axis=0,
    )
    phi = mm(coef, stacked)
    for f in range(freqs):
        block = phi[f * rows : (f + 1) * rows] * scale[f : f + 1, :]
        for k in range(2):
            modes[f, k] = block[k * var_count : (k + 1) * var_count]
    split_rows = jnp.concatenate(
        [
            jnp.where(
                div(iota((blocks, width), 1), 2 * blocks) == iota((blocks, width), 0),
                jnp.broadcast_to(mat[f : f + 1], (blocks, width)),
                0.0,
            )
            for f in range(freqs)
        ],
        axis=0,
    )
    thirds = jnp.concatenate(split3(split_rows), axis=0)
    for k in range(2):
        row, lane = (iota((width, blocks), 0), iota((width, blocks), 1))
        fold = one_hot(rem(row, 2 * blocks) == lane + k * blocks)
        got = sum_thirds(mm(thirds, fold))
        for f in range(freqs):
            csd[f, k] = got[f * blocks : (f + 1) * blocks]


def call(kernel, outs, ins, inputs, scratch, flops, moved):
    vmem = pl.BlockSpec(memory_space=pltpu.VMEM)
    return pl.pallas_call(
        kernel,
        out_shape=outs,
        in_specs=ins,
        out_specs=jax.tree.map(lambda _: vmem, outs),
        scratch_shapes=scratch,
        compiler_params=pltpu.CompilerParams(vmem_limit_bytes=VMEM_LIMIT),
        cost_estimate=pl.CostEstimate(flops=flops, bytes_accessed=moved, transcendentals=0),
    )(*inputs)


def on_device(snapshots, freq_index, weight_class, class_weight):
    row_count, var_count, points = snapshots.shape
    features = var_count * points
    slots = lax.axis_size("blk")
    half_slots = slots // 2
    me = lax.axis_index("blk")
    freqs = freq_index.shape[0] // slots
    group = 2 * freqs
    blocks = 2 * slots
    vmem = pl.BlockSpec(memory_space=pltpu.VMEM)
    smem = pl.BlockSpec(memory_space=pltpu.SMEM)
    hbm = pl.BlockSpec(memory_space=pltpu.HBM)
    shape = jax.ShapeDtypeStruct

    wide = half_slots * group
    groups = points // LANES
    bins = pltpu.with_memory_space_constraint(freq_index, pltpu.HBM)
    bins_smem = pltpu.SMEM(freq_index.shape, jnp.int32)
    source = pltpu.with_memory_space_constraint(snapshots, pltpu.HBM)
    half_block = (groups, HALF, var_count, LANES)
    payload = shape((wide, features + LANES), jnp.int16)
    width = HALF * var_count
    sems = [pltpu.SemaphoreType.DMA, pltpu.SemaphoreType.DMA((groups,))]
    raw = pltpu.VMEM((wide, features), F32)
    inner, near = call(
        functools.partial(inner_kernel, slots, group, var_count, points),
        [payload, shape(half_block, BF16)],
        [hbm, hbm],
        (bins, source),
        [bins_smem, pltpu.VMEM((wide * var_count, width), BF16), raw, *sems],
        2 * wide * features * width,
        row_count * features,
    )

    def swap(x, first, also):
        pairs = [(i, i + 1) for i in range(first, slots - 1, 2)]
        return lax.ppermute(x, "blk", pairs + [(b, a) for a, b in pairs] + also)

    keep = [0] + list(range(half_slots + 1, slots))
    piece = shape((group, features), BF16)
    wide_piece = shape((group, features), F32)
    outer, *pieces = call(
        functools.partial(block_kernel, slots, keep, group, var_count, points),
        [payload] + [piece] * slots + [wide_piece] * (2 * half_slots),
        [hbm, hbm, vmem],
        (bins, source, near),
        [
            bins_smem,
            pltpu.VMEM((2 * slots * group * var_count, width), BF16),
            pltpu.VMEM(half_block, BF16),
            raw,
            *sems,
        ],
        2 * 4 * slots * group * features * width,
        row_count * features,
    )
    from_outer = swap(outer, 0, [])
    from_inner = swap(inner, 1, [(slots - 1, 0)])

    def shift(x, s):
        return lax.ppermute(x, "blk", [(i, (i + s) % slots) for i in range(slots)])

    even = [pieces[0]] + [shift(pieces[s], s) for s in range(1, slots)]
    halves = pieces[slots:]
    joined = call(
        functools.partial(inner_join_kernel, half_slots, group),
        [piece] * half_slots,
        [vmem] * (slots + 1),
        (*halves, from_inner),
        [],
        slots * group * features,
        10 * slots * group * features,
    )
    odd = call(
        functools.partial(outer_join_kernel, half_slots, group),
        [piece] * slots,
        [vmem] * (slots + half_slots + 1),
        (*halves, from_outer, *joined),
        [],
        slots * group * features,
        10 * slots * group * features,
    )
    above = [odd[0]] + [shift(odd[i], s) for i, s in enumerate(keep) if i]
    under = [odd[half_slots]] + [shift(odd[half_slots + i], i) for i in range(1, half_slots)]
    tile = 2 * blocks * blocks
    spectra = (*even, *above, *under)
    packed = call(
        functools.partial(gram_kernel, slots, group, var_count, points),
        shape((freqs, tile), F32),
        [smem, vmem] + [vmem] * len(spectra),
        (class_weight, weight_class.reshape(1, points), *spectra),
        [],
        2 * (blocks * group) ** 2 * features,
        4 * blocks * group * features,
    )
    devices = lax.axis_size("pts")
    def from_peer(x, step):
        return lax.ppermute(x, "pts", [(i, i ^ step) for i in range(devices)])

    parts = [packed]
    step = 1
    while step < devices:
        total = functools.reduce(jnp.add, parts[:2])
        if len(parts) == 4:
            total = total + (parts[2] + parts[3])
        by_four = step > 1 and 4 * step <= devices
        steps = (step, 2 * step, 3 * step) if by_four else (step,)
        parts = [total] + [from_peer(total, i) for i in steps]
        step *= 4 if by_four else 2
    total_features = features * devices
    csd, eigval, modes = call(
        functools.partial(
            mode_kernel,
            slots,
            var_count,
            points,
            1.0 / (total_features * (3.0 * NFFT / 8.0)),
            total_features,
            len(parts),
        ),
        [
            shape((freqs, 2, blocks, blocks), F32),
            shape((1, freqs), F32),
            shape((freqs, 2, var_count, points), F32),
        ],
        [vmem] * (len(parts) + len(spectra)),
        (*parts, *spectra),
        [],
        2 * 2 * blocks * group * group * features,
        2 * blocks * group * features,
    )
    return (csd, eigval.reshape(freqs), modes)


def solution(mesh):
    in_specs = (P("blk", None, "pts"), P(), P("pts"), P())
    out_specs = (P("blk", None, None, None), P("blk"), P("blk", None, None, "pts"))
    return jax.shard_map(
        on_device, mesh=mesh, in_specs=in_specs, out_specs=out_specs, check_vma=False
    )
```

```python
import functools
import math

import jax
import jax.numpy as jnp
from jax import lax
from jax.experimental import pallas as pl
from jax.experimental.pallas import tpu as pltpu
from jax.sharding import PartitionSpec as P

NFFT = 768
HALF = NFFT // 2
ITERS = 3
LANES = 128
VMEM_LIMIT = 32 * 1024 * 1024
F32 = jnp.float32
BF16 = jnp.bfloat16


def iota(shape, axis):
    return lax.broadcasted_iota(jnp.int32, shape, axis)


def div(x, n):
    return x >> (n.bit_length() - 1) if n & (n - 1) == 0 else x // n


def rem(x, n):
    return x & (n - 1) if n & (n - 1) == 0 else x % n


def mm(a, b):
    return jnp.dot(a, b, preferred_element_type=F32)


def split3(x):
    high = x.astype(BF16)
    rest = x - high.astype(F32)
    mid = rest.astype(BF16)
    low = (rest - mid.astype(F32)).astype(BF16)
    return (high, mid, low)


def sum_thirds(x):
    rows = x.shape[0] // 3
    return x[:rows] + (x[rows : 2 * rows] + x[2 * rows :])


def one_hot(condition):
    return jnp.where(condition, 1.0, 0.0).astype(BF16)


def modulo(x, n):
    return jnp.where(x < 0, x + n, x)


def block_of(slot, me, slots):
    half_slots = slots // 2
    above = slot - slots
    below = above - half_slots
    even = 2 * modulo(me - slot, slots)
    upper = 2 * modulo(me - jnp.where(above == 0, 0, above + half_slots), slots) + 1
    lower = modulo(2 * modulo(me - below, slots) - 1, 2 * slots)
    return jnp.where(slot < slots, even, jnp.where(below < 0, upper, lower))


def trig(phase):
    quarter = ((phase + NFFT // 8) * 1366) >> 18
    angle = (2.0 * math.pi / NFFT) * (phase - (NFFT // 4) * quarter).astype(F32)
    x = angle * angle
    cos = 1.0 + x * (-1.0 / 2 + x * (1.0 / 24 + x * (-1.0 / 720 + x * (1.0 / 40320))))
    sin = 1.0 + x * (-1.0 / 6 + x * (1.0 / 120 + x * (-1.0 / 5040 + x * (1.0 / 362880))))
    sin = angle * sin
    odd = (quarter & 1) != 0
    real_part = jnp.where(odd, sin, cos)
    imag_part = jnp.where(odd, cos, sin)
    real_part = jnp.where(((quarter + 1) & 2) != 0, -real_part, real_part)
    imag_part = jnp.where((quarter & 2) != 0, -imag_part, imag_part)
    return (real_part, imag_part)


def transform_rows(freqs, me, wanted, slots, group, start):
    count = group // 2
    times = start + iota((count, HALF), 1)
    window = 0.5 - 0.5 * trig(times)[0]
    row = iota((count, HALF), 0)
    out = []
    for s in wanted:
        owner = lax.rem(me + s, slots)
        freq = jnp.zeros((count, HALF), jnp.int32)
        for f in range(count):
            freq = jnp.where(row == f, freqs[owner * count + f], freq)
        product = freq * times
        turns = ((product >> 8) * 21846) >> 16
        real_part, imag_part = trig(product - NFFT * turns)
        out.append(window * real_part)
        out.append(-window * imag_part)
    return jnp.concatenate(out, axis=0).astype(BF16)


def spread(rows, var_count):
    lane = iota((1, LANES * var_count), 1)
    pick = one_hot(div(lane, var_count) == iota((LANES, LANES * var_count), 0))
    pieces = [mm(rows[:, t : t + LANES], pick) for t in range(0, HALF, LANES)]
    wide = jnp.concatenate(pieces, axis=1)
    owner = rem(iota((1, HALF * var_count), 1), var_count)
    return [jnp.where(owner == v, wide, 0.0).astype(BF16) for v in range(var_count)]


def columns(held, j, var_count):
    rows = HALF * var_count
    parts = [held.at[j + i].reshape(rows, LANES)[...] for i in range(2)]
    return jnp.concatenate(parts, axis=1)


def load_copies(x_hbm, half, held, sems):
    rows = pl.ds(half * HALF, HALF)
    return [
        pltpu.make_async_copy(x_hbm.at[rows, :, pl.ds(j * LANES, LANES)], held.at[j], sems.at[j])
        for j in range(held.shape[0])
    ]


def encode(values, largest, coded):
    rows, features = values.shape
    largest = jnp.maximum(jnp.max(largest, axis=1, keepdims=True), 1e-30)
    exponent = jnp.floor(jnp.log2(32000.0 / largest))
    steps = values[...] * jnp.exp2(exponent)
    coded[:, :features] = jnp.round(steps).astype(jnp.int32).astype(jnp.int16)
    tail = jnp.broadcast_to(exponent, (rows, LANES))
    coded[:, features:] = tail.astype(jnp.int32).astype(jnp.int16)


def decode(coded, low, high):
    features = coded.shape[1] - LANES
    exponent = coded[low:high, features:].astype(jnp.int32).astype(F32)[:, :1]
    steps = coded[low:high, :features].astype(jnp.int32).astype(F32)
    return steps * (1.0 / jnp.exp2(exponent))


def bins_copy(bins, freqs, sem):
    return pltpu.make_async_copy(bins, freqs, sem)


def inner_kernel(slots, group, var_count, points, bins, x_hbm, inner, near, *refs):
    freqs, lhs, raw, bins_sem, sems = refs
    fetch = bins_copy(bins, freqs, bins_sem)
    fetch.start()
    me = lax.axis_index("blk")
    odd = lax.rem(me, 2)
    copies = load_copies(x_hbm, odd, near, sems)
    for copy in copies:
        copy.start()
    half_slots = slots // 2
    wide = half_slots * group
    first = jnp.where(odd == 1, 1, half_slots)
    fetch.wait()
    wanted = [first + i for i in range(half_slots)]
    rows = transform_rows(freqs, me, wanted, slots, group, (1 - odd) * HALF)
    for v, part in enumerate(spread(rows, var_count)):
        lhs[v * wide : (v + 1) * wide, :] = part
    most = jnp.zeros((wide, 2 * LANES), F32)
    for j in range(0, near.shape[0], 2):
        copies[j].wait()
        copies[j + 1].wait()
        got = mm(lhs[...], columns(near, j, var_count))
        for v in range(var_count):
            low = v * points + j * LANES
            mine = got[v * wide : (v + 1) * wide]
            most = jnp.maximum(most, jnp.abs(mine))
            raw[:, low : low + 2 * LANES] = mine
    encode(raw, most, inner)


def block_kernel(slots, keep, group, var_count, points, bins, x_hbm, near, *refs):
    outs, (freqs, lhs, far, raw, bins_sem, sems) = (refs[:-6], refs[-6:])
    fetch = bins_copy(bins, freqs, bins_sem)
    fetch.start()
    me = lax.axis_index("blk")
    odd = lax.rem(me, 2)
    copies = load_copies(x_hbm, 1 - odd, far, sems)
    for copy in copies:
        copy.start()
    half_slots = slots // 2
    outer = outs[0]
    even = outs[1 : 1 + slots]
    lead = outs[1 + slots : 1 + slots + half_slots]
    trail = outs[1 + slots + half_slots :]
    full = slots * group
    short = full + half_slots * group
    fetch.wait()
    rows = [
        transform_rows(freqs, me, range(slots), slots, group, start * HALF)
        for start in (odd, 1 - odd)
    ]
    for v, part in enumerate(spread(jnp.concatenate(rows, axis=0), var_count)):
        lhs[2 * v * full : 2 * (v + 1) * full, :] = part
    is_odd = odd == 1
    near_parts = []
    far_parts = []
    for v in range(var_count):
        base = 2 * v * full
        near_parts.append((base, full))
        for i, s in enumerate(keep):
            slot = jnp.where(is_odd, s, i)
            near_parts.append((pl.multiple_of(base + full + slot * group, group), group))
        far_parts.append((base + full, full))
        far_parts.append((base, full))

    def rows_of(parts):
        return jnp.concatenate([lhs[pl.ds(low, size), :] for low, size in parts], axis=0)

    most = jnp.zeros((half_slots * group, 2 * LANES), F32)
    for j in range(0, far.shape[0], 2):
        from_near = mm(rows_of(near_parts), columns(near, j, var_count))
        copies[j].wait()
        copies[j + 1].wait()
        from_far = mm(rows_of(far_parts), columns(far, j, var_count))
        for v in range(var_count):
            low = v * points + j * LANES
            high = low + 2 * LANES
            top = from_near[v * short : (v + 1) * short]
            bottom = from_far[2 * v * full : 2 * (v + 1) * full]
            whole = (top[:full] + bottom[:full]).astype(BF16)
            other = bottom[full:]
            for s in range(slots):
                even[s][:, low:high] = whole[s * group : (s + 1) * group]
            for i, s in enumerate(keep):
                mine = top[full + i * group : full + (i + 1) * group]
                begun = other[s * group : (s + 1) * group]
                ended = other[i * group : (i + 1) * group]
                lead[i][:, low:high] = jnp.where(is_odd, mine, begun)
                trail[i][:, low:high] = jnp.where(is_odd, ended, mine)
            sent = jnp.where(
                is_odd, other[half_slots * group :], other[group : (half_slots + 1) * group]
            )
            most = jnp.maximum(most, jnp.abs(sent))
            raw[:, low:high] = sent
    encode(raw, most, outer)


def inner_join_kernel(half_slots, group, *refs):
    lead = refs[:half_slots]
    trail = refs[half_slots : 2 * half_slots]
    inner = refs[2 * half_slots]
    joined = refs[2 * half_slots + 1 :]
    me = lax.axis_index("blk")
    odd = lax.rem(me, 2) == 1
    for i in range(half_slots):
        above = (i + half_slots - 1) % half_slots
        begun = lead[i][...] + decode(inner, above * group, (above + 1) * group)
        own = jnp.where(me == 0, 0.0, trail[i][...])
        ended = own + decode(inner, i * group, (i + 1) * group)
        joined[i][...] = jnp.where(odd, begun, ended).astype(BF16)


def outer_join_kernel(half_slots, group, *refs):
    lead = refs[:half_slots]
    trail = refs[half_slots : 2 * half_slots]
    outer = refs[2 * half_slots]
    joined = refs[2 * half_slots + 1 : 3 * half_slots + 1]
    outs = refs[3 * half_slots + 1 :]
    odd = lax.rem(lax.axis_index("blk"), 2) == 1
    for i in range(half_slots):
        above = (i + half_slots - 1) % half_slots
        begun = lead[i][...] + decode(outer, above * group, (above + 1) * group)
        ended = trail[i][...] + decode(outer, i * group, (i + 1) * group)
        other = jnp.where(odd, ended, begun).astype(BF16)
        outs[i][...] = jnp.where(odd, joined[i][...], other)
        outs[half_slots + i][...] = jnp.where(odd, other, joined[i][...])


def gram_kernel(slots, group, var_count, points, weights, classes, *refs):
    packed = refs[-1]
    blocks = 2 * slots
    me = lax.axis_index("blk")
    picked = jnp.zeros(classes.shape, F32)
    for k in range(weights.shape[0]):
        picked = picked + jnp.where(classes[...] == k, weights[k], jnp.float32(0.0))
    gram = None
    for v in range(var_count):
        part = slice(v * points, (v + 1) * points)
        left = jnp.concatenate([ref[:, part] for ref in refs[:-1]], axis=0)
        right = (left.astype(F32) * picked).astype(BF16)
        product = lax.dot_general(
            left, right, (((1,), (1,)), ((), ())), preferred_element_type=F32
        )
        gram = product if gram is None else gram + product
    size = blocks * group
    freqs = group // 2
    same = rem(iota((size, size), 0), freqs) == rem(iota((1, size), 1), freqs)
    gram = jnp.where(same, gram, 0.0).reshape(blocks, 2, freqs, size)
    rows_re = gram[:, 0].reshape(blocks * freqs, size)
    rows_im = gram[:, 1].reshape(blocks * freqs, size)
    width = 2 * blocks * blocks
    row, lane = (iota((size, 1), 0), iota((1, width), 1))
    fits = block_of(div(row, group), me, slots) == rem(lane, blocks)
    row_part = rem(div(row, freqs), 2)
    lane_part = rem(div(lane, blocks), 2)
    from_re = one_hot(fits & (row_part == lane_part))
    sign = jnp.where(lane_part == 0, 1.0, -1.0)
    from_im = jnp.where(fits & (row_part != lane_part), sign, 0.0).astype(BF16)
    total = mm(jnp.concatenate(split3(rows_re), axis=0), from_re)
    total = total + mm(jnp.concatenate(split3(rows_im), axis=0), from_im)
    total = sum_thirds(total)
    mine = div(iota((freqs, width), 1), 2 * blocks)
    out = jnp.zeros((freqs, width), F32)
    for b in range(blocks):
        block = block_of(jnp.int32(b), me, slots)
        out = out + jnp.where(mine == block, total[b * freqs : (b + 1) * freqs], 0.0)
    packed[...] = out


def mode_kernel(slots, var_count, points, scaling, feature_count, sums, *refs):
    csd_out, eig, modes_out, csd, modes, sems = refs[-6:]
    refs = refs[:-3]
    tiles, refs = ([ref[...] for ref in refs[:sums]], refs[sums:])
    blocks = 2 * slots
    me = lax.axis_index("blk")
    spectra = [ref[...] for ref in refs[:-3]]
    raw = tiles[0] + tiles[1]
    if sums == 4:
        raw = raw + (tiles[2] + tiles[3])
    freqs, width = raw.shape
    group = 2 * freqs
    size = blocks * group
    mat = scaling * raw
    lane_part = rem(div(iota((freqs, width), 1), blocks), 2)
    is_re = lane_part == 0
    gather = one_hot(
        div(iota((width, width), 0), 2 * blocks) == rem(iota((1, width), 1), blocks)
    )

    split_rows = jnp.concatenate(
        [
            jnp.where(
                div(iota((blocks, width), 1), 2 * blocks) == iota((blocks, width), 0),
                jnp.broadcast_to(mat[f : f + 1], (blocks, width)),
                0.0,
            )
            for f in range(freqs)
        ],
        axis=0,
    )
    thirds = jnp.concatenate(split3(split_rows), axis=0)
    for k in range(2):
        row, lane = (iota((width, blocks), 0), iota((width, blocks), 1))
        fold = one_hot(rem(row, 2 * blocks) == lane + k * blocks)
        got = sum_thirds(mm(thirds, fold))
        for f in range(freqs):
            csd[f, k] = got[f * blocks : (f + 1) * blocks]
    copies = [pltpu.make_async_copy(csd, csd_out, sems.at[0])]
    copies[0].start()

    def apply(*items):
        rows = []
        for matrix, vec_re, vec_im in items:
            rows.append(matrix * jnp.where(is_re, vec_re, -vec_im))
            rows.append(matrix * jnp.where(is_re, vec_im, vec_re))
        both = jnp.concatenate(rows, axis=0)
        got = sum_thirds(mm(jnp.concatenate(split3(both), axis=0), gather))
        return [got[i * freqs : (i + 1) * freqs] for i in range(2 * len(items))]

    def over_blocks(x):
        return jnp.sum(x, axis=1, keepdims=True) * jnp.float32(1.0 / (2 * blocks))

    vec_re = jnp.full((freqs, width), 1.0 / math.sqrt(blocks), F32)
    vec_im = jnp.zeros((freqs, width), F32)
    for _ in range(ITERS):
        out_re, out_im = apply((mat, vec_re, vec_im))
        length = jnp.sqrt(over_blocks(out_re * out_re + out_im * out_im))
        vec_re, vec_im = (out_re / length, out_im / length)
    low_re = vec_re.astype(BF16).astype(F32)
    low_im = vec_im.astype(BF16).astype(F32)
    out_re, out_im, low_out_re, low_out_im = apply((mat, vec_re, vec_im), (raw, low_re, low_im))
    value = over_blocks(vec_re * out_re + vec_im * out_im)
    diagonal = iota((freqs, freqs), 0) == iota((freqs, freqs), 1)
    eig[...] = jnp.sum(
        jnp.where(diagonal, jnp.broadcast_to(value, (freqs, freqs)), 0.0), axis=0, keepdims=True
    )
    normsq = over_blocks(low_re * low_out_re + low_im * low_out_im)
    scale = jnp.sqrt(jnp.float32(feature_count) / normsq)
    lane = iota((1, size), 1)
    expand = one_hot(iota((width, size), 0) == block_of(div(lane, group), me, slots))
    wide = mm(jnp.concatenate([vec_re, vec_im], axis=0).astype(BF16), expand)
    wide_re, wide_im = (wide[:freqs], wide[freqs:])
    part = rem(div(lane, freqs), 2)
    mine = rem(lane, freqs) == iota((freqs, size), 0)
    coef_re = jnp.where(mine, jnp.where(part == 0, wide_re, -wide_im), 0.0)
    coef_im = jnp.where(mine, jnp.where(part == 0, wide_im, wide_re), 0.0)
    rows = 2 * var_count
    upper = iota((rows, size), 0) < var_count
    var = rem(iota((rows, size), 0), var_count)
    tall = []
    for f in range(freqs):
        both = jnp.where(
            upper,
            jnp.broadcast_to(coef_re[f : f + 1], (rows, size)),
            jnp.broadcast_to(coef_im[f : f + 1], (rows, size)),
        )
        tall.append(
            jnp.concatenate([jnp.where(var == v, both, 0.0) for v in range(var_count)], axis=1)
        )
    coef = jnp.concatenate(tall, axis=0).astype(BF16)
    stacked = jnp.concatenate(
        [
            piece[:, v * points : (v + 1) * points]
            for v in range(var_count)
            for piece in spectra
        ],
        axis=0,
    )
    for i in range(2):
        part = slice(i * points // 2, (i + 1) * points // 2)
        phi = mm(coef, stacked[:, part])
        for f in range(freqs):
            block = phi[f * rows : (f + 1) * rows] * scale[f : f + 1, :]
            for k in range(2):
                modes[f, k, :, part] = block[k * var_count : (k + 1) * var_count]
        lanes = pl.ds(i * points // 2, points // 2)
        copy = pltpu.make_async_copy(
            modes.at[:, :, :, lanes], modes_out.at[:, :, :, lanes], sems.at[1 + i]
        )
        copy.start()
        copies.append(copy)
    for copy in copies:
        copy.wait()


def call(kernel, outs, ins, inputs, scratch, flops, moved, places=None):
    vmem = pl.BlockSpec(memory_space=pltpu.VMEM)
    return pl.pallas_call(
        kernel,
        out_shape=outs,
        in_specs=ins,
        out_specs=places or jax.tree.map(lambda _: vmem, outs),
        scratch_shapes=scratch,
        compiler_params=pltpu.CompilerParams(vmem_limit_bytes=VMEM_LIMIT),
        cost_estimate=pl.CostEstimate(flops=flops, bytes_accessed=moved, transcendentals=0),
    )(*inputs)


def on_device(snapshots, freq_index, weight_class, class_weight):
    row_count, var_count, points = snapshots.shape
    features = var_count * points
    slots = lax.axis_size("blk")
    half_slots = slots // 2
    me = lax.axis_index("blk")
    freqs = freq_index.shape[0] // slots
    group = 2 * freqs
    blocks = 2 * slots
    vmem = pl.BlockSpec(memory_space=pltpu.VMEM)
    smem = pl.BlockSpec(memory_space=pltpu.SMEM)
    hbm = pl.BlockSpec(memory_space=pltpu.HBM)
    shape = jax.ShapeDtypeStruct

    wide = half_slots * group
    groups = points // LANES
    bins = pltpu.with_memory_space_constraint(freq_index, pltpu.HBM)
    bins_smem = pltpu.SMEM(freq_index.shape, jnp.int32)
    source = pltpu.with_memory_space_constraint(snapshots, pltpu.HBM)
    half_block = (groups, HALF, var_count, LANES)
    payload = shape((wide, features + LANES), jnp.int16)
    width = HALF * var_count
    sems = [pltpu.SemaphoreType.DMA, pltpu.SemaphoreType.DMA((groups,))]
    raw = pltpu.VMEM((wide, features), F32)
    inner, near = call(
        functools.partial(inner_kernel, slots, group, var_count, points),
        [payload, shape(half_block, BF16)],
        [hbm, hbm],
        (bins, source),
        [bins_smem, pltpu.VMEM((wide * var_count, width), BF16), raw, *sems],
        2 * wide * features * width,
        row_count * features,
    )

    def swap(x, first, also):
        pairs = [(i, i + 1) for i in range(first, slots - 1, 2)]
        return lax.ppermute(x, "blk", pairs + [(b, a) for a, b in pairs] + also)

    keep = [0] + list(range(half_slots + 1, slots))
    piece = shape((group, features), BF16)
    wide_piece = shape((group, features), F32)
    outer, *pieces = call(
        functools.partial(block_kernel, slots, keep, group, var_count, points),
        [payload] + [piece] * slots + [wide_piece] * (2 * half_slots),
        [hbm, hbm, vmem],
        (bins, source, near),
        [
            bins_smem,
            pltpu.VMEM((2 * slots * group * var_count, width), BF16),
            pltpu.VMEM(half_block, BF16),
            raw,
            *sems,
        ],
        2 * 4 * slots * group * features * width,
        row_count * features,
    )
    from_outer = swap(outer, 0, [])
    from_inner = swap(inner, 1, [(slots - 1, 0)])

    def shift(x, s):
        return lax.ppermute(x, "blk", [(i, (i + s) % slots) for i in range(slots)])

    even = [pieces[0]] + [shift(pieces[s], s) for s in range(1, slots)]
    halves = pieces[slots:]
    joined = call(
        functools.partial(inner_join_kernel, half_slots, group),
        [piece] * half_slots,
        [vmem] * (slots + 1),
        (*halves, from_inner),
        [],
        slots * group * features,
        10 * slots * group * features,
    )
    odd = call(
        functools.partial(outer_join_kernel, half_slots, group),
        [piece] * slots,
        [vmem] * (slots + half_slots + 1),
        (*halves, from_outer, *joined),
        [],
        slots * group * features,
        10 * slots * group * features,
    )
    above = [odd[0]] + [shift(odd[i], s) for i, s in enumerate(keep) if i]
    under = [odd[half_slots]] + [shift(odd[half_slots + i], i) for i in range(1, half_slots)]
    tile = 2 * blocks * blocks
    spectra = (*even, *above, *under)
    packed = call(
        functools.partial(gram_kernel, slots, group, var_count, points),
        shape((freqs, tile), F32),
        [smem, vmem] + [vmem] * len(spectra),
        (class_weight, weight_class.reshape(1, points), *spectra),
        [],
        2 * (blocks * group) ** 2 * features,
        4 * blocks * group * features,
    )
    devices = lax.axis_size("pts")
    def from_peer(x, step):
        return lax.ppermute(x, "pts", [(i, i ^ step) for i in range(devices)])

    parts = [packed]
    step = 1
    while step < devices:
        total = functools.reduce(jnp.add, parts[:2])
        if len(parts) == 4:
            total = total + (parts[2] + parts[3])
        by_four = step > 1 and 4 * step <= devices
        steps = (step, 2 * step, 3 * step) if by_four else (step,)
        parts = [total] + [from_peer(total, i) for i in steps]
        step *= 4 if by_four else 2
    total_features = features * devices
    csd, eigval, modes = call(
        functools.partial(
            mode_kernel,
            slots,
            var_count,
            points,
            1.0 / (total_features * (3.0 * NFFT / 8.0)),
            total_features,
            len(parts),
        ),
        [
            shape((freqs, 2, blocks, blocks), F32),
            shape((1, freqs), F32),
            shape((freqs, 2, var_count, points), F32),
        ],
        [vmem] * (len(parts) + len(spectra)),
        (*parts, *spectra),
        [
            pltpu.VMEM((freqs, 2, blocks, blocks), F32),
            pltpu.VMEM((freqs, 2, var_count, points), F32),
            pltpu.SemaphoreType.DMA((3,)),
        ],
        2 * 2 * blocks * group * group * features,
        2 * blocks * group * features,
        [hbm, vmem, hbm],
    )
    return (csd, eigval.reshape(freqs), modes)


def solution(mesh):
    in_specs = (P("blk", None, "pts"), P(), P("pts"), P())
    out_specs = (P("blk", None, None, None), P("blk"), P("blk", None, None, "pts"))
    return jax.shard_map(
        on_device, mesh=mesh, in_specs=in_specs, out_specs=out_specs, check_vma=False
    )
```

```python
import functools
import math

import jax
import jax.numpy as jnp
from jax import lax
from jax.experimental import pallas as pl
from jax.experimental.pallas import tpu as pltpu
from jax.sharding import PartitionSpec as P

NFFT = 768
HALF = NFFT // 2
ITERS = 3
LANES = 128
VMEM_LIMIT = 32 * 1024 * 1024
F32 = jnp.float32
BF16 = jnp.bfloat16


def iota(shape, axis):
    return lax.broadcasted_iota(jnp.int32, shape, axis)


def div(x, n):
    return x >> (n.bit_length() - 1) if n & (n - 1) == 0 else x // n


def rem(x, n):
    return x & (n - 1) if n & (n - 1) == 0 else x % n


def mm(a, b):
    return jnp.dot(a, b, preferred_element_type=F32)


def split3(x):
    high = x.astype(BF16)
    rest = x - high.astype(F32)
    mid = rest.astype(BF16)
    low = (rest - mid.astype(F32)).astype(BF16)
    return (high, mid, low)


def sum_thirds(x):
    rows = x.shape[0] // 3
    return x[:rows] + (x[rows : 2 * rows] + x[2 * rows :])


def one_hot(condition):
    return jnp.where(condition, 1.0, 0.0).astype(BF16)


def modulo(x, n):
    return jnp.where(x < 0, x + n, x)


def block_of(slot, me, slots):
    half_slots = slots // 2
    above = slot - slots
    below = above - half_slots
    even = 2 * modulo(me - slot, slots)
    upper = 2 * modulo(me - jnp.where(above == 0, 0, above + half_slots), slots) + 1
    lower = modulo(2 * modulo(me - below, slots) - 1, 2 * slots)
    return jnp.where(slot < slots, even, jnp.where(below < 0, upper, lower))


def trig(phase):
    quarter = ((phase + NFFT // 8) * 1366) >> 18
    angle = (2.0 * math.pi / NFFT) * (phase - (NFFT // 4) * quarter).astype(F32)
    x = angle * angle
    cos = 1.0 + x * (-1.0 / 2 + x * (1.0 / 24 + x * (-1.0 / 720 + x * (1.0 / 40320))))
    sin = 1.0 + x * (-1.0 / 6 + x * (1.0 / 120 + x * (-1.0 / 5040 + x * (1.0 / 362880))))
    sin = angle * sin
    odd = (quarter & 1) != 0
    real_part = jnp.where(odd, sin, cos)
    imag_part = jnp.where(odd, cos, sin)
    real_part = jnp.where(((quarter + 1) & 2) != 0, -real_part, real_part)
    imag_part = jnp.where((quarter & 2) != 0, -imag_part, imag_part)
    return (real_part, imag_part)


def transform_rows(freqs, me, wanted, slots, group, start):
    count = group // 2
    times = start + iota((count, HALF), 1)
    window = 0.5 - 0.5 * trig(times)[0]
    row = iota((count, HALF), 0)
    out = []
    for s in wanted:
        owner = lax.rem(me + s, slots)
        freq = jnp.zeros((count, HALF), jnp.int32)
        for f in range(count):
            freq = jnp.where(row == f, freqs[owner * count + f], freq)
        product = freq * times
        turns = ((product >> 8) * 21846) >> 16
        real_part, imag_part = trig(product - NFFT * turns)
        out.append(window * real_part)
        out.append(-window * imag_part)
    return jnp.concatenate(out, axis=0).astype(BF16)


def spread(rows, var_count):
    lane = iota((1, LANES * var_count), 1)
    pick = one_hot(div(lane, var_count) == iota((LANES, LANES * var_count), 0))
    pieces = [mm(rows[:, t : t + LANES], pick) for t in range(0, HALF, LANES)]
    wide = jnp.concatenate(pieces, axis=1)
    owner = rem(iota((1, HALF * var_count), 1), var_count)
    return [jnp.where(owner == v, wide, 0.0).astype(BF16) for v in range(var_count)]


def columns(held, j, var_count):
    rows = HALF * var_count
    parts = [held.at[j + i].reshape(rows, LANES)[...] for i in range(2)]
    return jnp.concatenate(parts, axis=1)


def load_copies(x_hbm, half, held, sems):
    rows = pl.ds(half * HALF, HALF)
    return [
        pltpu.make_async_copy(x_hbm.at[rows, :, pl.ds(j * LANES, LANES)], held.at[j], sems.at[j])
        for j in range(held.shape[0])
    ]


def encode(values, largest, coded):
    rows, features = values.shape
    largest = jnp.maximum(jnp.max(largest, axis=1, keepdims=True), 1e-30)
    exponent = jnp.floor(jnp.log2(32000.0 / largest))
    steps = values[...] * jnp.exp2(exponent)
    coded[:, :features] = jnp.round(steps).astype(jnp.int32).astype(jnp.int16)
    tail = jnp.broadcast_to(exponent, (rows, LANES))
    coded[:, features:] = tail.astype(jnp.int32).astype(jnp.int16)


def decode(coded, low, high):
    features = coded.shape[1] - LANES
    exponent = coded[low:high, features:].astype(jnp.int32).astype(F32)[:, :1]
    steps = coded[low:high, :features].astype(jnp.int32).astype(F32)
    return steps * (1.0 / jnp.exp2(exponent))


def bins_copy(bins, freqs, sem):
    return pltpu.make_async_copy(bins, freqs, sem)


def inner_kernel(slots, group, var_count, points, bins, x_hbm, inner, near, *refs):
    freqs, lhs, raw, bins_sem, sems = refs
    fetch = bins_copy(bins, freqs, bins_sem)
    fetch.start()
    me = lax.axis_index("blk")
    odd = lax.rem(me, 2)
    copies = load_copies(x_hbm, odd, near, sems)
    for copy in copies:
        copy.start()
    half_slots = slots // 2
    wide = half_slots * group
    first = jnp.where(odd == 1, 1, half_slots)
    fetch.wait()
    wanted = [first + i for i in range(half_slots)]
    rows = transform_rows(freqs, me, wanted, slots, group, (1 - odd) * HALF)
    for v, part in enumerate(spread(rows, var_count)):
        lhs[v * wide : (v + 1) * wide, :] = part
    most = jnp.zeros((wide, 2 * LANES), F32)
    for j in range(0, near.shape[0], 2):
        copies[j].wait()
        copies[j + 1].wait()
        got = mm(lhs[...], columns(near, j, var_count))
        for v in range(var_count):
            low = v * points + j * LANES
            mine = got[v * wide : (v + 1) * wide]
            most = jnp.maximum(most, jnp.abs(mine))
            raw[:, low : low + 2 * LANES] = mine
    encode(raw, most, inner)


def block_kernel(slots, keep, group, var_count, points, bins, x_hbm, near, *refs):
    outs, (freqs, lhs, far, raw, bins_sem, sems) = (refs[:-6], refs[-6:])
    fetch = bins_copy(bins, freqs, bins_sem)
    fetch.start()
    me = lax.axis_index("blk")
    odd = lax.rem(me, 2)
    copies = load_copies(x_hbm, 1 - odd, far, sems)
    for copy in copies:
        copy.start()
    half_slots = slots // 2
    outer = outs[0]
    even = outs[1 : 1 + slots]
    lead = outs[1 + slots : 1 + slots + half_slots]
    trail = outs[1 + slots + half_slots :]
    full = slots * group
    short = full + half_slots * group
    fetch.wait()
    rows = [
        transform_rows(freqs, me, range(slots), slots, group, start * HALF)
        for start in (odd, 1 - odd)
    ]
    for v, part in enumerate(spread(jnp.concatenate(rows, axis=0), var_count)):
        lhs[2 * v * full : 2 * (v + 1) * full, :] = part
    is_odd = odd == 1
    near_parts = []
    far_parts = []
    for v in range(var_count):
        base = 2 * v * full
        near_parts.append((base, full))
        for i, s in enumerate(keep):
            slot = jnp.where(is_odd, s, i)
            near_parts.append((pl.multiple_of(base + full + slot * group, group), group))
        far_parts.append((base + full, full))
        far_parts.append((base, full))

    def rows_of(parts):
        return jnp.concatenate([lhs[pl.ds(low, size), :] for low, size in parts], axis=0)

    most = jnp.zeros((half_slots * group, 2 * LANES), F32)
    for j in range(0, far.shape[0], 2):
        from_near = mm(rows_of(near_parts), columns(near, j, var_count))
        copies[j].wait()
        copies[j + 1].wait()
        from_far = mm(rows_of(far_parts), columns(far, j, var_count))
        for v in range(var_count):
            low = v * points + j * LANES
            high = low + 2 * LANES
            top = from_near[v * short : (v + 1) * short]
            bottom = from_far[2 * v * full : 2 * (v + 1) * full]
            whole = (top[:full] + bottom[:full]).astype(BF16)
            other = bottom[full:]
            for s in range(slots):
                even[s][:, low:high] = whole[s * group : (s + 1) * group]
            for i, s in enumerate(keep):
                mine = top[full + i * group : full + (i + 1) * group]
                begun = other[s * group : (s + 1) * group]
                ended = other[i * group : (i + 1) * group]
                lead[i][:, low:high] = jnp.where(is_odd, mine, begun)
                trail[i][:, low:high] = jnp.where(is_odd, ended, mine)
            sent = jnp.where(
                is_odd, other[half_slots * group :], other[group : (half_slots + 1) * group]
            )
            most = jnp.maximum(most, jnp.abs(sent))
            raw[:, low:high] = sent
    encode(raw, most, outer)


def inner_join_kernel(half_slots, group, *refs):
    lead = refs[:half_slots]
    trail = refs[half_slots : 2 * half_slots]
    inner = refs[2 * half_slots]
    joined = refs[2 * half_slots + 1 :]
    me = lax.axis_index("blk")
    odd = lax.rem(me, 2) == 1
    for i in range(half_slots):
        above = (i + half_slots - 1) % half_slots
        begun = lead[i][...] + decode(inner, above * group, (above + 1) * group)
        own = jnp.where(me == 0, 0.0, trail[i][...])
        ended = own + decode(inner, i * group, (i + 1) * group)
        joined[i][...] = jnp.where(odd, begun, ended).astype(BF16)


def outer_join_kernel(half_slots, group, *refs):
    lead = refs[:half_slots]
    trail = refs[half_slots : 2 * half_slots]
    outer = refs[2 * half_slots]
    joined = refs[2 * half_slots + 1 : 3 * half_slots + 1]
    outs = refs[3 * half_slots + 1 :]
    odd = lax.rem(lax.axis_index("blk"), 2) == 1
    for i in range(half_slots):
        above = (i + half_slots - 1) % half_slots
        begun = lead[i][...] + decode(outer, above * group, (above + 1) * group)
        ended = trail[i][...] + decode(outer, i * group, (i + 1) * group)
        other = jnp.where(odd, ended, begun).astype(BF16)
        outs[i][...] = jnp.where(odd, joined[i][...], other)
        outs[half_slots + i][...] = jnp.where(odd, other, joined[i][...])


def gram_kernel(slots, group, var_count, points, weights, classes, *refs):
    packed = refs[-1]
    blocks = 2 * slots
    me = lax.axis_index("blk")
    picked = jnp.zeros(classes.shape, F32)
    for k in range(weights.shape[0]):
        picked = picked + jnp.where(classes[...] == k, weights[k], jnp.float32(0.0))
    gram = None
    for v in range(var_count):
        part = slice(v * points, (v + 1) * points)
        left = jnp.concatenate([ref[:, part] for ref in refs[:-1]], axis=0)
        right = (left.astype(F32) * picked).astype(BF16)
        product = lax.dot_general(
            left, right, (((1,), (1,)), ((), ())), preferred_element_type=F32
        )
        gram = product if gram is None else gram + product
    size = blocks * group
    freqs = group // 2
    same = rem(iota((size, size), 0), freqs) == rem(iota((1, size), 1), freqs)
    gram = jnp.where(same, gram, 0.0).reshape(blocks, 2, freqs, size)
    rows_re = gram[:, 0].reshape(blocks * freqs, size)
    rows_im = gram[:, 1].reshape(blocks * freqs, size)
    width = 2 * blocks * blocks
    row, lane = (iota((size, 1), 0), iota((1, width), 1))
    fits = block_of(div(row, group), me, slots) == rem(lane, blocks)
    row_part = rem(div(row, freqs), 2)
    lane_part = rem(div(lane, blocks), 2)
    from_re = one_hot(fits & (row_part == lane_part))
    sign = jnp.where(lane_part == 0, 1.0, -1.0)
    from_im = jnp.where(fits & (row_part != lane_part), sign, 0.0).astype(BF16)
    total = mm(jnp.concatenate(split3(rows_re), axis=0), from_re)
    total = total + mm(jnp.concatenate(split3(rows_im), axis=0), from_im)
    total = sum_thirds(total)
    mine = div(iota((freqs, width), 1), 2 * blocks)
    out = jnp.zeros((freqs, width), F32)
    for b in range(blocks):
        block = block_of(jnp.int32(b), me, slots)
        out = out + jnp.where(mine == block, total[b * freqs : (b + 1) * freqs], 0.0)
    packed[...] = out


def mode_kernel(slots, var_count, points, scaling, feature_count, sums, *refs):
    csd, eig, modes = refs[-3:]
    tiles, refs = ([ref[...] for ref in refs[:sums]], refs[sums:])
    blocks = 2 * slots
    me = lax.axis_index("blk")
    spectra = [ref[...] for ref in refs[:-3]]
    raw = tiles[0] + tiles[1]
    if sums == 4:
        raw = raw + (tiles[2] + tiles[3])
    freqs, width = raw.shape
    group = 2 * freqs
    size = blocks * group
    mat = scaling * raw
    lane_part = rem(div(iota((freqs, width), 1), blocks), 2)
    is_re = lane_part == 0
    gather = one_hot(
        div(iota((width, width), 0), 2 * blocks) == rem(iota((1, width), 1), blocks)
    )

    def apply(*items):
        rows = []
        for matrix, vec_re, vec_im in items:
            rows.append(matrix * jnp.where(is_re, vec_re, -vec_im))
            rows.append(matrix * jnp.where(is_re, vec_im, vec_re))
        both = jnp.concatenate(rows, axis=0)
        got = sum_thirds(mm(jnp.concatenate(split3(both), axis=0), gather))
        return [got[i * freqs : (i + 1) * freqs] for i in range(2 * len(items))]

    def over_blocks(x):
        return jnp.sum(x, axis=1, keepdims=True) * jnp.float32(1.0 / (2 * blocks))

    vec_re = jnp.full((freqs, width), 1.0 / math.sqrt(blocks), F32)
    vec_im = jnp.zeros((freqs, width), F32)
    for _ in range(ITERS):
        out_re, out_im = apply((mat, vec_re, vec_im))
        length = jnp.sqrt(over_blocks(out_re * out_re + out_im * out_im))
        vec_re, vec_im = (out_re / length, out_im / length)
    low_re = vec_re.astype(BF16).astype(F32)
    low_im = vec_im.astype(BF16).astype(F32)
    out_re, out_im, low_out_re, low_out_im = apply((mat, vec_re, vec_im), (raw, low_re, low_im))
    value = over_blocks(vec_re * out_re + vec_im * out_im)
    diagonal = iota((freqs, freqs), 0) == iota((freqs, freqs), 1)
    eig[...] = jnp.sum(
        jnp.where(diagonal, jnp.broadcast_to(value, (freqs, freqs)), 0.0), axis=0, keepdims=True
    )
    normsq = over_blocks(low_re * low_out_re + low_im * low_out_im)
    scale = jnp.sqrt(jnp.float32(feature_count) / normsq)
    lane = iota((1, size), 1)
    expand = one_hot(iota((width, size), 0) == block_of(div(lane, group), me, slots))
    wide = mm(jnp.concatenate([vec_re, vec_im], axis=0).astype(BF16), expand)
    wide_re, wide_im = (wide[:freqs], wide[freqs:])
    part = rem(div(lane, freqs), 2)
    mine = rem(lane, freqs) == iota((freqs, size), 0)
    coef_re = jnp.where(mine, jnp.where(part == 0, wide_re, -wide_im), 0.0)
    coef_im = jnp.where(mine, jnp.where(part == 0, wide_im, wide_re), 0.0)
    rows = 2 * var_count
    upper = iota((rows, size), 0) < var_count
    var = rem(iota((rows, size), 0), var_count)
    tall = []
    for f in range(freqs):
        both = jnp.where(
            upper,
            jnp.broadcast_to(coef_re[f : f + 1], (rows, size)),
            jnp.broadcast_to(coef_im[f : f + 1], (rows, size)),
        )
        tall.append(
            jnp.concatenate([jnp.where(var == v, both, 0.0) for v in range(var_count)], axis=1)
        )
    coef = jnp.concatenate(tall, axis=0).astype(BF16)
    stacked = jnp.concatenate(
        [
            piece[:, v * points : (v + 1) * points]
            for v in range(var_count)
            for piece in spectra
        ],
        axis=0,
    )
    phi = mm(coef, stacked)
    for f in range(freqs):
        block = phi[f * rows : (f + 1) * rows] * scale[f : f + 1, :]
        for k in range(2):
            modes[f, k] = block[k * var_count : (k + 1) * var_count]
    split_rows = jnp.concatenate(
        [
            jnp.where(
                div(iota((blocks, width), 1), 2 * blocks) == iota((blocks, width), 0),
                jnp.broadcast_to(mat[f : f + 1], (blocks, width)),
                0.0,
            )
            for f in range(freqs)
        ],
        axis=0,
    )
    thirds = jnp.concatenate(split3(split_rows), axis=0)
    for k in range(2):
        row, lane = (iota((width, blocks), 0), iota((width, blocks), 1))
        fold = one_hot(rem(row, 2 * blocks) == lane + k * blocks)
        got = sum_thirds(mm(thirds, fold))
        for f in range(freqs):
            csd[f, k] = got[f * blocks : (f + 1) * blocks]


def call(kernel, outs, ins, inputs, scratch, flops, moved):
    vmem = pl.BlockSpec(memory_space=pltpu.VMEM)
    return pl.pallas_call(
        kernel,
        out_shape=outs,
        in_specs=ins,
        out_specs=jax.tree.map(lambda _: vmem, outs),
        scratch_shapes=scratch,
        compiler_params=pltpu.CompilerParams(vmem_limit_bytes=VMEM_LIMIT),
        cost_estimate=pl.CostEstimate(flops=flops, bytes_accessed=moved, transcendentals=0),
    )(*inputs)


def on_device(snapshots, freq_index, weight_class, class_weight):
    row_count, var_count, points = snapshots.shape
    features = var_count * points
    slots = lax.axis_size("blk")
    half_slots = slots // 2
    me = lax.axis_index("blk")
    freqs = freq_index.shape[0] // slots
    group = 2 * freqs
    blocks = 2 * slots
    vmem = pl.BlockSpec(memory_space=pltpu.VMEM)
    smem = pl.BlockSpec(memory_space=pltpu.SMEM)
    hbm = pl.BlockSpec(memory_space=pltpu.HBM)
    shape = jax.ShapeDtypeStruct

    wide = half_slots * group
    groups = points // LANES
    bins = pltpu.with_memory_space_constraint(freq_index, pltpu.HBM)
    bins_smem = pltpu.SMEM(freq_index.shape, jnp.int32)
    source = pltpu.with_memory_space_constraint(snapshots, pltpu.HBM)
    half_block = (groups, HALF, var_count, LANES)
    payload = shape((wide, features + LANES), jnp.int16)
    width = HALF * var_count
    sems = [pltpu.SemaphoreType.DMA, pltpu.SemaphoreType.DMA((groups,))]
    raw = pltpu.VMEM((wide, features), F32)
    inner, near = call(
        functools.partial(inner_kernel, slots, group, var_count, points),
        [payload, shape(half_block, BF16)],
        [hbm, hbm],
        (bins, source),
        [bins_smem, pltpu.VMEM((wide * var_count, width), BF16), raw, *sems],
        2 * wide * features * width,
        row_count * features,
    )

    def swap(x, first, also):
        pairs = [(i, i + 1) for i in range(first, slots - 1, 2)]
        return lax.ppermute(x, "blk", pairs + [(b, a) for a, b in pairs] + also)

    keep = [0] + list(range(half_slots + 1, slots))
    piece = shape((group, features), BF16)
    wide_piece = shape((group, features), F32)
    outer, *pieces = call(
        functools.partial(block_kernel, slots, keep, group, var_count, points),
        [payload] + [piece] * slots + [wide_piece] * (2 * half_slots),
        [hbm, hbm, vmem],
        (bins, source, near),
        [
            bins_smem,
            pltpu.VMEM((2 * slots * group * var_count, width), BF16),
            pltpu.VMEM(half_block, BF16),
            raw,
            *sems,
        ],
        2 * 4 * slots * group * features * width,
        row_count * features,
    )
    from_outer = swap(outer, 0, [])
    from_inner = swap(inner, 1, [(slots - 1, 0)])

    def shift(x, s):
        return lax.ppermute(x, "blk", [(i, (i + s) % slots) for i in range(slots)])

    even = [pieces[0]] + [shift(pieces[s], s) for s in range(1, slots)]
    halves = pieces[slots:]
    joined = call(
        functools.partial(inner_join_kernel, half_slots, group),
        [piece] * half_slots,
        [vmem] * (slots + 1),
        (*halves, from_inner),
        [],
        slots * group * features,
        10 * slots * group * features,
    )
    odd = call(
        functools.partial(outer_join_kernel, half_slots, group),
        [piece] * slots,
        [vmem] * (slots + half_slots + 1),
        (*halves, from_outer, *joined),
        [],
        slots * group * features,
        10 * slots * group * features,
    )
    above = [odd[0]] + [shift(odd[i], s) for i, s in enumerate(keep) if i]
    under = [odd[half_slots]] + [shift(odd[half_slots + i], i) for i in range(1, half_slots)]
    tile = 2 * blocks * blocks
    spectra = (*even, *above, *under)
    packed = call(
        functools.partial(gram_kernel, slots, group, var_count, points),
        shape((freqs, tile), F32),
        [smem, vmem] + [vmem] * len(spectra),
        (class_weight, weight_class.reshape(1, points), *spectra),
        [],
        2 * (blocks * group) ** 2 * features,
        4 * blocks * group * features,
    )
    devices = lax.axis_size("pts")
    def from_peer(x, step):
        return lax.ppermute(x, "pts", [(i, i ^ step) for i in range(devices)])

    groups_of = []
    step = 2
    while step < devices:
        by_four = 4 * step <= devices
        groups_of.append((step, 2 * step, 3 * step) if by_four else (step,))
        step *= 4 if by_four else 2
    groups_of.append((1,))
    parts = [packed]
    for steps in groups_of:
        total = functools.reduce(jnp.add, parts[:2])
        if len(parts) == 4:
            total = total + (parts[2] + parts[3])
        parts = [total] + [from_peer(total, i) for i in steps]
    total_features = features * devices
    csd, eigval, modes = call(
        functools.partial(
            mode_kernel,
            slots,
            var_count,
            points,
            1.0 / (total_features * (3.0 * NFFT / 8.0)),
            total_features,
            len(parts),
        ),
        [
            shape((freqs, 2, blocks, blocks), F32),
            shape((1, freqs), F32),
            shape((freqs, 2, var_count, points), F32),
        ],
        [vmem] * (len(parts) + len(spectra)),
        (*parts, *spectra),
        [],
        2 * 2 * blocks * group * group * features,
        2 * blocks * group * features,
    )
    return (csd, eigval.reshape(freqs), modes)


def solution(mesh):
    in_specs = (P("blk", None, "pts"), P(), P("pts"), P())
    out_specs = (P("blk", None, None, None), P("blk"), P("blk", None, None, "pts"))
    return jax.shard_map(
        on_device, mesh=mesh, in_specs=in_specs, out_specs=out_specs, check_vma=False
    )
```
